32 devices in a mesh: replica: 16 (over z, y, core), fsdp: 2 (over x).
Axes of the slice: x: 2, y: 2, z: 4, core: 2. Of those that a mesh axis runs over, the one named last changes fastest.
Arguments:
- hidden: bfloat16 [2, 8192, 2048], P(None, ('replica', 'fsdp')), may hold values from -6 to 6
- targets: int32 [2, 8192], P(None, ('replica', 'fsdp')), may hold values from 0 to 511
- valid: int32 [2, 8192], P(None, ('replica', 'fsdp')), may hold values 0 or 1
- plan: int32 [2], replicated, may hold values from 0 to 1, each once
- outer_head: float32 [2048, 512], P('fsdp'), may hold values from -6 to 6
- drift: bfloat16 [16, 2048, 512], P('replica', 'fsdp'), may hold values from -4 to 4
- ref_head: bfloat16 [2048, 512], P(('replica', 'fsdp')), may hold values from -6 to 6
Outputs:
- new_outer: float32 [2048, 512], P('fsdp')
- new_inner: float32 [16, 2048, 512], P('replica', 'fsdp')
The draws below stay inside these ranges and needn't reach their ends.
Inputs may be any that keep to these rules, and one draw needn't show every extreme that they name: `plan`: each column block appears exactly once.
All inputs are finite; a program needn't handle non-finite values. No bound on the sum of `valid` on one device may be relied on, other than what follows from the above.
Results may differ from the reference program's by a relative error of at most 0.0003.
Values may be sent and summed in bfloat16 or wider, within the bound.
No kernel may reach another device: no remote copies, remote signals or barrier semaphores. Data moves between devices by JAX's collectives and lax.ppermute only.
A program may use at most 64 MiB of HBM per device.

```python
import math
import jax
import jax.numpy as jnp
import numpy as np
from jax import lax

D = 2048
V = 512
FRAGS = 2
STEPS = 2
TOK_DEV = 256
REPLICAS = 16
TOKENS = 8192
N_REPLICA = 16
N_FSDP = 2


def plant(values, own_key, smallest, high):
    longest = values.shape.index(max(values.shape))
    spots = []
    for shift in (0, 1):
        where = [jax.random.randint(jax.random.fold_in(own_key, axis), (), 0, length) for axis, length in enumerate(values.shape)]
        where[longest] = (where[longest] + shift) % values.shape[longest]
        spots.append(tuple(where))
    return values.at[spots[0]].set(smallest).at[spots[1]].set(high)


def block_scale(rng, extent, shards, low, largest):
    def one(position, blocks):
        steps = jax.random.uniform(jax.random.fold_in(jax.random.fold_in(rng, 6), position), (blocks,), jnp.float32, low / len(shards), largest / len(shards))
        return jnp.repeat(jnp.exp(steps), extent[position] // blocks).reshape((-1,) + (1,) * (len(extent) - position - 1))

    gain = one(*shards[0])
    for cut in shards[1:]:
        gain = gain * one(*cut)
    return gain


def rank_bounds(amount, lean):
    portions = [(1 << 20) // math.isqrt(grade ** lean) + 1 for grade in range(1, amount + 1)]
    scale = 1 + sum(portions) // (1 << 30)
    return np.cumsum(np.array([max(1, weight // scale) for weight in portions]))


def ranked(key, shape, count, slope):
    table = rank_bounds(count, slope)
    lot = jax.random.randint(jax.random.fold_in(key, 1), shape, 0, int(table[count - 1]))
    grade = jnp.searchsorted(jnp.asarray(table, jnp.int32), lot, side="right")
    return jax.random.permutation(jax.random.fold_in(key, 2), count)[grade].astype(jnp.int32)


def scatter_about(rng, shape, spread, bound, split=(), kind=jnp.bfloat16):
    loudness = block_scale(rng, shape, split, -0.22, 0.18) if split else 1.0
    array = jax.random.normal(rng, shape, jnp.float32) * spread * loudness
    return jnp.minimum(jnp.maximum(array, -bound), bound).astype(kind)


def setup_inputs(seed: int = 0) -> dict:
    splits = jax.random.split(jax.random.key(seed), 8)
    return {
        "hidden": scatter_about(splits[0], (STEPS, TOKENS, D), 1.0, 6.0, ((1, 32),)),
        "targets": plant(ranked(splits[1], (STEPS, TOKENS), V, 2), jax.random.fold_in(splits[1], 3), 0, V - 1).astype(jnp.int32),
        "valid": plant((jax.random.randint(splits[2], (STEPS, TOKENS), 0, 8) < 7).astype(jnp.int32), jax.random.fold_in(splits[2], 1), 0, 1),
        "plan": jax.random.permutation(splits[3], FRAGS).astype(jnp.int32),
        "outer_head": scatter_about(splits[4], (D, V), 1.0, 6.0, ((0, 2),), jnp.float32),
        "drift": scatter_about(splits[5], (REPLICAS, D, V), 0.3, 4.0, ((0, 16), (1, 2))),
        "ref_head": scatter_about(splits[6], (D, V), 1.0, 6.0, ((0, 32),)),
    }


soft_cap = 30.0
kl_weight = 0.5
inner_rate = 0.5
outer_rate = 0.7
mix_weight = 0.5
norm_eps = 1e-05

def normalize(hidden_rows):
    values = hidden_rows.astype(jnp.float32)
    factor = lax.rsqrt(lax.optimization_barrier(jnp.mean(values * values, axis=-1, keepdims=True)) + norm_eps)
    return (values * factor).astype(jnp.bfloat16)

def capped(raw):
    return soft_cap * jnp.tanh(raw * (4.0 / math.sqrt(D)) / soft_cap)

def logit_grads(policy, refer, target_ids, valid_rows):
    policy_log = policy - jnp.log(lax.optimization_barrier(jnp.sum(jnp.exp(policy), axis=-1, keepdims=True)))
    refer_log = refer - jnp.log(lax.optimization_barrier(jnp.sum(jnp.exp(refer), axis=-1, keepdims=True)))
    policy_prob = jnp.exp(policy_log)
    diverge = policy_log - refer_log
    kl_value = lax.optimization_barrier(jnp.sum(policy_prob * diverge, axis=-1, keepdims=True))
    entries = jnp.arange(policy.shape[-1], dtype=jnp.int32)
    onehot = (target_ids[:, None] == entries[None, :]).astype(jnp.float32)
    upstream = valid_rows[:, None].astype(jnp.float32) * (policy_prob - onehot + kl_weight * policy_prob * (diverge - kl_value))
    ratio = policy / soft_cap
    return (upstream * (1.0 - ratio * ratio) * (4.0 / math.sqrt(D))).astype(jnp.bfloat16)

def apply_sync(outer_head, inner, start, mean_delta, width_part):
    fresh = lax.dynamic_slice_in_dim(outer_head, start, width_part, 1) - outer_rate * mean_delta
    outer_head = lax.dynamic_update_slice_in_dim(outer_head, fresh, start, 1)
    inner_cols = lax.dynamic_slice_in_dim(inner, start, width_part, 2)
    mixed = mix_weight * inner_cols + (1.0 - mix_weight) * fresh[None]
    inner = lax.dynamic_update_slice_in_dim(inner, mixed, start, 2)
    return (outer_head, inner)

def reference(hidden, targets, valid, plan, outer_head, drift, ref_head):
    replicas = N_REPLICA
    per_replica = TOK_DEV * N_FSDP
    width_part = V // FRAGS
    inner = outer_head[None] + drift.astype(jnp.float32)
    pending = None
    for index_step in range(STEPS):
        hidden_now = hidden[index_step].reshape(replicas, per_replica, D)
        target_now = targets[index_step].reshape(replicas, per_replica)
        valid_now = valid[index_step].reshape(replicas, per_replica)

        def update(operands):
            weights, rows_hidden, rows_target, rows_valid = operands
            normed = normalize(rows_hidden)
            policy = capped(jnp.dot(normed, weights.astype(jnp.bfloat16), preferred_element_type=jnp.float32))
            refer = capped(jnp.dot(normed, ref_head, preferred_element_type=jnp.float32))
            grads = logit_grads(policy, refer, rows_target, rows_valid)
            return weights - inner_rate * jnp.dot(normed.T, grads, preferred_element_type=jnp.float32)
        inner = lax.map(update, (inner, hidden_now, target_now, valid_now))
        if pending is not None:
            outer_head, inner = apply_sync(outer_head, inner, pending[0], pending[1], width_part)
        start = (plan[index_step] * width_part).astype(jnp.int32)
        outer_cols = lax.dynamic_slice_in_dim(outer_head, start, width_part, 1)
        inner_cols = lax.dynamic_slice_in_dim(inner, start, width_part, 2)
        mean_delta = lax.optimization_barrier(jnp.sum(outer_cols[None] - inner_cols, axis=0)) / replicas
        pending = (start, mean_delta)
    outer_head, inner = apply_sync(outer_head, inner, pending[0], pending[1], width_part)
    return (outer_head, inner)
```

```python
import math

import jax
import jax.numpy as jnp
from jax import lax
from jax.sharding import PartitionSpec as P

D = 2048
FRAGS = 2
STEPS = 2
CORES = 2
MAJOR = 4

soft_cap = 30.0
kl_weight = 0.5
inner_rate = 0.5
outer_rate = 0.7
mix_weight = 0.5
norm_eps = 1e-05

f32 = jnp.float32
bf16 = jnp.bfloat16
f16 = jnp.float16
logit_type = jnp.float32


def swap(value, axis, mask):
    size = lax.axis_size(axis)
    return lax.ppermute(value, axis, [(i, i ^ mask) for i in range(size)])


def rows_at(value, block, count):
    return lax.dynamic_slice_in_dim(value, block * count, count, 0)


def columns_at(value, block, count):
    return lax.dynamic_slice_in_dim(value, block * count, count, 1)


def place(pieces, spots):
    count = pieces[0].shape[0]
    whole = jnp.zeros((count * len(pieces),) + pieces[0].shape[1:], pieces[0].dtype)
    for piece, spot in zip(pieces, spots):
        whole = lax.dynamic_update_slice_in_dim(whole, piece, spot * count, 0)
    return whole


def in_pair(first, own, other):
    return jnp.where(
        first, jnp.concatenate([own, other], 0), jnp.concatenate([other, own], 0)
    )


def grid_of_replicas():
    chips = lax.axis_size("replica") // CORES
    minor = chips // MAJOR
    me = lax.axis_index("replica")
    return minor, me % CORES, me // (CORES * minor)


def gather_reference(rows):
    minor, core, major = grid_of_replicas()
    fsdp = lax.axis_size("fsdp")
    me = lax.axis_index("fsdp")
    masks = range(fsdp)
    block = place([rows] + [swap(rows, "fsdp", m) for m in masks[1:]], [me ^ m for m in masks])
    spots = lax.axis_index("replica")
    blocks = [(block, spots)]
    step = CORES * minor
    blocks = [(swap(b, "replica", m * step) if m else b, s ^ (m * step)) for b, s in blocks for m in range(MAJOR)]
    mask = CORES
    while mask < step:
        stacked = jnp.concatenate([b for b, _ in blocks], 0)
        other = swap(stacked, "replica", mask)
        blocks = blocks + [
            (p, s ^ mask) for p, (_, s) in zip(jnp.split(other, len(blocks), 0), blocks)
        ]
        mask *= 2
    stacked = jnp.concatenate([b for b, _ in blocks], 0)
    other = swap(stacked, "replica", 1)
    blocks = blocks + [(p, s ^ 1) for p, (_, s) in zip(jnp.split(other, len(blocks), 0), blocks)]
    return place([b for b, _ in blocks], [s for _, s in blocks])


def mean_over_replicas(delta):
    minor, core, major = grid_of_replicas()
    replicas = lax.axis_size("replica")
    delta = delta * (1.0 / replicas)
    half = delta.shape[0] // CORES
    part = rows_at(delta, core, half) + swap(rows_at(delta, 1 - core, half), "replica", 1)
    step = CORES * minor
    quarter = half // MAJOR
    sent = part.astype(f16)
    own = rows_at(part, major, quarter)
    for m in (2, 1, 3):
        own = own + swap(rows_at(sent, major ^ m, quarter), "replica", m * step).astype(f32)
    mask = CORES
    while mask < step:
        own = own + swap(own, "replica", mask)
        mask *= 2
    own = own.astype(f16)
    pieces = [own] + [swap(own, "replica", m * step) for m in (2, 1, 3)]
    gathered = place(pieces, [major ^ m for m in (0, 2, 1, 3)])
    return in_pair(core == 0, gathered, swap(gathered, "replica", 1)).astype(f32)


def normalize(hidden_rows):
    values = hidden_rows.astype(f32)
    factor = lax.rsqrt(jnp.mean(values * values, axis=-1, keepdims=True) + norm_eps)
    return (values * factor).astype(bf16)


def capped(raw):
    return soft_cap * jnp.tanh(raw * (4.0 / math.sqrt(D)) / soft_cap)


def log_softmax(logits):
    return logits - jnp.log(jnp.sum(jnp.exp(logits), axis=-1, keepdims=True))


def logit_grads(policy, refer_log, target_ids, valid_rows):
    policy_log = log_softmax(policy)
    policy_prob = jnp.exp(policy_log)
    diverge = policy_log - refer_log
    kl_value = jnp.sum(policy_prob * diverge, axis=-1, keepdims=True)
    entries = jnp.arange(policy.shape[-1], dtype=jnp.int32)
    onehot = (target_ids[:, None] == entries[None, :]).astype(f32)
    upstream = valid_rows[:, None].astype(f32) * (
        policy_prob - onehot + kl_weight * policy_prob * (diverge - kl_value)
    )
    ratio = policy / soft_cap
    return (upstream * (1.0 - ratio * ratio) * (4.0 / math.sqrt(D))).astype(bf16)


def dot(a, b):
    return jnp.dot(a, b, preferred_element_type=f32)


def dot_rows(a, b):
    return lax.dot_general(a, b, (((0,), (0,)), ((), ())), preferred_element_type=f32)


def shards(hidden, targets, valid, plan, outer_head, drift, ref_head):
    rows_local, width = outer_head.shape
    part = width // FRAGS
    fsdp = lax.axis_size("fsdp")
    me = lax.axis_index("fsdp")
    masks = range(fsdp)

    normed = [normalize(hidden[s]) for s in range(STEPS)]
    features = [
        [columns_at(n, me, rows_local)]
        + [swap(columns_at(n, me ^ m, rows_local), "fsdp", m) for m in masks[1:]]
        for n in normed
    ]
    reference = gather_reference(ref_head)
    refer_log = [log_softmax(capped(dot(n, reference))) for n in normed]

    inner = outer_head + drift[0].astype(f32)
    means = []
    for s in range(STEPS):
        weights = inner.astype(bf16)
        raw = dot(features[s][0], weights)
        for m in masks[1:]:
            raw = raw + swap(dot(features[s][m], weights).astype(logit_type), "fsdp", m).astype(f32)
        grads = logit_grads(capped(raw), refer_log[s], targets[s], valid[s])
        total = dot_rows(features[s][0], grads)
        for m in masks[1:]:
            total = total + dot_rows(features[s][m], swap(grads, "fsdp", m))
        inner = inner - inner_rate * total
        start = plan[s] * part
        delta = lax.dynamic_slice_in_dim(outer_head - inner, start, part, 1)
        means.append(mean_over_replicas(delta))
    first, second = means
    mean = jnp.where(
        plan[0] == 0,
        jnp.concatenate([first, second], 1),
        jnp.concatenate([second, first], 1),
    )
    new_outer = outer_head - outer_rate * mean
    new_inner = mix_weight * inner + (1.0 - mix_weight) * new_outer
    return (new_outer, new_inner[None])


def solution(mesh):
    in_specs = (
        P(None, ("replica", "fsdp"), None),
        P(None, ("replica", "fsdp")),
        P(None, ("replica", "fsdp")),
        P(),
        P("fsdp", None),
        P("replica", "fsdp", None),
        P(("replica", "fsdp"), None),
    )
    out_specs = (P("fsdp", None), P("replica", "fsdp", None))
    return jax.shard_map(shards, mesh=mesh, in_specs=in_specs, out_specs=out_specs, check_vma=False)
```

```python
import math

import jax
import jax.numpy as jnp
from jax import lax
from jax.experimental import pallas as pl
from jax.experimental.pallas import tpu as pltpu
from jax.sharding import PartitionSpec as P

D = 2048
FRAGS = 2
STEPS = 2
CORES = 2
MAJOR = 4

soft_cap = 30.0
kl_weight = 0.5
inner_rate = 0.5
outer_rate = 0.7
mix_weight = 0.5
norm_eps = 1e-05

f32 = jnp.float32
bf16 = jnp.bfloat16
f16 = jnp.float16
logit_type = jnp.float32


def swap(value, axis, mask):
    size = lax.axis_size(axis)
    return lax.ppermute(value, axis, [(i, i ^ mask) for i in range(size)])


def rows_at(value, block, count):
    return lax.dynamic_slice_in_dim(value, block * count, count, 0)


def columns_at(value, block, count):
    return lax.dynamic_slice_in_dim(value, block * count, count, 1)


def place(pieces, spots):
    count = pieces[0].shape[0]
    whole = jnp.zeros((count * len(pieces),) + pieces[0].shape[1:], pieces[0].dtype)
    for piece, spot in zip(pieces, spots):
        whole = lax.dynamic_update_slice_in_dim(whole, piece, spot * count, 0)
    return whole


def in_pair(first, own, other):
    return jnp.where(
        first, jnp.concatenate([own, other], 0), jnp.concatenate([other, own], 0)
    )


def grid_of_replicas():
    chips = lax.axis_size("replica") // CORES
    minor = chips // MAJOR
    me = lax.axis_index("replica")
    return minor, me % CORES, me // (CORES * minor)


def gather_reference(rows):
    minor, core, major = grid_of_replicas()
    fsdp = lax.axis_size("fsdp")
    me = lax.axis_index("fsdp")
    masks = range(fsdp)
    block = place([rows] + [swap(rows, "fsdp", m) for m in masks[1:]], [me ^ m for m in masks])
    spots = lax.axis_index("replica")
    blocks = [(block, spots)]
    step = CORES * minor
    blocks = [(swap(b, "replica", m * step) if m else b, s ^ (m * step)) for b, s in blocks for m in range(MAJOR)]
    mask = CORES
    while mask < step:
        stacked = jnp.concatenate([b for b, _ in blocks], 0)
        other = swap(stacked, "replica", mask)
        blocks = blocks + [
            (p, s ^ mask) for p, (_, s) in zip(jnp.split(other, len(blocks), 0), blocks)
        ]
        mask *= 2
    stacked = jnp.concatenate([b for b, _ in blocks], 0)
    other = swap(stacked, "replica", 1)
    blocks = blocks + [(p, s ^ 1) for p, (_, s) in zip(jnp.split(other, len(blocks), 0), blocks)]
    return place([b for b, _ in blocks], [s for _, s in blocks])


def mean_over_replicas(delta):
    minor, core, major = grid_of_replicas()
    replicas = lax.axis_size("replica")
    delta = delta * (1.0 / replicas)
    half = delta.shape[0] // CORES
    part = rows_at(delta, core, half) + swap(rows_at(delta, 1 - core, half), "replica", 1)
    step = CORES * minor
    quarter = half // MAJOR
    sent = part.astype(f16)
    own = rows_at(part, major, quarter)
    for m in (2, 1, 3):
        own = own + swap(rows_at(sent, major ^ m, quarter), "replica", m * step).astype(f32)
    mask = CORES
    while mask < step:
        own = own + swap(own, "replica", mask)
        mask *= 2
    own = own.astype(f16)
    pieces = [own] + [swap(own, "replica", m * step) for m in (2, 1, 3)]
    gathered = place(pieces, [major ^ m for m in (0, 2, 1, 3)])
    return in_pair(core == 0, gathered, swap(gathered, "replica", 1)).astype(f32)


def normalize(hidden_rows):
    values = hidden_rows.astype(f32)
    factor = lax.rsqrt(jnp.mean(values * values, axis=-1, keepdims=True) + norm_eps)
    return (values * factor).astype(bf16)


def capped(raw):
    return soft_cap * jnp.tanh(raw * (4.0 / math.sqrt(D)) / soft_cap)


def log_softmax(logits):
    return logits - jnp.log(jnp.sum(jnp.exp(logits), axis=-1, keepdims=True))


def logit_grads(policy, refer_log, target_ids, valid_rows):
    policy_log = log_softmax(policy)
    policy_prob = jnp.exp(policy_log)
    diverge = policy_log - refer_log
    kl_value = jnp.sum(policy_prob * diverge, axis=-1, keepdims=True)
    entries = jnp.arange(policy.shape[-1], dtype=jnp.int32)
    onehot = (target_ids[:, None] == entries[None, :]).astype(f32)
    upstream = valid_rows[:, None].astype(f32) * (
        policy_prob - onehot + kl_weight * policy_prob * (diverge - kl_value)
    )
    ratio = policy / soft_cap
    return (upstream * (1.0 - ratio * ratio) * (4.0 / math.sqrt(D))).astype(bf16)


def dot(a, b):
    return jnp.dot(a, b, preferred_element_type=f32)


def dot_rows(a, b):
    return lax.dot_general(a, b, (((0,), (0,)), ((), ())), preferred_element_type=f32)


def shards_any(hidden, targets, valid, plan, outer_head, drift, ref_head):
    rows_local, width = outer_head.shape
    part = width // FRAGS
    fsdp = lax.axis_size("fsdp")
    me = lax.axis_index("fsdp")
    masks = range(fsdp)

    normed = [normalize(hidden[s]) for s in range(STEPS)]
    features = [
        [columns_at(n, me, rows_local)]
        + [swap(columns_at(n, me ^ m, rows_local), "fsdp", m) for m in masks[1:]]
        for n in normed
    ]
    reference = gather_reference(ref_head)
    refer_log = [log_softmax(capped(dot(n, reference))) for n in normed]

    inner = outer_head + drift[0].astype(f32)
    means = []
    for s in range(STEPS):
        weights = inner.astype(bf16)
        raw = dot(features[s][0], weights)
        for m in masks[1:]:
            raw = raw + swap(dot(features[s][m], weights).astype(logit_type), "fsdp", m).astype(f32)
        grads = logit_grads(capped(raw), refer_log[s], targets[s], valid[s])
        total = dot_rows(features[s][0], grads)
        for m in masks[1:]:
            total = total + dot_rows(features[s][m], swap(grads, "fsdp", m))
        inner = inner - inner_rate * total
        start = plan[s] * part
        delta = lax.dynamic_slice_in_dim(outer_head - inner, start, part, 1)
        means.append(mean_over_replicas(delta))
    first, second = means
    mean = jnp.where(
        plan[0] == 0,
        jnp.concatenate([first, second], 1),
        jnp.concatenate([second, first], 1),
    )
    new_outer = outer_head - outer_rate * mean
    new_inner = mix_weight * inner + (1.0 - mix_weight) * new_outer
    return (new_outer, new_inner[None])


def grant(**more):
    return pltpu.CompilerParams(vmem_limit_bytes=40 * 1024 * 1024, **more)


def anywhere(count):
    return [pl.BlockSpec(memory_space=pl.ANY)] * count


def after(value, *earlier):
    def kernel(*refs):
        pass

    return pl.pallas_call(
        kernel,
        out_shape=jax.ShapeDtypeStruct(value.shape, value.dtype),
        in_specs=anywhere(1 + len(earlier)),
        out_specs=pl.BlockSpec(memory_space=pl.ANY),
        input_output_aliases={0: 0},
    )(value, *earlier)


def normalized(hidden, step, spots):
    tokens, width = hidden.shape[1:]
    cols = width // 2
    tile = tokens // 4

    def kernel(spots_ref, hidden_ref, normed_ref, sent_ref):
        normed_ref[...] = normalize(hidden_ref[0])
        other = pl.multiple_of((1 - spots_ref[0]) * cols, cols)
        sent_ref[...] = normed_ref[:, pl.ds(other, cols)]

    return pl.pallas_call(
        kernel,
        out_shape=(
            jax.ShapeDtypeStruct((tokens, width), bf16),
            jax.ShapeDtypeStruct((tokens, cols), bf16),
        ),
        grid_spec=pltpu.PrefetchScalarGridSpec(
            num_scalar_prefetch=1,
            grid=(4,),
            in_specs=[pl.BlockSpec((1, tile, width), lambda i, spots_ref: (step, i, 0))],
            out_specs=(
                pl.BlockSpec((tile, width), lambda i, spots_ref: (i, 0)),
                pl.BlockSpec((tile, cols), lambda i, spots_ref: (i, 0)),
            ),
        ),
        compiler_params=grant(),
        cost_estimate=pl.CostEstimate(flops=4 * tokens * width, bytes_accessed=5 * tokens * width, transcendentals=0),
    )(spots, hidden)


def reference_logs(normed, stacks, spots):
    tokens, width = normed[0].shape
    entries = stacks[0].shape[1]
    rows = width // (2 * 2 * CORES * MAJOR)

    def kernel(spots_ref, first_ref, second_ref, *refs):
        stack_refs = refs[:4]
        out_ref, whole_ref, sems = refs[4:]
        fsdp, me = spots_ref[0], spots_ref[4]
        copies = []
        for number, stack_ref in enumerate(stack_refs):
            bit_core, bit_fsdp = number // 2, number % 2
            for p in range(2 * MAJOR):
                mask = bit_core + (p // MAJOR) * CORES + (p % MAJOR) * 2 * CORES
                block = jnp.bitwise_xor(me, mask) * 2 + jnp.bitwise_xor(fsdp, bit_fsdp)
                copies.append(
                    pltpu.make_async_copy(
                        stack_ref.at[pl.ds(p * rows, rows)],
                        whole_ref.at[pl.ds(pl.multiple_of(block * rows, rows), rows)],
                        sems.at[len(copies)],
                    )
                )
        for copy in copies:
            copy.start()
        for copy in copies:
            copy.wait()
        for step, normed_ref in enumerate((first_ref, second_ref)):
            for half in range(2):
                at = pl.ds(half * (tokens // 2), tokens // 2)
                out_ref[step, at, :] = log_softmax(capped(dot(normed_ref[at, :], whole_ref[...])))

    whole = pl.BlockSpec(memory_space=pltpu.VMEM)
    return pl.pallas_call(
        kernel,
        out_shape=jax.ShapeDtypeStruct((2, tokens, entries), f32),
        in_specs=[pl.BlockSpec(memory_space=pltpu.SMEM), whole, whole] + anywhere(4),
        out_specs=whole,
        scratch_shapes=[pltpu.VMEM((width, entries), bf16), pltpu.SemaphoreType.DMA((32,))],
        compiler_params=grant(),
        cost_estimate=pl.CostEstimate(
            flops=4 * tokens * width * entries, bytes_accessed=4 * width * entries, transcendentals=tokens * entries * 4
        ),
    )(spots, *normed, *stacks)


def gradients(own, received, refer_log, step, target_ids, valid_rows, *earlier):
    tokens, entries = own.shape
    tile = tokens // 2

    def kernel(own_ref, received_ref, refer_ref, target_ref, valid_ref, *refs):
        raw = own_ref[...] + received_ref[...].astype(f32)
        policy = capped(raw)
        policy_log = log_softmax(policy)
        policy_prob = jnp.exp(policy_log)
        diverge = policy_log - refer_ref[0]
        kl_value = jnp.sum(policy_prob * diverge, axis=-1, keepdims=True)
        here = lax.broadcasted_iota(jnp.int32, policy.shape, 1)
        onehot = jnp.where(target_ref[...] == here, 1.0, 0.0)
        upstream = valid_ref[...].astype(f32) * (
            policy_prob - onehot + kl_weight * policy_prob * (diverge - kl_value)
        )
        ratio = policy / soft_cap
        refs[-1][...] = (upstream * (1.0 - ratio * ratio) * (4.0 / math.sqrt(D))).astype(bf16)

    rows = pl.BlockSpec((tile, entries), lambda i: (i, 0))
    single = pl.BlockSpec((tile, 1), lambda i: (i, 0))
    return pl.pallas_call(
        kernel,
        out_shape=jax.ShapeDtypeStruct((tokens, entries), bf16),
        grid=(2,),
        in_specs=[rows, rows, pl.BlockSpec((1, tile, entries), lambda i: (step, i, 0)), single, single]
        + anywhere(len(earlier)),
        out_specs=rows,
        compiler_params=grant(),
        cost_estimate=pl.CostEstimate(
            flops=20 * tokens * entries, bytes_accessed=14 * tokens * entries, transcendentals=3 * tokens * entries
        ),
    )(own, received, refer_log, target_ids[:, None], valid_rows[:, None], *earlier)


def own_update(inner, normed, grads, spots, *earlier):
    rows, entries = inner.shape
    tokens = normed.shape[0]
    tile = rows // 4

    def kernel(spots_ref, inner_ref, normed_ref, grads_ref, *refs):
        refs[-1][...] = inner_ref[...] - inner_rate * dot_rows(normed_ref[...], grads_ref[...])

    return pl.pallas_call(
        kernel,
        out_shape=jax.ShapeDtypeStruct((rows, entries), f32),
        grid_spec=pltpu.PrefetchScalarGridSpec(
            num_scalar_prefetch=1,
            grid=(4,),
            in_specs=[
                pl.BlockSpec((tile, entries), lambda i, spots_ref: (i, 0)),
                pl.BlockSpec((tokens, tile), lambda i, spots_ref: (0, spots_ref[0] * 4 + i)),
                pl.BlockSpec((tokens, entries), lambda i, spots_ref: (0, 0)),
            ]
            + anywhere(len(earlier)),
            out_specs=pl.BlockSpec((tile, entries), lambda i, spots_ref: (i, 0)),
        ),
        compiler_params=grant(),
        cost_estimate=pl.CostEstimate(
            flops=2 * tokens * rows * entries, bytes_accessed=8 * rows * entries, transcendentals=0
        ),
    )(spots, inner, normed, grads, *earlier)


def update(inner, features, grads, outer_head, spots, step, replicas, following=None):
    rows, entries = inner.shape
    tokens = features.shape[0]
    part = entries // FRAGS
    tile = rows // 4
    more = following is not None

    def kernel(spots_ref, inner_ref, features_ref, grads_ref, outer_ref, *refs):
        if more:
            following_ref, new_ref, sent_ref, kept_ref, weights_ref, partial_ref = refs
        else:
            new_ref, sent_ref, kept_ref = refs
        i = pl.program_id(0)
        new_ref[...] = inner_ref[...] - inner_rate * dot_rows(features_ref[...], grads_ref[...])
        at = pl.ds(pl.multiple_of(spots_ref[2 + step] * part, part), part)
        delta = (outer_ref[:, at] - new_ref[:, at]) * (1.0 / replicas)

        @pl.when(i < 2)
        def _():
            sent_ref[...] = delta

        @pl.when(i >= 2)
        def _():
            kept_ref[...] = delta

        if more:
            weights = new_ref[...].astype(bf16)
            weights_ref[...] = weights
            product = dot(following_ref[...], weights)

            @pl.when(i == 0)
            def _():
                partial_ref[...] = product

            @pl.when(i > 0)
            def _():
                partial_ref[...] += product

    def row_tile(i, spots_ref):
        return lax.rem(i + 2 * (1 - spots_ref[1]), 4)

    rows_spec = pl.BlockSpec((tile, entries), lambda i, s: (row_tile(i, s), 0))
    columns_spec = pl.BlockSpec((tokens, tile), lambda i, s: (0, row_tile(i, s)))
    whole_spec = pl.BlockSpec((tokens, entries), lambda i, s: (0, 0))
    in_specs = [rows_spec, columns_spec, whole_spec, rows_spec]
    out_specs = [
        rows_spec,
        pl.BlockSpec((tile, part), lambda i, s: (jnp.minimum(i, 1), 0)),
        pl.BlockSpec((tile, part), lambda i, s: (jnp.maximum(i - 2, 0), 0)),
    ]
    out_shape = [
        jax.ShapeDtypeStruct((rows, entries), f32),
        jax.ShapeDtypeStruct((rows // 2, part), f32),
        jax.ShapeDtypeStruct((rows // 2, part), f32),
    ]
    operands = [inner, features, grads, outer_head]
    if more:
        in_specs += [columns_spec]
        out_specs += [rows_spec, whole_spec]
        out_shape += [
            jax.ShapeDtypeStruct((rows, entries), bf16),
            jax.ShapeDtypeStruct((tokens, entries), f32),
        ]
        operands += [following]
    return pl.pallas_call(
        kernel,
        out_shape=out_shape,
        grid_spec=pltpu.PrefetchScalarGridSpec(
            num_scalar_prefetch=1, grid=(4,), in_specs=in_specs, out_specs=out_specs
        ),
        compiler_params=grant(),
        cost_estimate=pl.CostEstimate(
            flops=(4 if more else 2) * tokens * rows * entries, bytes_accessed=12 * rows * entries, transcendentals=0
        ),
    )(spots, *operands)


def settled(outer_head, inner, means, spots):
    rows, entries = inner.shape
    part = entries // FRAGS
    tile = rows // (CORES * MAJOR)

    def kernel(spots_ref, outer_ref, inner_ref, own0, other0, own1, other1, new_outer_ref, new_inner_ref):
        i = pl.program_id(0)
        mine = i // MAJOR == spots_ref[1]
        for f in range(FRAGS):
            first = spots_ref[2] == f
            at = slice(f * part, (f + 1) * part)
            mean = jnp.where(
                mine,
                jnp.where(first, own0[...], own1[...]),
                jnp.where(first, other0[...], other1[...]),
            )
            fresh = outer_ref[:, at] - outer_rate * mean
            new_outer_ref[:, at] = fresh
            new_inner_ref[:, at] = mix_weight * inner_ref[:, at] + (1.0 - mix_weight) * fresh

    row_spec = pl.BlockSpec((tile, entries), lambda i, s: (i, 0))
    piece_spec = pl.BlockSpec(
        (tile, part), lambda i, s: (jnp.bitwise_xor(lax.rem(i, MAJOR), s[5]), 0)
    )
    return pl.pallas_call(
        kernel,
        out_shape=[jax.ShapeDtypeStruct((rows, entries), f32)] * 2,
        grid_spec=pltpu.PrefetchScalarGridSpec(
            num_scalar_prefetch=1,
            grid=(CORES * MAJOR,),
            in_specs=[row_spec, row_spec] + [piece_spec] * 4,
            out_specs=[row_spec, row_spec],
        ),
        compiler_params=grant(),
        cost_estimate=pl.CostEstimate(
            flops=6 * rows * entries, bytes_accessed=20 * rows * entries, transcendentals=0
        ),
    )(spots, outer_head, inner, *means[0], *means[1])


MASKS = (2, 1, 3)


def gathered_stacks(ref_head):
    step = 2 * CORES
    stacks = []
    for rows in (ref_head, swap(ref_head, "fsdp", 1)):
        along = jnp.concatenate([rows] + [swap(rows, "replica", m * step) for m in range(1, MAJOR)], 0)
        stacks.append(jnp.concatenate([along, swap(along, "replica", CORES)], 0))
    return stacks + [swap(s, "replica", 1) for s in stacks]


def quarters_sum(part, major):
    step = 2 * CORES
    quarter = part.shape[0] // MAJOR
    sent = part.astype(f16)
    own = rows_at(part, major, quarter)
    for m in MASKS:
        own = own + swap(rows_at(sent, major ^ m, quarter), "replica", m * step).astype(f32)
    return own


def quarters_gathered(own):
    step = 2 * CORES
    own = own.astype(f16)
    got = {m: swap(own, "replica", m * step) for m in MASKS}
    return jnp.concatenate([own, got[1], got[2], got[3]], 0).astype(f32)


def shards_pair(hidden, targets, valid, plan, outer_head, drift, ref_head):
    replicas = lax.axis_size("replica")
    fsdp = lax.axis_index("fsdp")
    replica = lax.axis_index("replica")
    core = replica % CORES
    major = replica // (2 * CORES)
    spots = jnp.stack([fsdp, core, plan[0], plan[1], replica, major]).astype(jnp.int32)
    rows = outer_head.shape[0]

    normed, features = [], []
    for s in range(STEPS):
        whole, sent = normalized(hidden, s, spots)
        normed.append(whole)
        features.append(swap(sent, "fsdp", 1))
    stacks = gathered_stacks(ref_head)
    refer_log = reference_logs(normed, stacks, spots)

    inner = outer_head + drift[0].astype(f32)
    weights = inner.astype(bf16)
    partial = dot(features[0], weights)
    own = dot(columns_at(normed[0], fsdp, rows), weights)
    grads = gradients(own, swap(partial.astype(logit_type), "fsdp", 1), refer_log, 0, targets[0], valid[0])
    halfway = own_update(inner, normed[0], grads, spots)
    inner, sent, kept, weights, partial = update(
        halfway, features[0], swap(grads, "fsdp", 1), outer_head, spots, 0, replicas, features[1]
    )

    received = swap(partial.astype(logit_type), "fsdp", 1)
    own = dot(columns_at(normed[1], fsdp, rows), weights)
    summed = kept + swap(sent, "replica", 1)
    grads = gradients(own, received, refer_log, 1, targets[1], valid[1], summed)
    quarter = quarters_sum(summed, major)
    partner_grads = swap(grads, "fsdp", 1)
    halfway = own_update(inner, normed[1], grads, spots, quarter)
    first = quarter + swap(quarter, "replica", CORES)
    inner, sent, kept = update(
        after(halfway, first), features[1], partner_grads, outer_head, spots, 1, replicas
    )

    summed = kept + swap(sent, "replica", 1)
    quarter = quarters_sum(summed, major)
    second = quarter + swap(quarter, "replica", CORES)
    first = quarters_gathered(first)
    second = quarters_gathered(after(second, first))
    means = [(m, swap(m, "replica", 1)) for m in (first, second)]
    new_outer, new_inner = settled(outer_head, inner, means, spots)
    return (new_outer, new_inner[None])


def solution(mesh):
    in_specs = (
        P(None, ("replica", "fsdp"), None),
        P(None, ("replica", "fsdp")),
        P(None, ("replica", "fsdp")),
        P(),
        P("fsdp", None),
        P("replica", "fsdp", None),
        P(("replica", "fsdp"), None),
    )
    out_specs = (P("fsdp", None), P("replica", "fsdp", None))
    chips = mesh.shape["replica"] // CORES
    pairs = mesh.shape["fsdp"] == 2 and chips == 2 * MAJOR
    shards = shards_pair if pairs else shards_any
    return jax.shard_map(shards, mesh=mesh, in_specs=in_specs, out_specs=out_specs, check_vma=False)
```

```python
import math

import jax
import jax.numpy as jnp
from jax import lax
from jax.experimental import pallas as pl
from jax.experimental.pallas import tpu as pltpu
from jax.sharding import PartitionSpec as P

D = 2048
FRAGS = 2
STEPS = 2
CORES = 2
MAJOR = 4

soft_cap = 30.0
kl_weight = 0.5
inner_rate = 0.5
outer_rate = 0.7
mix_weight = 0.5
norm_eps = 1e-05

f32 = jnp.float32
bf16 = jnp.bfloat16
f16 = jnp.float16
logit_type = jnp.float16


def swap(value, axis, mask):
    size = lax.axis_size(axis)
    return lax.ppermute(value, axis, [(i, i ^ mask) for i in range(size)])


def rows_at(value, block, count):
    return lax.dynamic_slice_in_dim(value, block * count, count, 0)


def columns_at(value, block, count):
    return lax.dynamic_slice_in_dim(value, block * count, count, 1)


def place(pieces, spots):
    count = pieces[0].shape[0]
    whole = jnp.zeros((count * len(pieces),) + pieces[0].shape[1:], pieces[0].dtype)
    for piece, spot in zip(pieces, spots):
        whole = lax.dynamic_update_slice_in_dim(whole, piece, spot * count, 0)
    return whole


def in_pair(first, own, other):
    return jnp.where(
        first, jnp.concatenate([own, other], 0), jnp.concatenate([other, own], 0)
    )


def grid_of_replicas():
    chips = lax.axis_size("replica") // CORES
    minor = chips // MAJOR
    me = lax.axis_index("replica")
    return minor, me % CORES, me // (CORES * minor)


def gather_reference(rows):
    minor, core, major = grid_of_replicas()
    fsdp = lax.axis_size("fsdp")
    me = lax.axis_index("fsdp")
    masks = range(fsdp)
    block = place([rows] + [swap(rows, "fsdp", m) for m in masks[1:]], [me ^ m for m in masks])
    spots = lax.axis_index("replica")
    blocks = [(block, spots)]
    step = CORES * minor
    blocks = [(swap(b, "replica", m * step) if m else b, s ^ (m * step)) for b, s in blocks for m in range(MAJOR)]
    mask = CORES
    while mask < step:
        stacked = jnp.concatenate([b for b, _ in blocks], 0)
        other = swap(stacked, "replica", mask)
        blocks = blocks + [
            (p, s ^ mask) for p, (_, s) in zip(jnp.split(other, len(blocks), 0), blocks)
        ]
        mask *= 2
    stacked = jnp.concatenate([b for b, _ in blocks], 0)
    other = swap(stacked, "replica", 1)
    blocks = blocks + [(p, s ^ 1) for p, (_, s) in zip(jnp.split(other, len(blocks), 0), blocks)]
    return place([b for b, _ in blocks], [s for _, s in blocks])


def mean_over_replicas(delta):
    minor, core, major = grid_of_replicas()
    replicas = lax.axis_size("replica")
    delta = delta * (1.0 / replicas)
    half = delta.shape[0] // CORES
    part = rows_at(delta, core, half) + swap(rows_at(delta, 1 - core, half), "replica", 1)
    step = CORES * minor
    quarter = half // MAJOR
    sent = part.astype(f16)
    own = rows_at(part, major, quarter)
    for m in (2, 1, 3):
        own = own + swap(rows_at(sent, major ^ m, quarter), "replica", m * step).astype(f32)
    mask = CORES
    while mask < step:
        own = own + swap(own, "replica", mask)
        mask *= 2
    own = own.astype(f16)
    pieces = [own] + [swap(own, "replica", m * step) for m in (2, 1, 3)]
    gathered = place(pieces, [major ^ m for m in (0, 2, 1, 3)])
    return in_pair(core == 0, gathered, swap(gathered, "replica", 1)).astype(f32)


def normalize(hidden_rows):
    values = hidden_rows.astype(f32)
    factor = lax.rsqrt(jnp.mean(values * values, axis=-1, keepdims=True) + norm_eps)
    return (values * factor).astype(bf16)


def capped(raw):
    return soft_cap * jnp.tanh(raw * (4.0 / math.sqrt(D)) / soft_cap)


def log_softmax(logits):
    return logits - jnp.log(jnp.sum(jnp.exp(logits), axis=-1, keepdims=True))


def logit_grads(policy, refer_log, target_ids, valid_rows):
    policy_log = log_softmax(policy)
    policy_prob = jnp.exp(policy_log)
    diverge = policy_log - refer_log
    kl_value = jnp.sum(policy_prob * diverge, axis=-1, keepdims=True)
    entries = jnp.arange(policy.shape[-1], dtype=jnp.int32)
    onehot = (target_ids[:, None] == entries[None, :]).astype(f32)
    upstream = valid_rows[:, None].astype(f32) * (
        policy_prob - onehot + kl_weight * policy_prob * (diverge - kl_value)
    )
    ratio = policy / soft_cap
    return (upstream * (1.0 - ratio * ratio) * (4.0 / math.sqrt(D))).astype(bf16)


def dot(a, b):
    return jnp.dot(a, b, preferred_element_type=f32)


def dot_rows(a, b):
    return lax.dot_general(a, b, (((0,), (0,)), ((), ())), preferred_element_type=f32)


def shards_any(hidden, targets, valid, plan, outer_head, drift, ref_head):
    rows_local, width = outer_head.shape
    part = width // FRAGS
    fsdp = lax.axis_size("fsdp")
    me = lax.axis_index("fsdp")
    masks = range(fsdp)

    normed = [normalize(hidden[s]) for s in range(STEPS)]
    features = [
        [columns_at(n, me, rows_local)]
        + [swap(columns_at(n, me ^ m, rows_local), "fsdp", m) for m in masks[1:]]
        for n in normed
    ]
    reference = gather_reference(ref_head)
    refer_log = [log_softmax(capped(dot(n, reference))) for n in normed]

    inner = outer_head + drift[0].astype(f32)
    means = []
    for s in range(STEPS):
        weights = inner.astype(bf16)
        raw = dot(features[s][0], weights)
        for m in masks[1:]:
            raw = raw + swap(dot(features[s][m], weights).astype(logit_type), "fsdp", m).astype(f32)
        grads = logit_grads(capped(raw), refer_log[s], targets[s], valid[s])
        total = dot_rows(features[s][0], grads)
        for m in masks[1:]:
            total = total + dot_rows(features[s][m], swap(grads, "fsdp", m))
        inner = inner - inner_rate * total
        start = plan[s] * part
        delta = lax.dynamic_slice_in_dim(outer_head - inner, start, part, 1)
        means.append(mean_over_replicas(delta))
    first, second = means
    mean = jnp.where(
        plan[0] == 0,
        jnp.concatenate([first, second], 1),
        jnp.concatenate([second, first], 1),
    )
    new_outer = outer_head - outer_rate * mean
    new_inner = mix_weight * inner + (1.0 - mix_weight) * new_outer
    return (new_outer, new_inner[None])


MASKS = (2, 1, 3)
VMEM = pl.BlockSpec(memory_space=pltpu.VMEM)
SMEM = pl.BlockSpec(memory_space=pltpu.SMEM)
ANY = pl.BlockSpec(memory_space=pl.ANY)
HBM = pl.BlockSpec(memory_space=pltpu.HBM)


def call(kernel, operands, in_specs, out_shape, out_specs, room, scratch=(), **more):
    return pl.pallas_call(
        kernel,
        out_shape=out_shape,
        in_specs=in_specs,
        out_specs=out_specs,
        scratch_shapes=scratch,
        compiler_params=pltpu.CompilerParams(vmem_limit_bytes=room * 1024 * 1024),
        cost_estimate=pl.CostEstimate(flops=1000, bytes_accessed=1000, transcendentals=0),
        **more,
    )(*operands)


def like(shape, kind):
    return jax.ShapeDtypeStruct(shape, kind)


def after(value, *earlier):
    def kernel(*refs):
        pass

    return call(
        kernel,
        (value,) + earlier,
        [ANY] * (1 + len(earlier)),
        like(value.shape, value.dtype),
        ANY,
        2,
        input_output_aliases={0: 0},
    )


def stacked(pieces):
    rows, cols = pieces[0].shape
    count = len(pieces)

    def kernel(*refs):
        out_ref, sems = refs[count:]
        copies = [
            pltpu.make_async_copy(refs[k], out_ref.at[pl.ds(k * rows, rows)], sems.at[k])
            for k in range(count)
        ]
        for copy in copies:
            copy.start()
        for copy in copies:
            copy.wait()

    return call(
        kernel,
        pieces,
        [ANY] * count,
        like((count * rows, cols), pieces[0].dtype),
        ANY,
        2,
        [pltpu.SemaphoreType.DMA((count,))],
    )


def normalized(hidden, step, spots):
    tokens, width = hidden.shape[1:]
    cols = width // 2
    parts = 4
    tile = tokens // parts

    def kernel(spots_ref, hidden_ref, normed_ref, sent_ref, held_ref, sems):
        other = pl.multiple_of((1 - spots_ref[0]) * cols, cols)
        copies = [
            pltpu.make_async_copy(
                hidden_ref.at[step, pl.ds(k * tile, tile)], held_ref.at[pl.ds(k * tile, tile)], sems.at[k]
            )
            for k in range(parts)
        ]
        for copy in copies:
            copy.start()
        for k, copy in enumerate(copies):
            copy.wait()
            at = pl.ds(k * tile, tile)
            normed_ref[at, :] = normalize(held_ref[at, :])
            sent_ref[at, :] = normed_ref[at, pl.ds(other, cols)]

    return call(
        kernel,
        (spots, hidden),
        [SMEM, HBM],
        (like((tokens, width), bf16), like((tokens, cols), bf16)),
        (VMEM, VMEM),
        8,
        [pltpu.VMEM((tokens, width), bf16), pltpu.SemaphoreType.DMA((parts,))],
    )


def reference_logs(normed, stacks, spots):
    tokens, width = normed.shape
    entries = stacks[0].shape[1]
    rows = stacks[0].shape[0] // MAJOR
    count = len(stacks)

    def kernel(spots_ref, normed_ref, *refs):
        out_ref, whole_ref, sems = refs[count:]
        fsdp, me = spots_ref[0], spots_ref[4]
        copies = []
        for number in range(count):
            bit_fsdp, bit_core, bit_y = number // 4, number // 2 % 2, number % 2
            for p in range(MAJOR):
                mask = bit_core + bit_y * CORES + p * 2 * CORES
                block = jnp.bitwise_xor(me, mask) * 2 + jnp.bitwise_xor(fsdp, bit_fsdp)
                copies.append(
                    pltpu.make_async_copy(
                        refs[number].at[pl.ds(p * rows, rows)],
                        whole_ref.at[pl.ds(pl.multiple_of(block * rows, rows), rows)],
                        sems.at[len(copies)],
                    )
                )
        for copy in copies:
            copy.start()
        for copy in copies:
            copy.wait()
        out_ref[...] = log_softmax(capped(dot(normed_ref[...], whole_ref[...])))

    return call(
        kernel,
        (spots, normed) + tuple(stacks),
        [SMEM, VMEM] + [ANY] * count,
        (like((tokens, entries), f32), like((width, entries), bf16)),
        (VMEM, VMEM),
        8,
        [pltpu.SemaphoreType.DMA((count * MAJOR,))],
    )


def more_reference_logs(normed, whole, *earlier):
    def kernel(normed_ref, whole_ref, *refs):
        refs[-1][...] = log_softmax(capped(dot(normed_ref[...], whole_ref[...])))

    return call(
        kernel,
        (normed, whole) + earlier,
        [VMEM, VMEM] + [ANY] * len(earlier),
        like((normed.shape[0], whole.shape[1]), f32),
        VMEM,
        8,
    )


def starting_weights(outer_head, drift):
    rows, entries = outer_head.shape

    def kernel(outer_ref, drift_ref, inner_ref, weights_ref):
        inner = outer_ref[...] + drift_ref[0].astype(f32)
        inner_ref[...] = inner
        weights_ref[...] = inner.astype(bf16)

    return call(
        kernel,
        (outer_head, drift),
        [VMEM, VMEM],
        (like((rows, entries), f32), like((rows, entries), bf16)),
        (VMEM, VMEM),
        10,
    )


def partial_logits(normed, weights, spots, own, *earlier):
    tokens = normed.shape[0]
    rows, entries = weights.shape

    def kernel(spots_ref, normed_ref, weights_ref, *refs):
        if own:
            values = normed_ref[:, pl.ds(pl.multiple_of(spots_ref[0] * rows, rows), rows)]
        else:
            values = normed_ref[...]
        refs[-1][...] = dot(values, weights_ref[...])

    return call(
        kernel,
        (spots, normed, weights) + earlier,
        [SMEM, VMEM, VMEM] + [ANY] * len(earlier),
        like((tokens, entries), f32),
        VMEM,
        8,
    )


def gradients(own, received, refer_log, target_ids, valid_rows, *earlier):
    tokens, entries = own.shape

    def kernel(own_ref, received_ref, refer_ref, target_ref, valid_ref, *refs):
        raw = own_ref[...] + received_ref[...].astype(f32)
        policy = capped(raw)
        policy_log = log_softmax(policy)
        policy_prob = jnp.exp(policy_log)
        diverge = policy_log - refer_ref[...]
        kl_value = jnp.sum(policy_prob * diverge, axis=-1, keepdims=True)
        here = lax.broadcasted_iota(jnp.int32, policy.shape, 1)
        onehot = jnp.where(target_ref[...] == here, 1.0, 0.0)
        upstream = valid_ref[...].astype(f32) * (
            policy_prob - onehot + kl_weight * policy_prob * (diverge - kl_value)
        )
        ratio = policy / soft_cap
        refs[-1][...] = (upstream * (1.0 - ratio * ratio) * (4.0 / math.sqrt(D))).astype(bf16)

    return call(
        kernel,
        (own, received, refer_log, target_ids[:, None], valid_rows[:, None]) + earlier,
        [VMEM] * 5 + [ANY] * len(earlier),
        like((tokens, entries), bf16),
        VMEM,
        8,
    )


def own_update(inner, normed, grads, spots, *earlier):
    rows, entries = inner.shape
    tile = rows // 4

    def kernel(spots_ref, inner_ref, normed_ref, grads_ref, *refs):
        for k in range(4):
            at = pl.ds(k * tile, tile)
            columns = pl.ds(pl.multiple_of(spots_ref[0] * rows + k * tile, tile), tile)
            refs[-1][at, :] = inner_ref[at, :] - inner_rate * dot_rows(normed_ref[:, columns], grads_ref[...])

    return call(
        kernel,
        (spots, inner, normed, grads) + earlier,
        [SMEM, VMEM, VMEM, VMEM] + [ANY] * len(earlier),
        like((rows, entries), f32),
        VMEM,
        10,
    )


def update(inner, features, grads, outer_head, spots, step, replicas, following=None):
    rows, entries = inner.shape
    tokens = features.shape[0]
    part = entries // FRAGS
    half = rows // 2
    tile = rows // 4
    more = following is not None

    def kernel(spots_ref, inner_ref, features_ref, grads_ref, outer_ref, *refs):
        if more:
            following_ref, new_ref, sent_ref, kept_ref, weights_ref, partial_ref = refs
        else:
            new_ref, sent_ref, kept_ref = refs
        for k in range(4):
            at = pl.ds(k * tile, tile)
            new = inner_ref[at, :] - inner_rate * dot_rows(features_ref[:, at], grads_ref[...])
            new_ref[at, :] = new
            if more:
                weights_ref[at, :] = new.astype(bf16)
        if more:
            partial_ref[...] = dot(following_ref[...], weights_ref[...])
        columns = pl.ds(pl.multiple_of(spots_ref[2 + step] * part, part), part)
        core = spots_ref[1]
        for place_ref, which in ((sent_ref, 1 - core), (kept_ref, core)):
            at = pl.ds(pl.multiple_of(which * half, half), half)
            place_ref[...] = (outer_ref[at, columns] - new_ref[at, columns]) * (1.0 / replicas)

    operands = (spots, inner, features, grads, outer_head)
    out_shape = [like((rows, entries), f32), like((half, part), f32), like((half, part), f32)]
    if more:
        operands += (following,)
        out_shape += [like((rows, entries), bf16), like((tokens, entries), f32)]
    return call(
        kernel,
        operands,
        [SMEM] + [VMEM] * (len(operands) - 1),
        out_shape,
        [VMEM] * len(out_shape),
        14,
    )


def settled(outer_head, inner, means, spots):
    rows, entries = inner.shape
    part = entries // FRAGS
    tile = rows // (CORES * MAJOR)
    steps = 4
    each = CORES * MAJOR // steps

    def kernel(spots_ref, outer_ref, inner_ref, own0, other0, own1, other1, new_outer_ref, new_inner_ref):
        for k in range(each):
            i = pl.program_id(0) * each + k
            mine = i // MAJOR == spots_ref[1]
            there = jnp.bitwise_xor(lax.rem(i, MAJOR), spots_ref[5])
            source = pl.ds(pl.multiple_of(there * tile, tile), tile)
            at = pl.ds(pl.multiple_of(i * tile, tile), tile)
            to = pl.ds(k * tile, tile)
            mean0 = jnp.where(mine, own0[source, :], other0[source, :])
            mean1 = jnp.where(mine, own1[source, :], other1[source, :])
            for f in range(FRAGS):
                columns = pl.ds(f * part, part)
                mean = jnp.where(spots_ref[2] == f, mean0, mean1)
                fresh = outer_ref[at, columns] - outer_rate * mean
                new_outer_ref[to, columns] = fresh
                new_inner_ref[to, columns] = mix_weight * inner_ref[at, columns] + (1.0 - mix_weight) * fresh

    block = pl.BlockSpec((each * tile, entries), lambda i: (i, 0))
    return call(
        kernel,
        (spots, outer_head, inner) + tuple(means[0]) + tuple(means[1]),
        [SMEM] + [VMEM] * 6,
        [like((rows, entries), f32)] * 2,
        [block, block],
        14,
        grid=(steps,),
    )


def gathered_stacks(ref_head, sent, normed):
    step = 2 * CORES
    stacks = []
    for rows in (after(ref_head, normed), swap(after(ref_head, sent), "fsdp", 1)):
        along = stacked([rows] + [swap(rows, "replica", m * step) for m in range(1, MAJOR)])
        both = [along, swap(along, "replica", CORES)]
        stacks += both + [swap(s, "replica", 1) for s in both]
    return stacks


def quarters_sum(part, major):
    step = 2 * CORES
    quarter = part.shape[0] // MAJOR
    sent = part.astype(f16)
    own = rows_at(part, major, quarter)
    for m in MASKS:
        own = own + swap(rows_at(sent, major ^ m, quarter), "replica", m * step).astype(f32)
    return own


def quarters_gathered(own):
    step = 2 * CORES
    got = {m: swap(own, "replica", m * step) for m in MASKS}
    return jnp.concatenate([own, got[1], got[2], got[3]], 0).astype(f32)


def shards_pair(hidden, targets, valid, plan, outer_head, drift, ref_head):
    replicas = lax.axis_size("replica")
    fsdp = lax.axis_index("fsdp")
    replica = lax.axis_index("replica")
    core = replica % CORES
    major = replica // (2 * CORES)
    spots = jnp.stack([fsdp, core, plan[0], plan[1], replica, major]).astype(jnp.int32)

    normed0, sent0 = normalized(hidden, 0, spots)
    features0 = swap(sent0, "fsdp", 1)
    normed1, sent1 = normalized(hidden, 1, spots)
    stacks = gathered_stacks(ref_head, sent0, normed1)

    inner, weights = starting_weights(outer_head, drift)
    partial = partial_logits(features0, weights, spots, False)
    received = swap(partial.astype(logit_type), "fsdp", 1).astype(f32)
    own = partial_logits(normed0, weights, spots, True)
    features1 = swap(after(sent1, received), "fsdp", 1)
    refer_log, whole = reference_logs(normed0, stacks, spots)
    grads = gradients(own, received, refer_log, targets[0], valid[0])
    partner_grads = swap(grads, "fsdp", 1)
    halfway = own_update(inner, normed0, grads, spots)
    refer_log = more_reference_logs(normed1, whole, halfway)
    inner, sent, kept, weights, partial = update(
        halfway, features0, partner_grads, outer_head, spots, 0, replicas, features1
    )

    received = swap(partial.astype(logit_type), "fsdp", 1).astype(f32)
    own = partial_logits(normed1, weights, spots, True)
    summed = kept + swap(sent, "replica", 1)
    grads = gradients(own, received, refer_log, targets[1], valid[1], summed)
    quarter = quarters_sum(summed, major)
    partner_grads = swap(grads, "fsdp", 1)
    halfway = own_update(inner, normed1, grads, spots, quarter)
    first = quarter + swap(quarter, "replica", CORES)
    inner, sent, kept = update(
        halfway, features1, after(partner_grads, first), outer_head, spots, 1, replicas
    )

    summed = kept + swap(sent, "replica", 1)
    quarter = quarters_sum(summed, major)
    second = quarter + swap(quarter, "replica", CORES)
    first = quarters_gathered(first.astype(f16))
    second = quarters_gathered(second.astype(f16))
    means = [(m, swap(m, "replica", 1)) for m in (first, second)]
    new_outer, new_inner = settled(outer_head, inner, means, spots)
    return (new_outer, new_inner[None])


def solution(mesh):
    in_specs = (
        P(None, ("replica", "fsdp"), None),
        P(None, ("replica", "fsdp")),
        P(None, ("replica", "fsdp")),
        P(),
        P("fsdp", None),
        P("replica", "fsdp", None),
        P(("replica", "fsdp"), None),
    )
    out_specs = (P("fsdp", None), P("replica", "fsdp", None))
    chips = mesh.shape["replica"] // CORES
    pairs = mesh.shape["fsdp"] == 2 and chips == 2 * MAJOR
    shards = shards_pair if pairs else shards_any
    return jax.shard_map(shards, mesh=mesh, in_specs=in_specs, out_specs=out_specs, check_vma=False)
```

```python
import math

import jax
import jax.numpy as jnp
from jax import lax
from jax.experimental import pallas as pl
from jax.experimental.pallas import tpu as pltpu
from jax.sharding import PartitionSpec as P

D = 2048
FRAGS = 2
STEPS = 2
CORES = 2
MAJOR = 4

soft_cap = 30.0
kl_weight = 0.5
inner_rate = 0.5
outer_rate = 0.7
mix_weight = 0.5
norm_eps = 1e-05

f32 = jnp.float32
bf16 = jnp.bfloat16
f16 = jnp.float16
logit_type = jnp.float32


def swap(value, axis, mask):
    size = lax.axis_size(axis)
    return lax.ppermute(value, axis, [(i, i ^ mask) for i in range(size)])


def rows_at(value, block, count):
    return lax.dynamic_slice_in_dim(value, block * count, count, 0)


def columns_at(value, block, count):
    return lax.dynamic_slice_in_dim(value, block * count, count, 1)


def place(pieces, spots):
    count = pieces[0].shape[0]
    whole = jnp.zeros((count * len(pieces),) + pieces[0].shape[1:], pieces[0].dtype)
    for piece, spot in zip(pieces, spots):
        whole = lax.dynamic_update_slice_in_dim(whole, piece, spot * count, 0)
    return whole


def in_pair(first, own, other):
    return jnp.where(
        first, jnp.concatenate([own, other], 0), jnp.concatenate([other, own], 0)
    )


def grid_of_replicas():
    chips = lax.axis_size("replica") // CORES
    minor = chips // MAJOR
    me = lax.axis_index("replica")
    return minor, me % CORES, me // (CORES * minor)


def gather_reference(rows):
    minor, core, major = grid_of_replicas()
    fsdp = lax.axis_size("fsdp")
    me = lax.axis_index("fsdp")
    masks = range(fsdp)
    block = place([rows] + [swap(rows, "fsdp", m) for m in masks[1:]], [me ^ m for m in masks])
    spots = lax.axis_index("replica")
    blocks = [(block, spots)]
    step = CORES * minor
    blocks = [(swap(b, "replica", m * step) if m else b, s ^ (m * step)) for b, s in blocks for m in range(MAJOR)]
    mask = CORES
    while mask < step:
        stacked = jnp.concatenate([b for b, _ in blocks], 0)
        other = swap(stacked, "replica", mask)
        blocks = blocks + [
            (p, s ^ mask) for p, (_, s) in zip(jnp.split(other, len(blocks), 0), blocks)
        ]
        mask *= 2
    stacked = jnp.concatenate([b for b, _ in blocks], 0)
    other = swap(stacked, "replica", 1)
    blocks = blocks + [(p, s ^ 1) for p, (_, s) in zip(jnp.split(other, len(blocks), 0), blocks)]
    return place([b for b, _ in blocks], [s for _, s in blocks])


def mean_over_replicas(delta):
    minor, core, major = grid_of_replicas()
    replicas = lax.axis_size("replica")
    delta = delta * (1.0 / replicas)
    half = delta.shape[0] // CORES
    part = rows_at(delta, core, half) + swap(rows_at(delta, 1 - core, half), "replica", 1)
    step = CORES * minor
    quarter = half // MAJOR
    sent = part.astype(f16)
    own = rows_at(part, major, quarter)
    for m in (2, 1, 3):
        own = own + swap(rows_at(sent, major ^ m, quarter), "replica", m * step).astype(f32)
    mask = CORES
    while mask < step:
        own = own + swap(own, "replica", mask)
        mask *= 2
    own = own.astype(f16)
    pieces = [own] + [swap(own, "replica", m * step) for m in (2, 1, 3)]
    gathered = place(pieces, [major ^ m for m in (0, 2, 1, 3)])
    return in_pair(core == 0, gathered, swap(gathered, "replica", 1)).astype(f32)


def normalize(hidden_rows):
    values = hidden_rows.astype(f32)
    factor = lax.rsqrt(jnp.mean(values * values, axis=-1, keepdims=True) + norm_eps)
    return (values * factor).astype(bf16)


def capped(raw):
    return soft_cap * jnp.tanh(raw * (4.0 / math.sqrt(D)) / soft_cap)


def log_softmax(logits):
    return logits - jnp.log(jnp.sum(jnp.exp(logits), axis=-1, keepdims=True))


def logit_grads(policy, refer_log, target_ids, valid_rows):
    policy_log = log_softmax(policy)
    policy_prob = jnp.exp(policy_log)
    diverge = policy_log - refer_log
    kl_value = jnp.sum(policy_prob * diverge, axis=-1, keepdims=True)
    entries = jnp.arange(policy.shape[-1], dtype=jnp.int32)
    onehot = (target_ids[:, None] == entries[None, :]).astype(f32)
    upstream = valid_rows[:, None].astype(f32) * (
        policy_prob - onehot + kl_weight * policy_prob * (diverge - kl_value)
    )
    ratio = policy / soft_cap
    return (upstream * (1.0 - ratio * ratio) * (4.0 / math.sqrt(D))).astype(bf16)


def dot(a, b):
    return jnp.dot(a, b, preferred_element_type=f32)


def dot_rows(a, b):
    return lax.dot_general(a, b, (((0,), (0,)), ((), ())), preferred_element_type=f32)


def shards_any(hidden, targets, valid, plan, outer_head, drift, ref_head):
    rows_local, width = outer_head.shape
    part = width // FRAGS
    fsdp = lax.axis_size("fsdp")
    me = lax.axis_index("fsdp")
    masks = range(fsdp)

    normed = [normalize(hidden[s]) for s in range(STEPS)]
    features = [
        [columns_at(n, me, rows_local)]
        + [swap(columns_at(n, me ^ m, rows_local), "fsdp", m) for m in masks[1:]]
        for n in normed
    ]
    reference = gather_reference(ref_head)
    refer_log = [log_softmax(capped(dot(n, reference))) for n in normed]

    inner = outer_head + drift[0].astype(f32)
    means = []
    for s in range(STEPS):
        weights = inner.astype(bf16)
        raw = dot(features[s][0], weights)
        for m in masks[1:]:
            raw = raw + swap(dot(features[s][m], weights).astype(logit_type), "fsdp", m).astype(f32)
        grads = logit_grads(capped(raw), refer_log[s], targets[s], valid[s])
        total = dot_rows(features[s][0], grads)
        for m in masks[1:]:
            total = total + dot_rows(features[s][m], swap(grads, "fsdp", m))
        inner = inner - inner_rate * total
        start = plan[s] * part
        delta = lax.dynamic_slice_in_dim(outer_head - inner, start, part, 1)
        means.append(mean_over_replicas(delta))
    first, second = means
    mean = jnp.where(
        plan[0] == 0,
        jnp.concatenate([first, second], 1),
        jnp.concatenate([second, first], 1),
    )
    new_outer = outer_head - outer_rate * mean
    new_inner = mix_weight * inner + (1.0 - mix_weight) * new_outer
    return (new_outer, new_inner[None])


MASKS = (2, 1, 3)
VMEM = pl.BlockSpec(memory_space=pltpu.VMEM)
SMEM = pl.BlockSpec(memory_space=pltpu.SMEM)
ANY = pl.BlockSpec(memory_space=pl.ANY)
HBM = pl.BlockSpec(memory_space=pltpu.HBM)


def call(kernel, operands, in_specs, out_shape, out_specs, room, scratch=(), **more):
    return pl.pallas_call(
        kernel,
        out_shape=out_shape,
        in_specs=in_specs,
        out_specs=out_specs,
        scratch_shapes=scratch,
        compiler_params=pltpu.CompilerParams(vmem_limit_bytes=room * 1024 * 1024),
        cost_estimate=pl.CostEstimate(flops=1000, bytes_accessed=1000, transcendentals=0),
        **more,
    )(*operands)


def like(shape, kind):
    return jax.ShapeDtypeStruct(shape, kind)


def after(value, *earlier):
    def kernel(*refs):
        pass

    return call(
        kernel,
        (value,) + earlier,
        [ANY] * (1 + len(earlier)),
        like(value.shape, value.dtype),
        ANY,
        2,
        input_output_aliases={0: 0},
    )


def stacked(pieces):
    rows, cols = pieces[0].shape
    count = len(pieces)

    def kernel(*refs):
        out_ref, sems = refs[count:]
        copies = [
            pltpu.make_async_copy(refs[k], out_ref.at[pl.ds(k * rows, rows)], sems.at[k])
            for k in range(count)
        ]
        for copy in copies:
            copy.start()
        for copy in copies:
            copy.wait()

    return call(
        kernel,
        pieces,
        [ANY] * count,
        like((count * rows, cols), pieces[0].dtype),
        ANY,
        2,
        [pltpu.SemaphoreType.DMA((count,))],
    )


def positions():
    replica = lax.axis_index("replica")
    return lax.axis_index("fsdp"), replica, lax.rem(replica, CORES), replica // (2 * CORES)


LEVEL = math.log(2.0) / 64.0


def scale_of(code):
    return jnp.exp(code.astype(f32) * LEVEL)


def packed_rows(rows):
    return rows + 8


def pack(out_ref, first, second):
    rows = first.shape[0]
    codes, values = [], []
    for x in (first, second):
        top = jnp.maximum(jnp.max(jnp.abs(x), axis=0, keepdims=True), 1e-30)
        code = jnp.ceil(jnp.log(top) * (1.0 / LEVEL)).astype(jnp.int32) + 1
        codes.append(code)
        values.append(jnp.round(x * (32767.0 / scale_of(code))).astype(jnp.int32))
    out_ref[0:rows, :] = (values[0] << 16) | (values[1] & 0xFFFF)
    row = lax.broadcasted_iota(jnp.int32, (8, first.shape[1]), 0)
    out_ref[rows : rows + 8, :] = jnp.where(row == 0, codes[0], codes[1])


def unpack(ref, start=0, rows=None):
    rows = ref.shape[0] - 8 if rows is None else rows
    both = ref[pl.ds(start, rows), :]
    codes = ref[pl.ds(start + rows, 8), :]
    unit = scale_of(codes) * (1.0 / 32767.0)
    return (both >> 16).astype(f32) * unit[0:1, :], ((both << 16) >> 16).astype(f32) * unit[1:2, :]


def column(ref, step):
    row = ref[step : step + 1, :]
    return jnp.broadcast_to(row, (128, row.shape[1])).T[:, 0:1]


def normalized(hidden, step, pieces, room, passed=(), earlier=()):
    tokens, width = hidden.shape[1:]
    cols = width // 2
    parts = 4
    tile = tokens // parts
    each = tokens // pieces

    def kernel(hidden_ref, *refs):
        passed_refs, refs = refs[: len(passed)], refs[len(passed) + len(earlier) :]
        normed_ref, refs = refs[0], refs[1:]
        sent_refs, refs = refs[:pieces], refs[pieces:]
        copy_refs, (held_ref, sems) = refs[: len(passed)], refs[len(passed) :]
        other = pl.multiple_of((1 - lax.axis_index("fsdp")) * cols, cols)
        copies = [
            pltpu.make_async_copy(
                hidden_ref.at[step, pl.ds(k * tile, tile)], held_ref.at[pl.ds(k * tile, tile)], sems.at[k]
            )
            for k in range(parts)
        ]
        for copy in copies:
            copy.start()
        for source, target in zip(passed_refs, copy_refs):
            target[...] = source[...]
        for k, copy in enumerate(copies):
            copy.wait()
            at = pl.ds(k * tile, tile)
            normed_ref[at, :] = normalize(held_ref[at, :])
            sent_refs[k * tile // each][pl.ds(k * tile % each, tile), :] = normed_ref[at, pl.ds(other, cols)]

    return call(
        kernel,
        (hidden,) + passed + earlier,
        [HBM] + [VMEM] * len(passed) + [ANY] * len(earlier),
        [like((tokens, width), bf16)]
        + [like((each, cols), bf16)] * pieces
        + [like(p.shape, p.dtype) for p in passed],
        [VMEM] * (1 + pieces + len(passed)),
        room,
        [pltpu.VMEM((tokens, width), bf16), pltpu.SemaphoreType.DMA((parts,))],
    )


def reference_logs(normed, stacks, *earlier):
    tokens, width = normed.shape
    entries = stacks[0].shape[1]
    rows = stacks[0].shape[0] // MAJOR
    count = len(stacks)

    def kernel(normed_ref, *refs):
        out_ref, whole_ref = refs[count + len(earlier) :]
        fsdp, me, _, _ = positions()
        for number in range(count):
            bit_fsdp, bit_core, bit_y = number // 4, number // 2 % 2, number % 2
            for p in range(MAJOR):
                mask = bit_core + bit_y * CORES + p * 2 * CORES
                block = jnp.bitwise_xor(me, mask) * 2 + jnp.bitwise_xor(fsdp, bit_fsdp)
                to = pl.ds(pl.multiple_of(block * rows, rows), rows)
                whole_ref[to, :] = refs[number][p * rows : (p + 1) * rows, :]
        out_ref[...] = log_softmax(capped(dot(normed_ref[...], whole_ref[...])))

    return call(
        kernel,
        (normed,) + tuple(stacks) + earlier,
        [VMEM] * (1 + count) + [ANY] * len(earlier),
        (like((tokens, entries), f32), like((width, entries), bf16)),
        (VMEM, VMEM),
        10,
    )


def more_reference_logs(normed, whole, *earlier):
    def kernel(normed_ref, whole_ref, *refs):
        refs[-1][...] = log_softmax(capped(dot(normed_ref[...], whole_ref[...])))

    return call(
        kernel,
        (normed, whole) + earlier,
        [VMEM, VMEM] + [ANY] * len(earlier),
        like((normed.shape[0], whole.shape[1]), f32),
        VMEM,
        8,
    )


def starting_weights(outer_head, drift, *earlier):
    rows, entries = outer_head.shape

    def kernel(outer_ref, drift_ref, *refs):
        inner_ref, weights_ref = refs[-2:]
        inner = outer_ref[...] + drift_ref[0].astype(f32)
        inner_ref[...] = inner
        weights_ref[...] = inner.astype(bf16)

    return call(
        kernel,
        (outer_head, drift) + earlier,
        [VMEM, VMEM] + [ANY] * len(earlier),
        (like((rows, entries), f32), like((rows, entries), bf16)),
        (VMEM, VMEM),
        10,
    )


def pack_logits(out_ref, logits):
    half = logits.shape[1] // 2
    pack(out_ref, logits[:, :half], logits[:, half:])


def partner_logits(features, weights):
    tokens = features.shape[0]
    entries = weights.shape[1]

    def kernel(features_ref, weights_ref, out_ref):
        pack_logits(out_ref, dot(features_ref[...], weights_ref[...]))

    return call(
        kernel,
        (features, weights),
        [VMEM, VMEM],
        like((packed_rows(tokens), entries // 2), jnp.int32),
        VMEM,
        8,
    )


def own_logits(normed, weights, *earlier):
    tokens = normed.shape[0]
    rows, entries = weights.shape

    def kernel(normed_ref, weights_ref, *refs):
        at = pl.ds(pl.multiple_of(lax.axis_index("fsdp") * rows, rows), rows)
        refs[-1][...] = dot(normed_ref[:, at], weights_ref[...])

    return call(
        kernel,
        (normed, weights) + earlier,
        [VMEM, VMEM] + [ANY] * len(earlier),
        like((tokens, entries), f32),
        VMEM,
        8,
    )


def gradients(own, received, refer_log, targets, valid, step, *earlier):
    tokens, entries = own.shape

    def kernel(own_ref, received_ref, refer_ref, targets_ref, valid_ref, *refs):
        raw = own_ref[...] + jnp.concatenate(unpack(received_ref), axis=1)
        policy = capped(raw)
        policy_log = log_softmax(policy)
        policy_prob = jnp.exp(policy_log)
        diverge = policy_log - refer_ref[...]
        kl_value = jnp.sum(policy_prob * diverge, axis=-1, keepdims=True)
        here = lax.broadcasted_iota(jnp.int32, policy.shape, 1)
        onehot = jnp.where(column(targets_ref, step) == here, 1.0, 0.0)
        upstream = column(valid_ref, step).astype(f32) * (
            policy_prob - onehot + kl_weight * policy_prob * (diverge - kl_value)
        )
        ratio = policy / soft_cap
        refs[-1][...] = (upstream * (1.0 - ratio * ratio) * (4.0 / math.sqrt(D))).astype(bf16)

    return call(
        kernel,
        (own, received, refer_log, targets, valid) + earlier,
        [VMEM] * 5 + [ANY] * len(earlier),
        like((tokens, entries), bf16),
        VMEM,
        8,
    )


def own_update(inner, normed, grads, *earlier):
    rows, entries = inner.shape
    tile = rows // 4

    def kernel(inner_ref, normed_ref, grads_ref, *refs):
        for k in range(4):
            at = pl.ds(k * tile, tile)
            columns = pl.ds(pl.multiple_of(lax.axis_index("fsdp") * rows + k * tile, tile), tile)
            refs[-1][at, :] = inner_ref[at, :] - inner_rate * dot_rows(normed_ref[:, columns], grads_ref[...])

    return call(
        kernel,
        (inner, normed, grads) + earlier,
        [VMEM] * 3 + [ANY] * len(earlier),
        like((rows, entries), f32),
        VMEM,
        10,
    )


def update(inner, features, grads, outer_head, plan, step, replicas, following=(), earlier=()):
    rows, entries = inner.shape
    tokens = features.shape[0]
    part = entries // FRAGS
    half = rows // 2
    tile = rows // 4
    pieces = len(following)

    def kernel(plan_ref, inner_ref, features_ref, grads_ref, outer_ref, *refs):
        following_refs, refs = refs[:pieces], refs[pieces + len(earlier) :]
        new_ref, sent_ref, kept_ref = refs[:3]
        for k in range(4):
            at = pl.ds(k * tile, tile)
            new = inner_ref[at, :] - inner_rate * dot_rows(features_ref[:, at], grads_ref[...])
            new_ref[at, :] = new
            if pieces:
                refs[4][at, :] = new.astype(bf16)
        if pieces:
            next_ref, weights_ref, partial_ref = refs[3:]
            each = tokens // pieces
            for k, piece_ref in enumerate(following_refs):
                next_ref[k * each : (k + 1) * each, :] = piece_ref[...]
            pack_logits(partial_ref, dot(next_ref[...], weights_ref[...]))
        columns = pl.ds(pl.multiple_of(plan_ref[step] * part, part), part)
        core = positions()[2]
        for place_ref, which in ((sent_ref, 1 - core), (kept_ref, core)):
            at = pl.ds(pl.multiple_of(which * half, half), half)
            place_ref[...] = (outer_ref[at, columns] - new_ref[at, columns]) * (1.0 / replicas)

    operands = (plan, inner, features, grads, outer_head) + tuple(following)
    out_shape = [like((rows, entries), f32), like((half, part), f32), like((half, part), f32)]
    if pieces:
        out_shape += [
            like((tokens, rows), bf16),
            like((rows, entries), bf16),
            like((packed_rows(tokens), entries // 2), jnp.int32),
        ]
    return call(
        kernel,
        operands + tuple(earlier),
        [SMEM] + [VMEM] * (len(operands) - 1) + [ANY] * len(earlier),
        out_shape,
        [VMEM] * len(out_shape),
        16,
    )


def pack_quarter(out_ref, quarter):
    half = quarter.shape[0] // 2
    pack(out_ref, quarter[:half], quarter[half:])


def unpack_quarter(ref, start=0, rows=None):
    return jnp.concatenate(unpack(ref, start, rows), axis=0)


def quarters(kept, received):
    rows, cols = kept.shape
    quarter = rows // MAJOR

    def kernel(kept_ref, received_ref, own_ref, *refs):
        major = positions()[3]

        def piece(mask):
            at = pl.ds(pl.multiple_of(jnp.bitwise_xor(major, mask) * quarter, quarter), quarter)
            return kept_ref[at, :] + received_ref[at, :]

        for mask, out_ref in zip(MASKS, refs):
            pack_quarter(out_ref, piece(mask))
        own_ref[...] = piece(0)

    small = like((packed_rows(quarter // 2), cols), jnp.int32)
    return call(
        kernel,
        (kept, received),
        [VMEM] * 2,
        [like((quarter, cols), f32)] + [small] * len(MASKS),
        [VMEM] * (1 + len(MASKS)),
        6,
    )


def quarter_sum(own, pieces, *earlier):
    def kernel(own_ref, *refs):
        total = own_ref[...]
        for ref in refs[: len(pieces)]:
            total = total + unpack_quarter(ref)
        pack_quarter(refs[-1], total)

    return call(
        kernel,
        (own,) + tuple(pieces) + earlier,
        [VMEM] * (1 + len(pieces)) + [ANY] * len(earlier),
        like(pieces[0].shape, jnp.int32),
        VMEM,
        4,
    )


def pair_sum(one, other):
    def kernel(one_ref, other_ref, out_ref):
        pack_quarter(out_ref, unpack_quarter(one_ref) + unpack_quarter(other_ref))

    return call(kernel, (one, other), [VMEM] * 2, like(one.shape, jnp.int32), VMEM, 4)


def settled(outer_head, inner, means, plan):
    rows, entries = inner.shape
    part = entries // FRAGS
    tile = rows // (CORES * MAJOR)
    steps = CORES * MAJOR
    small = packed_rows(tile // 2)

    def kernel(plan_ref, outer_ref, inner_ref, own0, other0, own1, other1, new_outer_ref, new_inner_ref, *scratch):
        mean_ref, outer_held, inner_held, sems = scratch
        _, _, core, major = positions()
        copies = []
        for i in range(steps):
            start = pl.multiple_of(jnp.bitwise_xor(i % MAJOR, major) * small, small)
            at = pl.ds(i * tile, tile)

            @pl.when(i // MAJOR == core)
            def _():
                mean_ref[0] = unpack_quarter(own0, start, tile // 2)
                mean_ref[1] = unpack_quarter(own1, start, tile // 2)

            @pl.when(i // MAJOR != core)
            def _():
                mean_ref[0] = unpack_quarter(other0, start, tile // 2)
                mean_ref[1] = unpack_quarter(other1, start, tile // 2)

            for f in range(FRAGS):
                columns = pl.ds(f * part, part)
                mean = mean_ref[jnp.where(plan_ref[0] == f, 0, 1)]
                fresh = outer_ref[at, columns] - outer_rate * mean
                outer_held[at, columns] = fresh
                inner_held[at, columns] = mix_weight * inner_ref[at, columns] + (1.0 - mix_weight) * fresh
            for k, (held, out) in enumerate(((outer_held, new_outer_ref), (inner_held, new_inner_ref))):
                copies.append(pltpu.make_async_copy(held.at[at], out.at[at], sems.at[2 * i + k]))
                copies[-1].start()
        for copy in copies:
            copy.wait()

    return call(
        kernel,
        (plan, outer_head, inner) + tuple(means[0]) + tuple(means[1]),
        [SMEM] + [VMEM] * 6,
        [like((rows, entries), f32)] * 2,
        [HBM, HBM],
        14,
        [
            pltpu.VMEM((2, tile, part), f32),
            pltpu.VMEM((rows, entries), f32),
            pltpu.VMEM((rows, entries), f32),
            pltpu.SemaphoreType.DMA((2 * steps,)),
        ],
    )


def gathered_stacks(ref_own, ref_partner):
    step = 2 * CORES
    stacks = []
    for rows in (ref_own, ref_partner):
        along = stacked([rows] + [swap(rows, "replica", m * step) for m in range(1, MAJOR)])
        both = [along, swap(along, "replica", CORES)]
        stacks += both + [swap(s, "replica", 1) for s in both]
    return stacks


def gathered_quarters(own):
    step = 2 * CORES
    got = {m: swap(own, "replica", m * step) for m in MASKS}
    stack = stacked([own, got[1], got[2], got[3]])
    return stack, swap(stack, "replica", 1)


def chip_quarters(sent, kept):
    own, *pieces = quarters(kept, swap(sent, "replica", 1))
    return own, [swap(p, "replica", m * 2 * CORES) for p, m in zip(pieces, MASKS)]


def shards_pair(hidden, targets, valid, plan, outer_head, drift, ref_head):
    replicas = lax.axis_size("replica")

    ref_partner = swap(ref_head, "fsdp", 1)
    normed0, sent0 = normalized(hidden, 0, 1, 60)
    features0 = swap(after(sent0, ref_partner), "fsdp", 1)
    normed1, sent1a, sent1b, *pieces = normalized(hidden, 1, 2, 8, (ref_head, ref_partner), (sent0,))
    features1a = swap(sent1a, "fsdp", 1)
    stacks = gathered_stacks(*pieces)

    inner, weights = starting_weights(outer_head, drift)
    partial = partner_logits(features0, weights)
    received = swap(partial, "fsdp", 1)
    own = own_logits(normed0, weights, partial)
    features1b = swap(after(sent1b, own), "fsdp", 1)
    refer_log, whole = reference_logs(normed0, stacks, features1a)
    grads = gradients(own, received, refer_log, targets, valid, 0)
    partner_grads = swap(grads, "fsdp", 1)
    halfway = own_update(inner, normed0, grads, features1b)
    refer_log = more_reference_logs(normed1, whole, halfway)
    inner, sent, kept, features1, weights, partial = update(
        halfway, features0, partner_grads, outer_head, plan, 0, replicas, (features1a, features1b), (refer_log,)
    )

    received = swap(partial, "fsdp", 1)
    own = own_logits(normed1, weights)
    quarter, pieces = chip_quarters(sent, kept)
    grads = gradients(own, received, refer_log, targets, valid, 1, *pieces)
    partner_grads = swap(grads, "fsdp", 1)
    halfway = own_update(inner, normed1, grads)
    quarter = quarter_sum(quarter, pieces, halfway)
    first = pair_sum(quarter, swap(quarter, "replica", CORES))
    inner, sent, kept = update(
        halfway, features1, partner_grads, outer_head, plan, 1, replicas, (), (first,)
    )

    quarter, pieces = chip_quarters(sent, kept)
    quarter = quarter_sum(quarter, pieces)
    second = pair_sum(quarter, swap(quarter, "replica", CORES))
    means = [gathered_quarters(m) for m in (first, second)]
    new_outer, new_inner = settled(outer_head, inner, means, plan)
    return (new_outer, new_inner[None])


def solution(mesh):
    in_specs = (
        P(None, ("replica", "fsdp"), None),
        P(None, ("replica", "fsdp")),
        P(None, ("replica", "fsdp")),
        P(),
        P("fsdp", None),
        P("replica", "fsdp", None),
        P(("replica", "fsdp"), None),
    )
    out_specs = (P("fsdp", None), P("replica", "fsdp", None))
    chips = mesh.shape["replica"] // CORES
    pairs = mesh.shape["fsdp"] == 2 and chips == 2 * MAJOR
    shards = shards_pair if pairs else shards_any
    return jax.shard_map(shards, mesh=mesh, in_specs=in_specs, out_specs=out_specs, check_vma=False)
```

```python
import math

import jax
import jax.numpy as jnp
from jax import lax
from jax.experimental import pallas as pl
from jax.experimental.pallas import tpu as pltpu
from jax.sharding import PartitionSpec as P

D = 2048
FRAGS = 2
STEPS = 2
CORES = 2
MAJOR = 4

soft_cap = 30.0
kl_weight = 0.5
inner_rate = 0.5
outer_rate = 0.7
mix_weight = 0.5
norm_eps = 1e-05

f32 = jnp.float32
bf16 = jnp.bfloat16
f16 = jnp.float16
logit_type = jnp.float32


def swap(value, axis, mask):
    size = lax.axis_size(axis)
    return lax.ppermute(value, axis, [(i, i ^ mask) for i in range(size)])


def rows_at(value, block, count):
    return lax.dynamic_slice_in_dim(value, block * count, count, 0)


def columns_at(value, block, count):
    return lax.dynamic_slice_in_dim(value, block * count, count, 1)


def place(pieces, spots):
    count = pieces[0].shape[0]
    whole = jnp.zeros((count * len(pieces),) + pieces[0].shape[1:], pieces[0].dtype)
    for piece, spot in zip(pieces, spots):
        whole = lax.dynamic_update_slice_in_dim(whole, piece, spot * count, 0)
    return whole


def in_pair(first, own, other):
    return jnp.where(
        first, jnp.concatenate([own, other], 0), jnp.concatenate([other, own], 0)
    )


def grid_of_replicas():
    chips = lax.axis_size("replica") // CORES
    minor = chips // MAJOR
    me = lax.axis_index("replica")
    return minor, me % CORES, me // (CORES * minor)


def gather_reference(rows):
    minor, core, major = grid_of_replicas()
    fsdp = lax.axis_size("fsdp")
    me = lax.axis_index("fsdp")
    masks = range(fsdp)
    block = place([rows] + [swap(rows, "fsdp", m) for m in masks[1:]], [me ^ m for m in masks])
    spots = lax.axis_index("replica")
    blocks = [(block, spots)]
    step = CORES * minor
    blocks = [(swap(b, "replica", m * step) if m else b, s ^ (m * step)) for b, s in blocks for m in range(MAJOR)]
    mask = CORES
    while mask < step:
        stacked = jnp.concatenate([b for b, _ in blocks], 0)
        other = swap(stacked, "replica", mask)
        blocks = blocks + [
            (p, s ^ mask) for p, (_, s) in zip(jnp.split(other, len(blocks), 0), blocks)
        ]
        mask *= 2
    stacked = jnp.concatenate([b for b, _ in blocks], 0)
    other = swap(stacked, "replica", 1)
    blocks = blocks + [(p, s ^ 1) for p, (_, s) in zip(jnp.split(other, len(blocks), 0), blocks)]
    return place([b for b, _ in blocks], [s for _, s in blocks])


def mean_over_replicas(delta):
    minor, core, major = grid_of_replicas()
    replicas = lax.axis_size("replica")
    delta = delta * (1.0 / replicas)
    half = delta.shape[0] // CORES
    part = rows_at(delta, core, half) + swap(rows_at(delta, 1 - core, half), "replica", 1)
    step = CORES * minor
    quarter = half // MAJOR
    sent = part.astype(f16)
    own = rows_at(part, major, quarter)
    for m in (2, 1, 3):
        own = own + swap(rows_at(sent, major ^ m, quarter), "replica", m * step).astype(f32)
    mask = CORES
    while mask < step:
        own = own + swap(own, "replica", mask)
        mask *= 2
    own = own.astype(f16)
    pieces = [own] + [swap(own, "replica", m * step) for m in (2, 1, 3)]
    gathered = place(pieces, [major ^ m for m in (0, 2, 1, 3)])
    return in_pair(core == 0, gathered, swap(gathered, "replica", 1)).astype(f32)


def normalize(hidden_rows):
    values = hidden_rows.astype(f32)
    factor = lax.rsqrt(jnp.mean(values * values, axis=-1, keepdims=True) + norm_eps)
    return (values * factor).astype(bf16)


def capped(raw):
    return soft_cap * jnp.tanh(raw * (4.0 / math.sqrt(D)) / soft_cap)


def log_softmax(logits):
    return logits - jnp.log(jnp.sum(jnp.exp(logits), axis=-1, keepdims=True))


def logit_grads(policy, refer_log, target_ids, valid_rows):
    policy_log = log_softmax(policy)
    policy_prob = jnp.exp(policy_log)
    diverge = policy_log - refer_log
    kl_value = jnp.sum(policy_prob * diverge, axis=-1, keepdims=True)
    entries = jnp.arange(policy.shape[-1], dtype=jnp.int32)
    onehot = (target_ids[:, None] == entries[None, :]).astype(f32)
    upstream = valid_rows[:, None].astype(f32) * (
        policy_prob - onehot + kl_weight * policy_prob * (diverge - kl_value)
    )
    ratio = policy / soft_cap
    return (upstream * (1.0 - ratio * ratio) * (4.0 / math.sqrt(D))).astype(bf16)


def dot(a, b):
    return jnp.dot(a, b, preferred_element_type=f32)


def dot_rows(a, b):
    return lax.dot_general(a, b, (((0,), (0,)), ((), ())), preferred_element_type=f32)


def shards_any(hidden, targets, valid, plan, outer_head, drift, ref_head):
    rows_local, width = outer_head.shape
    part = width // FRAGS
    fsdp = lax.axis_size("fsdp")
    me = lax.axis_index("fsdp")
    masks = range(fsdp)

    normed = [normalize(hidden[s]) for s in range(STEPS)]
    features = [
        [columns_at(n, me, rows_local)]
        + [swap(columns_at(n, me ^ m, rows_local), "fsdp", m) for m in masks[1:]]
        for n in normed
    ]
    reference = gather_reference(ref_head)
    refer_log = [log_softmax(capped(dot(n, reference))) for n in normed]

    inner = outer_head + drift[0].astype(f32)
    means = []
    for s in range(STEPS):
        weights = inner.astype(bf16)
        raw = dot(features[s][0], weights)
        for m in masks[1:]:
            raw = raw + swap(dot(features[s][m], weights).astype(logit_type), "fsdp", m).astype(f32)
        grads = logit_grads(capped(raw), refer_log[s], targets[s], valid[s])
        total = dot_rows(features[s][0], grads)
        for m in masks[1:]:
            total = total + dot_rows(features[s][m], swap(grads, "fsdp", m))
        inner = inner - inner_rate * total
        start = plan[s] * part
        delta = lax.dynamic_slice_in_dim(outer_head - inner, start, part, 1)
        means.append(mean_over_replicas(delta))
    first, second = means
    mean = jnp.where(
        plan[0] == 0,
        jnp.concatenate([first, second], 1),
        jnp.concatenate([second, first], 1),
    )
    new_outer = outer_head - outer_rate * mean
    new_inner = mix_weight * inner + (1.0 - mix_weight) * new_outer
    return (new_outer, new_inner[None])


MASKS = (2, 1, 3)
VMEM = pl.BlockSpec(memory_space=pltpu.VMEM)
SMEM = pl.BlockSpec(memory_space=pltpu.SMEM)
ANY = pl.BlockSpec(memory_space=pl.ANY)
HBM = pl.BlockSpec(memory_space=pltpu.HBM)


def call(kernel, operands, in_specs, out_shape, out_specs, room, scratch=(), **more):
    return pl.pallas_call(
        kernel,
        out_shape=out_shape,
        in_specs=in_specs,
        out_specs=out_specs,
        scratch_shapes=scratch,
        compiler_params=pltpu.CompilerParams(vmem_limit_bytes=room * 1024 * 1024),
        cost_estimate=pl.CostEstimate(flops=1000, bytes_accessed=1000, transcendentals=0),
        **more,
    )(*operands)


def like(shape, kind):
    return jax.ShapeDtypeStruct(shape, kind)


def after(value, *earlier):
    def kernel(*refs):
        pass

    return call(
        kernel,
        (value,) + earlier,
        [ANY] * (1 + len(earlier)),
        like(value.shape, value.dtype),
        ANY,
        2,
        input_output_aliases={0: 0},
    )


def stacked(pieces):
    rows, cols = pieces[0].shape
    count = len(pieces)

    def kernel(*refs):
        out_ref, sems = refs[count:]
        copies = [
            pltpu.make_async_copy(refs[k], out_ref.at[pl.ds(k * rows, rows)], sems.at[k])
            for k in range(count)
        ]
        for copy in copies:
            copy.start()
        for copy in copies:
            copy.wait()

    return call(
        kernel,
        pieces,
        [ANY] * count,
        like((count * rows, cols), pieces[0].dtype),
        ANY,
        2,
        [pltpu.SemaphoreType.DMA((count,))],
    )


def positions():
    replica = lax.axis_index("replica")
    return lax.axis_index("fsdp"), replica, lax.rem(replica, CORES), replica // (2 * CORES)


LEVEL = math.log(2.0) / 64.0


def scale_of(code):
    return jnp.exp(code.astype(f32) * LEVEL)


def packed_rows(rows):
    return rows + 8


def pack(out_ref, first, second):
    rows = first.shape[0]
    codes, values = [], []
    for x in (first, second):
        top = jnp.maximum(jnp.max(jnp.abs(x), axis=0, keepdims=True), 1e-30)
        code = jnp.ceil(jnp.log(top) * (1.0 / LEVEL)).astype(jnp.int32) + 1
        codes.append(code)
        values.append(jnp.round(x * (32767.0 / scale_of(code))).astype(jnp.int32))
    out_ref[0:rows, :] = (values[0] << 16) | (values[1] & 0xFFFF)
    row = lax.broadcasted_iota(jnp.int32, (8, first.shape[1]), 0)
    out_ref[rows : rows + 8, :] = jnp.where(row == 0, codes[0], codes[1])


def unpack(ref, start=0, rows=None):
    rows = ref.shape[0] - 8 if rows is None else rows
    both = ref[pl.ds(start, rows), :]
    codes = ref[pl.ds(start + rows, 8), :]
    unit = scale_of(codes) * (1.0 / 32767.0)
    return (both >> 16).astype(f32) * unit[0:1, :], ((both << 16) >> 16).astype(f32) * unit[1:2, :]


def column(ref, step):
    row = ref[step : step + 1, :]
    return jnp.broadcast_to(row, (128, row.shape[1])).T[:, 0:1]


def normalized(hidden, sizes, passed=(), folded=(), earlier=()):
    tokens, width = hidden.shape
    cols = width // 2
    tile = 64
    extra = [f.shape[0] * f.shape[1] // cols for f in folded]
    starts = [sum(sizes[:k]) for k in range(len(sizes))]
    lengths = [size + sum(extra) * (k == 0) for k, size in enumerate(sizes)]

    def kernel(hidden_ref, *refs):
        passed_refs, refs = refs[: len(passed)], refs[len(passed) :]
        folded_refs, refs = refs[: len(folded)], refs[len(folded) + len(earlier) :]
        normed_ref, sent_refs, copy_refs = refs[0], refs[1 : 1 + len(sizes)], refs[1 + len(sizes) :]
        other = pl.multiple_of((1 - lax.axis_index("fsdp")) * cols, cols)
        for source, target in zip(passed_refs, copy_refs):
            target[...] = source[...]
        for ref, rows in zip(folded_refs, extra):
            part = ref.shape[1]
            for k in range(cols // part):
                sent_refs[0][sizes[0] : sizes[0] + rows, k * part : (k + 1) * part] = ref[k * rows : (k + 1) * rows, :]
        for start, size, sent_ref in zip(starts, sizes, sent_refs):
            for k in range(0, size, tile):
                at = pl.ds(start + k, tile)
                normed_ref[at, :] = normalize(hidden_ref[at, :])
                sent_ref[k : k + tile, :] = normed_ref[at, pl.ds(other, cols)]

    return call(
        kernel,
        (hidden,) + passed + folded + earlier,
        [VMEM] * (1 + len(passed) + len(folded)) + [ANY] * len(earlier),
        [like((tokens, width), bf16)]
        + [like((length, cols), bf16) for length in lengths]
        + [like(p.shape, p.dtype) for p in passed],
        [VMEM] * (1 + len(sizes) + len(passed)),
        8,
    )


def unfolded(message, start, shape):
    def kernel(message_ref, out_ref):
        rows = message.shape[0] - start
        for k in range(shape[0] // rows):
            out_ref[k * rows : (k + 1) * rows, :] = message_ref[start:, k * shape[1] : (k + 1) * shape[1]]

    return call(kernel, (message,), [VMEM], like(shape, message.dtype), VMEM, 4)


def reference_logs(normed, stacks, *earlier):
    tokens, width = normed.shape
    entries = stacks[0][0].shape[1]
    marks = [m for _, m in stacks]
    stacks = tuple(a for a, _ in stacks)
    rows = stacks[0].shape[0] // len(marks[0])
    count = len(stacks)

    def kernel(normed_ref, *refs):
        out_ref, whole_ref = refs[count + len(earlier) :]
        fsdp, me, _, _ = positions()
        for number in range(count):
            for p, (mask, bit_fsdp) in enumerate(marks[number]):
                block = jnp.bitwise_xor(me, mask) * 2 + jnp.bitwise_xor(fsdp, bit_fsdp)
                to = pl.ds(pl.multiple_of(block * rows, rows), rows)
                whole_ref[to, :] = refs[number][p * rows : (p + 1) * rows, :]
        out_ref[...] = log_softmax(capped(dot(normed_ref[...], whole_ref[...])))

    return call(
        kernel,
        (normed,) + tuple(stacks) + earlier,
        [VMEM] * (1 + count) + [ANY] * len(earlier),
        (like((tokens, entries), f32), like((width, entries), bf16)),
        (VMEM, VMEM),
        10,
    )


def more_reference_logs(normed, whole, *earlier):
    def kernel(normed_ref, whole_ref, *refs):
        refs[-1][...] = log_softmax(capped(dot(normed_ref[...], whole_ref[...])))

    return call(
        kernel,
        (normed, whole) + earlier,
        [VMEM, VMEM] + [ANY] * len(earlier),
        like((normed.shape[0], whole.shape[1]), f32),
        VMEM,
        8,
    )


def starting_weights(outer_head, drift, *earlier):
    rows, entries = outer_head.shape

    def kernel(outer_ref, drift_ref, *refs):
        inner_ref, weights_ref = refs[-2:]
        inner = outer_ref[...] + drift_ref[0].astype(f32)
        inner_ref[...] = inner
        weights_ref[...] = inner.astype(bf16)

    return call(
        kernel,
        (outer_head, drift) + earlier,
        [VMEM, VMEM] + [ANY] * len(earlier),
        (like((rows, entries), f32), like((rows, entries), bf16)),
        (VMEM, VMEM),
        10,
    )


def pack_logits(out_ref, logits):
    half = logits.shape[1] // 2
    pack(out_ref, logits[:, :half], logits[:, half:])


def put_together(out_ref, refs, sizes):
    start = 0
    for ref, size in zip(refs, sizes):
        out_ref[start : start + size, :] = ref[0:size, :]
        start += size


def partner_logits(pieces, sizes, weights):
    tokens, cols = sum(sizes), pieces[0].shape[1]
    entries = weights.shape[1]

    def kernel(weights_ref, *refs):
        features_ref, out_ref = refs[-2:]
        put_together(features_ref, refs[:-2], sizes)
        pack_logits(out_ref, dot(features_ref[...], weights_ref[...]))

    return call(
        kernel,
        (weights,) + tuple(pieces),
        [VMEM] * (1 + len(pieces)),
        (like((tokens, cols), bf16), like((packed_rows(tokens), entries // 2), jnp.int32)),
        (VMEM, VMEM),
        10,
    )


def own_logits(normed, weights, *earlier):
    tokens = normed.shape[0]
    rows, entries = weights.shape

    def kernel(normed_ref, weights_ref, *refs):
        at = pl.ds(pl.multiple_of(lax.axis_index("fsdp") * rows, rows), rows)
        refs[-1][...] = dot(normed_ref[:, at], weights_ref[...])

    return call(
        kernel,
        (normed, weights) + earlier,
        [VMEM, VMEM] + [ANY] * len(earlier),
        like((tokens, entries), f32),
        VMEM,
        8,
    )


def gradients(own, received, refer_log, targets, valid, step, *earlier):
    tokens, entries = own.shape

    def kernel(own_ref, received_ref, refer_ref, targets_ref, valid_ref, *refs):
        raw = own_ref[...] + jnp.concatenate(unpack(received_ref), axis=1)
        policy = capped(raw)
        policy_log = log_softmax(policy)
        policy_prob = jnp.exp(policy_log)
        diverge = policy_log - refer_ref[...]
        kl_value = jnp.sum(policy_prob * diverge, axis=-1, keepdims=True)
        here = lax.broadcasted_iota(jnp.int32, policy.shape, 1)
        onehot = jnp.where(column(targets_ref, step) == here, 1.0, 0.0)
        upstream = column(valid_ref, step).astype(f32) * (
            policy_prob - onehot + kl_weight * policy_prob * (diverge - kl_value)
        )
        ratio = policy / soft_cap
        refs[-1][...] = (upstream * (1.0 - ratio * ratio) * (4.0 / math.sqrt(D))).astype(bf16)

    return call(
        kernel,
        (own, received, refer_log, targets, valid) + earlier,
        [VMEM] * 5 + [ANY] * len(earlier),
        like((tokens, entries), bf16),
        VMEM,
        8,
    )


def own_update(inner, normed, grads, *earlier):
    rows, entries = inner.shape
    tile = rows // 4

    def kernel(inner_ref, normed_ref, grads_ref, *refs):
        for k in range(4):
            at = pl.ds(k * tile, tile)
            columns = pl.ds(pl.multiple_of(lax.axis_index("fsdp") * rows + k * tile, tile), tile)
            refs[-1][at, :] = inner_ref[at, :] - inner_rate * dot_rows(normed_ref[:, columns], grads_ref[...])

    return call(
        kernel,
        (inner, normed, grads) + earlier,
        [VMEM] * 3 + [ANY] * len(earlier),
        like((rows, entries), f32),
        VMEM,
        10,
    )


def update(inner, features, grads, outer_head, plan, step, replicas, following=(), earlier=()):
    rows, entries = inner.shape
    tokens = features.shape[0]
    part = entries // FRAGS
    half = rows // 2
    tile = rows // 4
    pieces = len(following)

    def kernel(plan_ref, inner_ref, features_ref, grads_ref, outer_ref, *refs):
        following_refs, refs = refs[:pieces], refs[pieces + len(earlier) :]
        new_ref, sent_ref, kept_ref = refs[:3]
        for k in range(4):
            at = pl.ds(k * tile, tile)
            new = inner_ref[at, :] - inner_rate * dot_rows(features_ref[:, at], grads_ref[...])
            new_ref[at, :] = new
            if pieces:
                refs[4][at, :] = new.astype(bf16)
        if pieces:
            next_ref, weights_ref, partial_ref = refs[3:]
            put_together(next_ref, following_refs, [f.shape[0] for f in following])
            pack_logits(partial_ref, dot(next_ref[...], weights_ref[...]))
        columns = pl.ds(pl.multiple_of(plan_ref[step] * part, part), part)
        core = positions()[2]
        for place_ref, which in ((sent_ref, 1 - core), (kept_ref, core)):
            at = pl.ds(pl.multiple_of(which * half, half), half)
            place_ref[...] = (outer_ref[at, columns] - new_ref[at, columns]) * (1.0 / replicas)

    operands = (plan, inner, features, grads, outer_head) + tuple(following)
    out_shape = [like((rows, entries), f32), like((half, part), f32), like((half, part), f32)]
    if pieces:
        out_shape += [
            like((tokens, rows), bf16),
            like((rows, entries), bf16),
            like((packed_rows(tokens), entries // 2), jnp.int32),
        ]
    return call(
        kernel,
        operands + tuple(earlier),
        [SMEM] + [VMEM] * (len(operands) - 1) + [ANY] * len(earlier),
        out_shape,
        [VMEM] * len(out_shape),
        16,
    )


def pack_quarter(out_ref, quarter):
    half = quarter.shape[0] // 2
    pack(out_ref, quarter[:half], quarter[half:])


def unpack_quarter(ref, start=0, rows=None):
    return jnp.concatenate(unpack(ref, start, rows), axis=0)


def quarters(kept, received):
    rows, cols = kept.shape
    quarter = rows // MAJOR

    def kernel(kept_ref, received_ref, own_ref, *refs):
        major = positions()[3]

        def piece(mask):
            at = pl.ds(pl.multiple_of(jnp.bitwise_xor(major, mask) * quarter, quarter), quarter)
            return kept_ref[at, :] + received_ref[at, :]

        for mask, out_ref in zip(MASKS, refs):
            pack_quarter(out_ref, piece(mask))
        own_ref[...] = piece(0)

    small = like((packed_rows(quarter // 2), cols), jnp.int32)
    return call(
        kernel,
        (kept, received),
        [VMEM] * 2,
        [like((quarter, cols), f32)] + [small] * len(MASKS),
        [VMEM] * (1 + len(MASKS)),
        6,
    )


def quarter_sum(own, pieces, *earlier):
    def kernel(own_ref, *refs):
        total = own_ref[...]
        for ref in refs[: len(pieces)]:
            total = total + unpack_quarter(ref)
        pack_quarter(refs[-1], total)

    return call(
        kernel,
        (own,) + tuple(pieces) + earlier,
        [VMEM] * (1 + len(pieces)) + [ANY] * len(earlier),
        like(pieces[0].shape, jnp.int32),
        VMEM,
        4,
    )


def pair_sum(one, other, *earlier):
    def kernel(one_ref, other_ref, *refs):
        pack_quarter(refs[-1], unpack_quarter(one_ref) + unpack_quarter(other_ref))

    return call(
        kernel,
        (one, other) + earlier,
        [VMEM] * 2 + [ANY] * len(earlier),
        like(one.shape, jnp.int32),
        VMEM,
        4,
    )


def settled(outer_head, inner, means, plan):
    rows, entries = inner.shape
    part = entries // FRAGS
    tile = rows // (CORES * MAJOR)
    steps = CORES * MAJOR
    small = packed_rows(tile // 2)

    def kernel(plan_ref, outer_ref, inner_ref, own0, other0, own1, other1, new_outer_ref, new_inner_ref, *scratch):
        mean_ref, outer_held, inner_held, sems = scratch
        _, _, core, major = positions()
        copies = []
        for i in range(steps):
            start = pl.multiple_of(jnp.bitwise_xor(i % MAJOR, major) * small, small)
            at = pl.ds(i * tile, tile)

            @pl.when(i // MAJOR == core)
            def _():
                mean_ref[0] = unpack_quarter(own0, start, tile // 2)
                mean_ref[1] = unpack_quarter(own1, start, tile // 2)

            @pl.when(i // MAJOR != core)
            def _():
                mean_ref[0] = unpack_quarter(other0, start, tile // 2)
                mean_ref[1] = unpack_quarter(other1, start, tile // 2)

            for f in range(FRAGS):
                columns = pl.ds(f * part, part)
                mean = mean_ref[jnp.where(plan_ref[0] == f, 0, 1)]
                fresh = outer_ref[at, columns] - outer_rate * mean
                outer_held[at, columns] = fresh
                inner_held[at, columns] = mix_weight * inner_ref[at, columns] + (1.0 - mix_weight) * fresh
            for k, (held, out) in enumerate(((outer_held, new_outer_ref), (inner_held, new_inner_ref))):
                copies.append(pltpu.make_async_copy(held.at[at], out.at[at], sems.at[2 * i + k]))
                copies[-1].start()
        for copy in copies:
            copy.wait()

    return call(
        kernel,
        (plan, outer_head, inner) + tuple(means[0]) + tuple(means[1]),
        [SMEM] + [VMEM] * 6,
        [like((rows, entries), f32)] * 2,
        [HBM, HBM],
        14,
        [
            pltpu.VMEM((2, tile, part), f32),
            pltpu.VMEM((rows, entries), f32),
            pltpu.VMEM((rows, entries), f32),
            pltpu.SemaphoreType.DMA((2 * steps,)),
        ],
    )


def along(stack, *masks):
    array, marks = stack
    return (
        stacked([array] + [swap(array, "replica", m) for m in masks]),
        [(mark ^ m, bit) for m in (0,) + masks for mark, bit in marks],
    )


def across(stack, mask):
    array, marks = stack
    return swap(array, "replica", mask), [(mark ^ mask, bit) for mark, bit in marks]


def gathered_stacks(ref_own, ref_partner):
    along_z = [m * 2 * CORES for m in range(1, MAJOR)]
    stacks = []
    for piece in ((ref_own, [(0, 0)]), (ref_partner, [(0, 1)])):
        first = along(piece, *along_z)
        second = across(first, CORES)
        stacks += [first, second, across(first, 1), across(second, 1)]
    return stacks


def quarters_along(own):
    return [own] + [swap(own, "replica", m * 2 * CORES) for m in range(1, MAJOR)]


def gathered_quarters(pieces):
    stack = stacked(pieces)
    return stack, swap(stack, "replica", 1)


def chip_quarters(sent, kept):
    own, *pieces = quarters(kept, swap(sent, "replica", 1))
    return own, [swap(p, "replica", m * 2 * CORES) for p, m in zip(pieces, MASKS)]


def shards_pair(hidden, targets, valid, plan, outer_head, drift, ref_head):
    replicas = lax.axis_size("replica")

    tokens = hidden.shape[1]
    sizes0 = (tokens // 4, 3 * tokens // 4)
    sizes1 = (tokens // 2, tokens // 2)

    normed0, *sent0 = normalized(hidden[0], sizes0, (), (ref_head,))
    features0 = [swap(s, "fsdp", 1) for s in sent0]
    normed1, sent1a, sent1b, ref_own = normalized(hidden[1], sizes1, (ref_head,), (), tuple(sent0))
    features1a = swap(sent1a, "fsdp", 1)
    stacks = gathered_stacks(ref_own, unfolded(features0[0], sizes0[0], ref_head.shape))

    inner, weights = starting_weights(outer_head, drift, normed1)
    features0, partial = partner_logits(features0, sizes0, weights)
    received = swap(partial, "fsdp", 1)
    own = own_logits(normed0, weights, partial)
    features1b = swap(after(sent1b, partial), "fsdp", 1)
    refer_log, whole = reference_logs(normed0, stacks, features1a)
    grads = gradients(own, received, refer_log, targets, valid, 0)
    partner_grads = swap(grads, "fsdp", 1)
    halfway = own_update(inner, normed0, grads, features1b)
    refer_log = more_reference_logs(normed1, whole, halfway)
    inner, sent, kept, features1, weights, partial = update(
        halfway, features0, partner_grads, outer_head, plan, 0, replicas, (features1a, features1b), (refer_log,)
    )

    received = swap(partial, "fsdp", 1)
    own = own_logits(normed1, weights)
    quarter, pieces = chip_quarters(sent, kept)
    grads = gradients(own, received, refer_log, targets, valid, 1, *pieces)
    partner_grads = swap(grads, "fsdp", 1)
    halfway = own_update(inner, normed1, grads)
    quarter = quarter_sum(quarter, pieces, halfway)
    first = pair_sum(quarter, swap(quarter, "replica", CORES))
    inner, sent, kept = update(
        halfway, features1, partner_grads, outer_head, plan, 1, replicas, (), (first,)
    )

    quarter, pieces = chip_quarters(sent, kept)
    quarter = quarter_sum(quarter, pieces)
    first = quarters_along(first)
    second = pair_sum(quarter, swap(quarter, "replica", CORES), first[1], first[2])
    means = [gathered_quarters(m) for m in (first, quarters_along(second))]
    new_outer, new_inner = settled(outer_head, inner, means, plan)
    return (new_outer, new_inner[None])


def solution(mesh):
    in_specs = (
        P(None, ("replica", "fsdp"), None),
        P(None, ("replica", "fsdp")),
        P(None, ("replica", "fsdp")),
        P(),
        P("fsdp", None),
        P("replica", "fsdp", None),
        P(("replica", "fsdp"), None),
    )
    out_specs = (P("fsdp", None), P("replica", "fsdp", None))
    chips = mesh.shape["replica"] // CORES
    pairs = mesh.shape["fsdp"] == 2 and chips == 2 * MAJOR
    shards = shards_pair if pairs else shards_any
    return jax.shard_map(shards, mesh=mesh, in_specs=in_specs, out_specs=out_specs, check_vma=False)
```

```python
import math

import jax
import jax.numpy as jnp
from jax import lax
from jax.experimental import pallas as pl
from jax.experimental.pallas import tpu as pltpu
from jax.sharding import PartitionSpec as P

D = 2048
FRAGS = 2
STEPS = 2
CORES = 2
MAJOR = 4

soft_cap = 30.0
kl_weight = 0.5
inner_rate = 0.5
outer_rate = 0.7
mix_weight = 0.5
norm_eps = 1e-05

f32 = jnp.float32
bf16 = jnp.bfloat16
f16 = jnp.float16
logit_type = jnp.float32


def swap(value, axis, mask):
    size = lax.axis_size(axis)
    return lax.ppermute(value, axis, [(i, i ^ mask) for i in range(size)])


def rows_at(value, block, count):
    return lax.dynamic_slice_in_dim(value, block * count, count, 0)


def columns_at(value, block, count):
    return lax.dynamic_slice_in_dim(value, block * count, count, 1)


def place(pieces, spots):
    count = pieces[0].shape[0]
    whole = jnp.zeros((count * len(pieces),) + pieces[0].shape[1:], pieces[0].dtype)
    for piece, spot in zip(pieces, spots):
        whole = lax.dynamic_update_slice_in_dim(whole, piece, spot * count, 0)
    return whole


def in_pair(first, own, other):
    return jnp.where(
        first, jnp.concatenate([own, other], 0), jnp.concatenate([other, own], 0)
    )


def grid_of_replicas():
    chips = lax.axis_size("replica") // CORES
    minor = chips // MAJOR
    me = lax.axis_index("replica")
    return minor, me % CORES, me // (CORES * minor)


def gather_reference(rows):
    minor, core, major = grid_of_replicas()
    fsdp = lax.axis_size("fsdp")
    me = lax.axis_index("fsdp")
    masks = range(fsdp)
    block = place([rows] + [swap(rows, "fsdp", m) for m in masks[1:]], [me ^ m for m in masks])
    spots = lax.axis_index("replica")
    blocks = [(block, spots)]
    step = CORES * minor
    blocks = [(swap(b, "replica", m * step) if m else b, s ^ (m * step)) for b, s in blocks for m in range(MAJOR)]
    mask = CORES
    while mask < step:
        stacked = jnp.concatenate([b for b, _ in blocks], 0)
        other = swap(stacked, "replica", mask)
        blocks = blocks + [
            (p, s ^ mask) for p, (_, s) in zip(jnp.split(other, len(blocks), 0), blocks)
        ]
        mask *= 2
    stacked = jnp.concatenate([b for b, _ in blocks], 0)
    other = swap(stacked, "replica", 1)
    blocks = blocks + [(p, s ^ 1) for p, (_, s) in zip(jnp.split(other, len(blocks), 0), blocks)]
    return place([b for b, _ in blocks], [s for _, s in blocks])


def mean_over_replicas(delta):
    minor, core, major = grid_of_replicas()
    replicas = lax.axis_size("replica")
    delta = delta * (1.0 / replicas)
    half = delta.shape[0] // CORES
    part = rows_at(delta, core, half) + swap(rows_at(delta, 1 - core, half), "replica", 1)
    step = CORES * minor
    quarter = half // MAJOR
    sent = part.astype(f16)
    own = rows_at(part, major, quarter)
    for m in (2, 1, 3):
        own = own + swap(rows_at(sent, major ^ m, quarter), "replica", m * step).astype(f32)
    mask = CORES
    while mask < step:
        own = own + swap(own, "replica", mask)
        mask *= 2
    own = own.astype(f16)
    pieces = [own] + [swap(own, "replica", m * step) for m in (2, 1, 3)]
    gathered = place(pieces, [major ^ m for m in (0, 2, 1, 3)])
    return in_pair(core == 0, gathered, swap(gathered, "replica", 1)).astype(f32)


def normalize(hidden_rows):
    values = hidden_rows.astype(f32)
    factor = lax.rsqrt(jnp.mean(values * values, axis=-1, keepdims=True) + norm_eps)
    return (values * factor).astype(bf16)


def capped(raw):
    return soft_cap * jnp.tanh(raw * (4.0 / math.sqrt(D)) / soft_cap)


def log_softmax(logits):
    return logits - jnp.log(jnp.sum(jnp.exp(logits), axis=-1, keepdims=True))


def logit_grads(policy, refer_log, target_ids, valid_rows):
    policy_log = log_softmax(policy)
    policy_prob = jnp.exp(policy_log)
    diverge = policy_log - refer_log
    kl_value = jnp.sum(policy_prob * diverge, axis=-1, keepdims=True)
    entries = jnp.arange(policy.shape[-1], dtype=jnp.int32)
    onehot = (target_ids[:, None] == entries[None, :]).astype(f32)
    upstream = valid_rows[:, None].astype(f32) * (
        policy_prob - onehot + kl_weight * policy_prob * (diverge - kl_value)
    )
    ratio = policy / soft_cap
    return (upstream * (1.0 - ratio * ratio) * (4.0 / math.sqrt(D))).astype(bf16)


def dot(a, b):
    return jnp.dot(a, b, preferred_element_type=f32)


def dot_rows(a, b):
    return lax.dot_general(a, b, (((0,), (0,)), ((), ())), preferred_element_type=f32)


def shards_any(hidden, targets, valid, plan, outer_head, drift, ref_head):
    rows_local, width = outer_head.shape
    part = width // FRAGS
    fsdp = lax.axis_size("fsdp")
    me = lax.axis_index("fsdp")
    masks = range(fsdp)

    normed = [normalize(hidden[s]) for s in range(STEPS)]
    features = [
        [columns_at(n, me, rows_local)]
        + [swap(columns_at(n, me ^ m, rows_local), "fsdp", m) for m in masks[1:]]
        for n in normed
    ]
    reference = gather_reference(ref_head)
    refer_log = [log_softmax(capped(dot(n, reference))) for n in normed]

    inner = outer_head + drift[0].astype(f32)
    means = []
    for s in range(STEPS):
        weights = inner.astype(bf16)
        raw = dot(features[s][0], weights)
        for m in masks[1:]:
            raw = raw + swap(dot(features[s][m], weights).astype(logit_type), "fsdp", m).astype(f32)
        grads = logit_grads(capped(raw), refer_log[s], targets[s], valid[s])
        total = dot_rows(features[s][0], grads)
        for m in masks[1:]:
            total = total + dot_rows(features[s][m], swap(grads, "fsdp", m))
        inner = inner - inner_rate * total
        start = plan[s] * part
        delta = lax.dynamic_slice_in_dim(outer_head - inner, start, part, 1)
        means.append(mean_over_replicas(delta))
    first, second = means
    mean = jnp.where(
        plan[0] == 0,
        jnp.concatenate([first, second], 1),
        jnp.concatenate([second, first], 1),
    )
    new_outer = outer_head - outer_rate * mean
    new_inner = mix_weight * inner + (1.0 - mix_weight) * new_outer
    return (new_outer, new_inner[None])


MASKS = (3, 1, 2)
VMEM = pl.BlockSpec(memory_space=pltpu.VMEM)
SMEM = pl.BlockSpec(memory_space=pltpu.SMEM)
ANY = pl.BlockSpec(memory_space=pl.ANY)
HBM = pl.BlockSpec(memory_space=pltpu.HBM)


def call(kernel, operands, in_specs, out_shape, out_specs, room, scratch=(), **more):
    return pl.pallas_call(
        kernel,
        out_shape=out_shape,
        in_specs=in_specs,
        out_specs=out_specs,
        scratch_shapes=scratch,
        compiler_params=pltpu.CompilerParams(vmem_limit_bytes=room * 1024 * 1024),
        cost_estimate=pl.CostEstimate(flops=1000, bytes_accessed=1000, transcendentals=0),
        **more,
    )(*operands)


def like(shape, kind):
    return jax.ShapeDtypeStruct(shape, kind)


def after(value, *earlier):
    def kernel(*refs):
        pass

    return call(
        kernel,
        (value,) + earlier,
        [ANY] * (1 + len(earlier)),
        like(value.shape, value.dtype),
        ANY,
        2,
        input_output_aliases={0: 0},
    )


def stacked(pieces):
    rows, cols = pieces[0].shape
    count = len(pieces)

    def kernel(*refs):
        out_ref, sems = refs[count:]
        copies = [
            pltpu.make_async_copy(refs[k], out_ref.at[pl.ds(k * rows, rows)], sems.at[k])
            for k in range(count)
        ]
        for copy in copies:
            copy.start()
        for copy in copies:
            copy.wait()

    return call(
        kernel,
        pieces,
        [ANY] * count,
        like((count * rows, cols), pieces[0].dtype),
        ANY,
        2,
        [pltpu.SemaphoreType.DMA((count,))],
    )


def positions():
    replica = lax.axis_index("replica")
    return lax.axis_index("fsdp"), replica, lax.rem(replica, CORES), replica // (2 * CORES)


LEVEL = math.log(2.0) / 64.0


def scale_of(code):
    return jnp.exp(code.astype(f32) * LEVEL)


def packed_rows(rows):
    return rows + 8


def pack(out_ref, first, second):
    rows = first.shape[0]
    codes, values = [], []
    for x in (first, second):
        top = jnp.maximum(jnp.max(jnp.abs(x), axis=0, keepdims=True), 1e-30)
        code = jnp.ceil(jnp.log(top) * (1.0 / LEVEL)).astype(jnp.int32) + 1
        codes.append(code)
        values.append(jnp.round(x * (32767.0 / scale_of(code))).astype(jnp.int32))
    out_ref[0:rows, :] = (values[0] << 16) | (values[1] & 0xFFFF)
    row = lax.broadcasted_iota(jnp.int32, (8, first.shape[1]), 0)
    out_ref[rows : rows + 8, :] = jnp.where(row == 0, codes[0], codes[1])


def unpack(ref, start=0, rows=None):
    rows = ref.shape[0] - 8 if rows is None else rows
    both = ref[pl.ds(start, rows), :]
    codes = ref[pl.ds(start + rows, 8), :]
    unit = scale_of(codes) * (1.0 / 32767.0)
    return (both >> 16).astype(f32) * unit[0:1, :], ((both << 16) >> 16).astype(f32) * unit[1:2, :]


def column(ref, step):
    row = ref[step : step + 1, :]
    return jnp.broadcast_to(row, (128, row.shape[1])).T[:, 0:1]


def normalized(hidden, sizes, passed=(), folded=(), earlier=()):
    tokens, width = hidden.shape
    cols = width // 2
    tile = 64
    extra = [f.shape[0] * f.shape[1] // cols for f in folded]
    starts = [sum(sizes[:k]) for k in range(len(sizes))]
    lengths = [size + sum(extra) * (k == 0) for k, size in enumerate(sizes)]

    def kernel(hidden_ref, *refs):
        passed_refs, refs = refs[: len(passed)], refs[len(passed) :]
        folded_refs, refs = refs[: len(folded)], refs[len(folded) + len(earlier) :]
        normed_ref, sent_refs, copy_refs = refs[0], refs[1 : 1 + len(sizes)], refs[1 + len(sizes) :]
        other = pl.multiple_of((1 - lax.axis_index("fsdp")) * cols, cols)
        for source, target in zip(passed_refs, copy_refs):
            target[...] = source[...]
        for ref, rows in zip(folded_refs, extra):
            part = ref.shape[1]
            for k in range(cols // part):
                sent_refs[0][sizes[0] : sizes[0] + rows, k * part : (k + 1) * part] = ref[k * rows : (k + 1) * rows, :]
        for start, size, sent_ref in zip(starts, sizes, sent_refs):
            for k in range(0, size, tile):
                at = pl.ds(start + k, tile)
                normed_ref[at, :] = normalize(hidden_ref[at, :])
                sent_ref[k : k + tile, :] = normed_ref[at, pl.ds(other, cols)]

    return call(
        kernel,
        (hidden,) + passed + folded + earlier,
        [VMEM] * (1 + len(passed) + len(folded)) + [ANY] * len(earlier),
        [like((tokens, width), bf16)]
        + [like((length, cols), bf16) for length in lengths]
        + [like(p.shape, p.dtype) for p in passed],
        [VMEM] * (1 + len(sizes) + len(passed)),
        8,
    )


def unfolded(message, start, shape):
    def kernel(message_ref, out_ref):
        rows = message.shape[0] - start
        for k in range(shape[0] // rows):
            out_ref[k * rows : (k + 1) * rows, :] = message_ref[start:, k * shape[1] : (k + 1) * shape[1]]

    return call(kernel, (message,), [VMEM], like(shape, message.dtype), VMEM, 4)


def reference_logs(normed, stacks, *earlier):
    tokens, width = normed.shape
    entries = stacks[0][0].shape[1]
    marks = [m for _, m in stacks]
    stacks = tuple(a for a, _ in stacks)
    rows = stacks[0].shape[0] // len(marks[0])
    count = len(stacks)

    def kernel(normed_ref, *refs):
        out_ref, whole_ref = refs[count + len(earlier) :]
        fsdp, me, _, _ = positions()
        for number in range(count):
            for p, (mask, bit_fsdp) in enumerate(marks[number]):
                block = jnp.bitwise_xor(me, mask) * 2 + jnp.bitwise_xor(fsdp, bit_fsdp)
                to = pl.ds(pl.multiple_of(block * rows, rows), rows)
                whole_ref[to, :] = refs[number][p * rows : (p + 1) * rows, :]
        out_ref[...] = log_softmax(capped(dot(normed_ref[...], whole_ref[...])))

    return call(
        kernel,
        (normed,) + tuple(stacks) + earlier,
        [VMEM] * (1 + count) + [ANY] * len(earlier),
        (like((tokens, entries), f32), like((width, entries), bf16)),
        (VMEM, VMEM),
        10,
    )


def more_reference_logs(normed, whole, *earlier):
    def kernel(normed_ref, whole_ref, *refs):
        refs[-1][...] = log_softmax(capped(dot(normed_ref[...], whole_ref[...])))

    return call(
        kernel,
        (normed, whole) + earlier,
        [VMEM, VMEM] + [ANY] * len(earlier),
        like((normed.shape[0], whole.shape[1]), f32),
        VMEM,
        8,
    )


def starting_weights(outer_head, drift, *earlier):
    rows, entries = outer_head.shape

    def kernel(outer_ref, drift_ref, *refs):
        inner_ref, weights_ref = refs[-2:]
        inner = outer_ref[...] + drift_ref[0].astype(f32)
        inner_ref[...] = inner
        weights_ref[...] = inner.astype(bf16)

    return call(
        kernel,
        (outer_head, drift) + earlier,
        [VMEM, VMEM] + [ANY] * len(earlier),
        (like((rows, entries), f32), like((rows, entries), bf16)),
        (VMEM, VMEM),
        10,
    )


def pack_logits(out_ref, logits):
    half = logits.shape[1] // 2
    pack(out_ref, logits[:, :half], logits[:, half:])


def put_together(out_ref, refs, sizes):
    start = 0
    for ref, size in zip(refs, sizes):
        out_ref[start : start + size, :] = ref[0:size, :]
        start += size


def partner_logits(pieces, sizes, weights):
    tokens, cols = sum(sizes), pieces[0].shape[1]
    entries = weights.shape[1]

    def kernel(weights_ref, *refs):
        features_ref, out_ref = refs[-2:]
        put_together(features_ref, refs[:-2], sizes)
        pack_logits(out_ref, dot(features_ref[...], weights_ref[...]))

    return call(
        kernel,
        (weights,) + tuple(pieces),
        [VMEM] * (1 + len(pieces)),
        (like((tokens, cols), bf16), like((packed_rows(tokens), entries // 2), jnp.int32)),
        (VMEM, VMEM),
        10,
    )


def own_logits(normed, weights, *earlier):
    tokens = normed.shape[0]
    rows, entries = weights.shape

    def kernel(normed_ref, weights_ref, *refs):
        at = pl.ds(pl.multiple_of(lax.axis_index("fsdp") * rows, rows), rows)
        refs[-1][...] = dot(normed_ref[:, at], weights_ref[...])

    return call(
        kernel,
        (normed, weights) + earlier,
        [VMEM, VMEM] + [ANY] * len(earlier),
        like((tokens, entries), f32),
        VMEM,
        8,
    )


def gradients(own, received, refer_log, targets, valid, step, *earlier):
    tokens, entries = own.shape

    def kernel(own_ref, received_ref, refer_ref, targets_ref, valid_ref, *refs):
        raw = own_ref[...] + jnp.concatenate(unpack(received_ref), axis=1)
        policy = capped(raw)
        policy_log = log_softmax(policy)
        policy_prob = jnp.exp(policy_log)
        diverge = policy_log - refer_ref[...]
        kl_value = jnp.sum(policy_prob * diverge, axis=-1, keepdims=True)
        here = lax.broadcasted_iota(jnp.int32, policy.shape, 1)
        onehot = jnp.where(column(targets_ref, step) == here, 1.0, 0.0)
        upstream = column(valid_ref, step).astype(f32) * (
            policy_prob - onehot + kl_weight * policy_prob * (diverge - kl_value)
        )
        ratio = policy / soft_cap
        refs[-1][...] = (upstream * (1.0 - ratio * ratio) * (4.0 / math.sqrt(D))).astype(bf16)

    return call(
        kernel,
        (own, received, refer_log, targets, valid) + earlier,
        [VMEM] * 5 + [ANY] * len(earlier),
        like((tokens, entries), bf16),
        VMEM,
        8,
    )


def own_update(inner, normed, grads, *earlier):
    rows, entries = inner.shape
    tile = rows // 4

    def kernel(inner_ref, normed_ref, grads_ref, *refs):
        for k in range(4):
            at = pl.ds(k * tile, tile)
            columns = pl.ds(pl.multiple_of(lax.axis_index("fsdp") * rows + k * tile, tile), tile)
            refs[-1][at, :] = inner_ref[at, :] - inner_rate * dot_rows(normed_ref[:, columns], grads_ref[...])

    return call(
        kernel,
        (inner, normed, grads) + earlier,
        [VMEM] * 3 + [ANY] * len(earlier),
        like((rows, entries), f32),
        VMEM,
        10,
    )


def update(inner, features, grads, outer_head, plan, step, replicas, following=(), earlier=()):
    rows, entries = inner.shape
    tokens = features.shape[0]
    part = entries // FRAGS
    half = rows // 2
    tile = rows // 4
    pieces = len(following)

    def kernel(plan_ref, inner_ref, features_ref, grads_ref, outer_ref, *refs):
        following_refs, refs = refs[:pieces], refs[pieces + len(earlier) :]
        new_ref, sent_ref, kept_ref = refs[:3]
        for k in range(4):
            at = pl.ds(k * tile, tile)
            new = inner_ref[at, :] - inner_rate * dot_rows(features_ref[:, at], grads_ref[...])
            new_ref[at, :] = new
            if pieces:
                refs[4][at, :] = new.astype(bf16)
        if pieces:
            next_ref, weights_ref, partial_ref = refs[3:]
            put_together(next_ref, following_refs, [f.shape[0] for f in following])
            pack_logits(partial_ref, dot(next_ref[...], weights_ref[...]))
        columns = pl.ds(pl.multiple_of(plan_ref[step] * part, part), part)
        core = positions()[2]
        for place_ref, which in ((sent_ref, 1 - core), (kept_ref, core)):
            at = pl.ds(pl.multiple_of(which * half, half), half)
            place_ref[...] = (outer_ref[at, columns] - new_ref[at, columns]) * (1.0 / replicas)

    operands = (plan, inner, features, grads, outer_head) + tuple(following)
    out_shape = [like((rows, entries), f32), like((half, part), f32), like((half, part), f32)]
    if pieces:
        out_shape += [
            like((tokens, rows), bf16),
            like((rows, entries), bf16),
            like((packed_rows(tokens), entries // 2), jnp.int32),
        ]
    return call(
        kernel,
        operands + tuple(earlier),
        [SMEM] + [VMEM] * (len(operands) - 1) + [ANY] * len(earlier),
        out_shape,
        [VMEM] * len(out_shape),
        16,
    )


def pack_quarter(out_ref, quarter):
    half = quarter.shape[0] // 2
    pack(out_ref, quarter[:half], quarter[half:])


def unpack_quarter(ref, start=0, rows=None):
    return jnp.concatenate(unpack(ref, start, rows), axis=0)


def quarters(kept, received):
    rows, cols = kept.shape
    quarter = rows // MAJOR

    def kernel(kept_ref, received_ref, own_ref, *refs):
        major = positions()[3]

        def piece(mask):
            at = pl.ds(pl.multiple_of(jnp.bitwise_xor(major, mask) * quarter, quarter), quarter)
            return kept_ref[at, :] + received_ref[at, :]

        for mask, out_ref in zip(MASKS, refs):
            pack_quarter(out_ref, piece(mask))
        own_ref[...] = piece(0)

    small = like((packed_rows(quarter // 2), cols), jnp.int32)
    return call(
        kernel,
        (kept, received),
        [VMEM] * 2,
        [like((quarter, cols), f32)] + [small] * len(MASKS),
        [VMEM] * (1 + len(MASKS)),
        6,
    )


def quarter_sum(own, pieces, *earlier):
    def kernel(own_ref, *refs):
        total = own_ref[...]
        for ref in refs[: len(pieces)]:
            total = total + unpack_quarter(ref)
        pack_quarter(refs[-1], total)

    return call(
        kernel,
        (own,) + tuple(pieces) + earlier,
        [VMEM] * (1 + len(pieces)) + [ANY] * len(earlier),
        like(pieces[0].shape, jnp.int32),
        VMEM,
        4,
    )


def pair_sum(one, other, *earlier):
    def kernel(one_ref, other_ref, *refs):
        pack_quarter(refs[-1], unpack_quarter(one_ref) + unpack_quarter(other_ref))

    return call(
        kernel,
        (one, other) + earlier,
        [VMEM] * 2 + [ANY] * len(earlier),
        like(one.shape, jnp.int32),
        VMEM,
        4,
    )


def settled(outer_head, inner, means, plan):
    rows, entries = inner.shape
    part = entries // FRAGS
    tile = rows // (CORES * MAJOR)
    steps = CORES * MAJOR
    small = packed_rows(tile // 2)

    def kernel(plan_ref, outer_ref, inner_ref, own0, other0, own1, other1, new_outer_ref, new_inner_ref, *scratch):
        mean_ref, outer_held, inner_held, sems = scratch
        _, _, core, major = positions()
        copies = []
        for i in range(steps):
            start = pl.multiple_of(jnp.bitwise_xor(i % MAJOR, major) * small, small)
            at = pl.ds(i * tile, tile)

            @pl.when(i // MAJOR == core)
            def _():
                mean_ref[0] = unpack_quarter(own0, start, tile // 2)
                mean_ref[1] = unpack_quarter(own1, start, tile // 2)

            @pl.when(i // MAJOR != core)
            def _():
                mean_ref[0] = unpack_quarter(other0, start, tile // 2)
                mean_ref[1] = unpack_quarter(other1, start, tile // 2)

            for f in range(FRAGS):
                columns = pl.ds(f * part, part)
                mean = mean_ref[jnp.where(plan_ref[0] == f, 0, 1)]
                fresh = outer_ref[at, columns] - outer_rate * mean
                outer_held[at, columns] = fresh
                inner_held[at, columns] = mix_weight * inner_ref[at, columns] + (1.0 - mix_weight) * fresh
            for k, (held, out) in enumerate(((outer_held, new_outer_ref), (inner_held, new_inner_ref))):
                copies.append(pltpu.make_async_copy(held.at[at], out.at[at], sems.at[2 * i + k]))
                copies[-1].start()
        for copy in copies:
            copy.wait()

    return call(
        kernel,
        (plan, outer_head, inner) + tuple(means[0]) + tuple(means[1]),
        [SMEM] + [VMEM] * 6,
        [like((rows, entries), f32)] * 2,
        [HBM, HBM],
        14,
        [
            pltpu.VMEM((2, tile, part), f32),
            pltpu.VMEM((rows, entries), f32),
            pltpu.VMEM((rows, entries), f32),
            pltpu.SemaphoreType.DMA((2 * steps,)),
        ],
    )


def along(stack, *masks):
    array, marks = stack
    return (
        stacked([array] + [swap(array, "replica", m) for m in masks]),
        [(mark ^ m, bit) for m in (0,) + masks for mark, bit in marks],
    )


def across(stack, mask):
    array, marks = stack
    return swap(array, "replica", mask), [(mark ^ mask, bit) for mark, bit in marks]


def gathered_stacks(ref_own, ref_partner):
    along_z = [m * 2 * CORES for m in range(1, MAJOR)]
    stacks = []
    for piece in ((ref_own, [(0, 0)]), (ref_partner, [(0, 1)])):
        first = along(piece, *along_z)
        second = across(first, CORES)
        stacks += [first, second, across(first, 1), across(second, 1)]
    return stacks


def quarters_along(own):
    return [own] + [swap(own, "replica", m * 2 * CORES) for m in range(1, MAJOR)]


def gathered_quarters(pieces):
    stack = stacked(pieces)
    return stack, swap(stack, "replica", 1)


def chip_quarters(sent, kept):
    own, *pieces = quarters(kept, swap(sent, "replica", 1))
    return own, [swap(p, "replica", m * 2 * CORES) for p, m in zip(pieces, MASKS)]


def shards_pair(hidden, targets, valid, plan, outer_head, drift, ref_head):
    replicas = lax.axis_size("replica")

    tokens = hidden.shape[1]
    sizes0 = (tokens // 4, 3 * tokens // 4)
    sizes1 = (tokens // 2, tokens // 2)

    normed0, *sent0 = normalized(hidden[0], sizes0, (), (ref_head,))
    features0 = [swap(s, "fsdp", 1) for s in sent0]
    normed1, sent1a, sent1b, ref_own = normalized(hidden[1], sizes1, (ref_head,), (), tuple(sent0))
    features1a = swap(sent1a, "fsdp", 1)
    stacks = gathered_stacks(ref_own, unfolded(features0[0], sizes0[0], ref_head.shape))

    inner, weights = starting_weights(outer_head, drift, normed1)
    features0, partial = partner_logits(features0, sizes0, weights)
    received = swap(partial, "fsdp", 1)
    own = own_logits(normed0, weights, partial)
    features1b = swap(after(sent1b, partial), "fsdp", 1)
    refer_log, whole = reference_logs(normed0, stacks, features1a)
    grads = gradients(own, received, refer_log, targets, valid, 0)
    partner_grads = swap(grads, "fsdp", 1)
    halfway = own_update(inner, normed0, grads, features1b)
    refer_log = more_reference_logs(normed1, whole, halfway)
    inner, sent, kept, features1, weights, partial = update(
        halfway, features0, partner_grads, outer_head, plan, 0, replicas, (features1a, features1b), (refer_log,)
    )

    received = swap(partial, "fsdp", 1)
    own = own_logits(normed1, weights)
    quarter, pieces = chip_quarters(sent, kept)
    grads = gradients(own, received, refer_log, targets, valid, 1, pieces[0])
    partner_grads = swap(grads, "fsdp", 1)
    halfway = own_update(inner, normed1, grads)
    quarter = quarter_sum(quarter, pieces, halfway)
    first = pair_sum(quarter, swap(quarter, "replica", CORES))
    inner, sent, kept = update(
        halfway, features1, partner_grads, outer_head, plan, 1, replicas, (), (quarter,)
    )

    quarter, pieces = chip_quarters(sent, kept)
    quarter = quarter_sum(quarter, pieces)
    first = quarters_along(first)
    second = pair_sum(quarter, swap(quarter, "replica", CORES), first[1], first[2])
    means = [gathered_quarters(m) for m in (first, quarters_along(second))]
    new_outer, new_inner = settled(outer_head, inner, means, plan)
    return (new_outer, new_inner[None])


def solution(mesh):
    in_specs = (
        P(None, ("replica", "fsdp"), None),
        P(None, ("replica", "fsdp")),
        P(None, ("replica", "fsdp")),
        P(),
        P("fsdp", None),
        P("replica", "fsdp", None),
        P(("replica", "fsdp"), None),
    )
    out_specs = (P("fsdp", None), P("replica", "fsdp", None))
    chips = mesh.shape["replica"] // CORES
    pairs = mesh.shape["fsdp"] == 2 and chips == 2 * MAJOR
    shards = shards_pair if pairs else shards_any
    return jax.shard_map(shards, mesh=mesh, in_specs=in_specs, out_specs=out_specs, check_vma=False)
```

```python
import math

import jax
import jax.numpy as jnp
from jax import lax
from jax.experimental import pallas as pl
from jax.experimental.pallas import tpu as pltpu
from jax.sharding import PartitionSpec as P

D = 2048
FRAGS = 2
STEPS = 2
CORES = 2
MAJOR = 4

soft_cap = 30.0
kl_weight = 0.5
inner_rate = 0.5
outer_rate = 0.7
mix_weight = 0.5
norm_eps = 1e-05

f32 = jnp.float32
bf16 = jnp.bfloat16
f16 = jnp.float16
logit_type = jnp.float32


def swap(value, axis, mask):
    size = lax.axis_size(axis)
    return lax.ppermute(value, axis, [(i, i ^ mask) for i in range(size)])


def rows_at(value, block, count):
    return lax.dynamic_slice_in_dim(value, block * count, count, 0)


def columns_at(value, block, count):
    return lax.dynamic_slice_in_dim(value, block * count, count, 1)


def place(pieces, spots):
    count = pieces[0].shape[0]
    whole = jnp.zeros((count * len(pieces),) + pieces[0].shape[1:], pieces[0].dtype)
    for piece, spot in zip(pieces, spots):
        whole = lax.dynamic_update_slice_in_dim(whole, piece, spot * count, 0)
    return whole


def in_pair(first, own, other):
    return jnp.where(
        first, jnp.concatenate([own, other], 0), jnp.concatenate([other, own], 0)
    )


def grid_of_replicas():
    chips = lax.axis_size("replica") // CORES
    minor = chips // MAJOR
    me = lax.axis_index("replica")
    return minor, me % CORES, me // (CORES * minor)


def gather_reference(rows):
    minor, core, major = grid_of_replicas()
    fsdp = lax.axis_size("fsdp")
    me = lax.axis_index("fsdp")
    masks = range(fsdp)
    block = place([rows] + [swap(rows, "fsdp", m) for m in masks[1:]], [me ^ m for m in masks])
    spots = lax.axis_index("replica")
    blocks = [(block, spots)]
    step = CORES * minor
    blocks = [(swap(b, "replica", m * step) if m else b, s ^ (m * step)) for b, s in blocks for m in range(MAJOR)]
    mask = CORES
    while mask < step:
        stacked = jnp.concatenate([b for b, _ in blocks], 0)
        other = swap(stacked, "replica", mask)
        blocks = blocks + [
            (p, s ^ mask) for p, (_, s) in zip(jnp.split(other, len(blocks), 0), blocks)
        ]
        mask *= 2
    stacked = jnp.concatenate([b for b, _ in blocks], 0)
    other = swap(stacked, "replica", 1)
    blocks = blocks + [(p, s ^ 1) for p, (_, s) in zip(jnp.split(other, len(blocks), 0), blocks)]
    return place([b for b, _ in blocks], [s for _, s in blocks])


def mean_over_replicas(delta):
    minor, core, major = grid_of_replicas()
    replicas = lax.axis_size("replica")
    delta = delta * (1.0 / replicas)
    half = delta.shape[0] // CORES
    part = rows_at(delta, core, half) + swap(rows_at(delta, 1 - core, half), "replica", 1)
    step = CORES * minor
    quarter = half // MAJOR
    sent = part.astype(f16)
    own = rows_at(part, major, quarter)
    for m in (2, 1, 3):
        own = own + swap(rows_at(sent, major ^ m, quarter), "replica", m * step).astype(f32)
    mask = CORES
    while mask < step:
        own = own + swap(own, "replica", mask)
        mask *= 2
    own = own.astype(f16)
    pieces = [own] + [swap(own, "replica", m * step) for m in (2, 1, 3)]
    gathered = place(pieces, [major ^ m for m in (0, 2, 1, 3)])
    return in_pair(core == 0, gathered, swap(gathered, "replica", 1)).astype(f32)


def normalize(hidden_rows):
    values = hidden_rows.astype(f32)
    factor = lax.rsqrt(jnp.mean(values * values, axis=-1, keepdims=True) + norm_eps)
    return (values * factor).astype(bf16)


def capped(raw):
    return soft_cap * jnp.tanh(raw * (4.0 / math.sqrt(D)) / soft_cap)


def log_softmax(logits):
    return logits - jnp.log(jnp.sum(jnp.exp(logits), axis=-1, keepdims=True))


def logit_grads(policy, refer_log, target_ids, valid_rows):
    policy_log = log_softmax(policy)
    policy_prob = jnp.exp(policy_log)
    diverge = policy_log - refer_log
    kl_value = jnp.sum(policy_prob * diverge, axis=-1, keepdims=True)
    entries = jnp.arange(policy.shape[-1], dtype=jnp.int32)
    onehot = (target_ids[:, None] == entries[None, :]).astype(f32)
    upstream = valid_rows[:, None].astype(f32) * (
        policy_prob - onehot + kl_weight * policy_prob * (diverge - kl_value)
    )
    ratio = policy / soft_cap
    return (upstream * (1.0 - ratio * ratio) * (4.0 / math.sqrt(D))).astype(bf16)


def dot(a, b):
    return jnp.dot(a, b, preferred_element_type=f32)


def dot_rows(a, b):
    return lax.dot_general(a, b, (((0,), (0,)), ((), ())), preferred_element_type=f32)


def shards_any(hidden, targets, valid, plan, outer_head, drift, ref_head):
    rows_local, width = outer_head.shape
    part = width // FRAGS
    fsdp = lax.axis_size("fsdp")
    me = lax.axis_index("fsdp")
    masks = range(fsdp)

    normed = [normalize(hidden[s]) for s in range(STEPS)]
    features = [
        [columns_at(n, me, rows_local)]
        + [swap(columns_at(n, me ^ m, rows_local), "fsdp", m) for m in masks[1:]]
        for n in normed
    ]
    reference = gather_reference(ref_head)
    refer_log = [log_softmax(capped(dot(n, reference))) for n in normed]

    inner = outer_head + drift[0].astype(f32)
    means = []
    for s in range(STEPS):
        weights = inner.astype(bf16)
        raw = dot(features[s][0], weights)
        for m in masks[1:]:
            raw = raw + swap(dot(features[s][m], weights).astype(logit_type), "fsdp", m).astype(f32)
        grads = logit_grads(capped(raw), refer_log[s], targets[s], valid[s])
        total = dot_rows(features[s][0], grads)
        for m in masks[1:]:
            total = total + dot_rows(features[s][m], swap(grads, "fsdp", m))
        inner = inner - inner_rate * total
        start = plan[s] * part
        delta = lax.dynamic_slice_in_dim(outer_head - inner, start, part, 1)
        means.append(mean_over_replicas(delta))
    first, second = means
    mean = jnp.where(
        plan[0] == 0,
        jnp.concatenate([first, second], 1),
        jnp.concatenate([second, first], 1),
    )
    new_outer = outer_head - outer_rate * mean
    new_inner = mix_weight * inner + (1.0 - mix_weight) * new_outer
    return (new_outer, new_inner[None])


MASKS = (3, 2, 1)
COST = {
    "stacked": 5000000000,
    "more_reference_logs": 100000000,
    "own_logits": 100000000,
    "own_update": 5000000000,
    "update": 1000000000,
}
VMEM = pl.BlockSpec(memory_space=pltpu.VMEM)
SMEM = pl.BlockSpec(memory_space=pltpu.SMEM)
ANY = pl.BlockSpec(memory_space=pl.ANY)
HBM = pl.BlockSpec(memory_space=pltpu.HBM)


def call(kernel, operands, in_specs, out_shape, out_specs, room, scratch=(), **more):
    return pl.pallas_call(
        kernel,
        out_shape=out_shape,
        in_specs=in_specs,
        out_specs=out_specs,
        scratch_shapes=scratch,
        compiler_params=pltpu.CompilerParams(vmem_limit_bytes=room * 1024 * 1024),
        cost_estimate=pl.CostEstimate(flops=COST.get(kernel.__qualname__.split(".")[0], 1000), bytes_accessed=1000, transcendentals=0),
        **more,
    )(*operands)


def like(shape, kind):
    return jax.ShapeDtypeStruct(shape, kind)


def after(value, *earlier):
    def kernel(*refs):
        pass

    return call(
        kernel,
        (value,) + earlier,
        [ANY] * (1 + len(earlier)),
        like(value.shape, value.dtype),
        ANY,
        2,
        input_output_aliases={0: 0},
    )


def stacked(pieces):
    rows, cols = pieces[0].shape
    count = len(pieces)

    def kernel(*refs):
        out_ref, sems = refs[count:]
        copies = [
            pltpu.make_async_copy(refs[k], out_ref.at[pl.ds(k * rows, rows)], sems.at[k])
            for k in range(count)
        ]
        for copy in copies:
            copy.start()
        for copy in copies:
            copy.wait()

    return call(
        kernel,
        pieces,
        [ANY] * count,
        like((count * rows, cols), pieces[0].dtype),
        ANY,
        2,
        [pltpu.SemaphoreType.DMA((count,))],
    )


def positions():
    replica = lax.axis_index("replica")
    return lax.axis_index("fsdp"), replica, lax.rem(replica, CORES), replica // (2 * CORES)


LEVEL = math.log(2.0) / 64.0


def scale_of(code):
    return jnp.exp(code.astype(f32) * LEVEL)


def packed_rows(rows):
    return rows + 8


def pack(out_ref, first, second):
    rows = first.shape[0]
    codes, values = [], []
    for x in (first, second):
        top = jnp.maximum(jnp.max(jnp.abs(x), axis=0, keepdims=True), 1e-30)
        code = jnp.ceil(jnp.log(top) * (1.0 / LEVEL)).astype(jnp.int32) + 1
        codes.append(code)
        values.append(jnp.round(x * (32767.0 / scale_of(code))).astype(jnp.int32))
    out_ref[0:rows, :] = (values[0] << 16) | (values[1] & 0xFFFF)
    row = lax.broadcasted_iota(jnp.int32, (8, first.shape[1]), 0)
    out_ref[rows : rows + 8, :] = jnp.where(row == 0, codes[0], codes[1])


def unpack(ref, start=0, rows=None):
    rows = ref.shape[0] - 8 if rows is None else rows
    both = ref[pl.ds(start, rows), :]
    codes = ref[pl.ds(start + rows, 8), :]
    unit = scale_of(codes) * (1.0 / 32767.0)
    return (both >> 16).astype(f32) * unit[0:1, :], ((both << 16) >> 16).astype(f32) * unit[1:2, :]


def column(ref, step):
    row = ref[step : step + 1, :]
    return jnp.broadcast_to(row, (128, row.shape[1])).T[:, 0:1]


def normalized(hidden, sizes, passed=(), folded=(), earlier=()):
    tokens, width = hidden.shape
    cols = width // 2
    tile = 16
    extra = [f.shape[0] * f.shape[1] // cols for f in folded]
    starts = [sum(sizes[:k]) for k in range(len(sizes))]
    lengths = [size + sum(extra) * (k == 0) for k, size in enumerate(sizes)]

    def kernel(hidden_ref, *refs):
        passed_refs, refs = refs[: len(passed)], refs[len(passed) :]
        folded_refs, refs = refs[: len(folded)], refs[len(folded) + len(earlier) :]
        normed_ref, sent_refs, copy_refs = refs[0], refs[1 : 1 + len(sizes)], refs[1 + len(sizes) :]
        other = pl.multiple_of((1 - lax.axis_index("fsdp")) * cols, cols)
        for source, target in zip(passed_refs, copy_refs):
            target[...] = source[...]
        for ref, rows in zip(folded_refs, extra):
            part = ref.shape[1]
            for k in range(cols // part):
                sent_refs[0][sizes[0] : sizes[0] + rows, k * part : (k + 1) * part] = ref[k * rows : (k + 1) * rows, :]
        for start, size, sent_ref in zip(starts, sizes, sent_refs):
            for k in range(0, size, tile):
                at = pl.ds(start + k, tile)
                normed_ref[at, :] = normalize(hidden_ref[at, :])
                sent_ref[k : k + tile, :] = normed_ref[at, pl.ds(other, cols)]

    return call(
        kernel,
        (hidden,) + passed + folded + earlier,
        [VMEM] * (1 + len(passed) + len(folded)) + [ANY] * len(earlier),
        [like((tokens, width), bf16)]
        + [like((length, cols), bf16) for length in lengths]
        + [like(p.shape, p.dtype) for p in passed],
        [VMEM] * (1 + len(sizes) + len(passed)),
        8,
    )


def unfolded(message, start, shape):
    def kernel(message_ref, out_ref):
        rows = message.shape[0] - start
        for k in range(shape[0] // rows):
            out_ref[k * rows : (k + 1) * rows, :] = message_ref[start:, k * shape[1] : (k + 1) * shape[1]]

    return call(kernel, (message,), [VMEM], like(shape, message.dtype), VMEM, 4)


def reference_logs(normed, stacks, *earlier):
    tokens, width = normed.shape
    entries = stacks[0][0].shape[1]
    marks = [m for _, m in stacks]
    stacks = tuple(a for a, _ in stacks)
    rows = stacks[0].shape[0] // len(marks[0])
    count = len(stacks)

    def kernel(normed_ref, *refs):
        out_ref, whole_ref = refs[count + len(earlier) :]
        fsdp, me, _, _ = positions()
        for number in range(count):
            for p, (mask, bit_fsdp) in enumerate(marks[number]):
                block = jnp.bitwise_xor(me, mask) * 2 + jnp.bitwise_xor(fsdp, bit_fsdp)
                to = pl.ds(pl.multiple_of(block * rows, rows), rows)
                whole_ref[to, :] = refs[number][p * rows : (p + 1) * rows, :]
        out_ref[...] = log_softmax(capped(dot(normed_ref[...], whole_ref[...])))

    return call(
        kernel,
        (normed,) + tuple(stacks) + earlier,
        [VMEM] * (1 + count) + [ANY] * len(earlier),
        (like((tokens, entries), f32), like((width, entries), bf16)),
        (VMEM, VMEM),
        10,
    )


def more_reference_logs(normed, whole, *earlier):
    def kernel(normed_ref, whole_ref, *refs):
        refs[-1][...] = log_softmax(capped(dot(normed_ref[...], whole_ref[...])))

    return call(
        kernel,
        (normed, whole) + earlier,
        [VMEM, VMEM] + [ANY] * len(earlier),
        like((normed.shape[0], whole.shape[1]), f32),
        VMEM,
        8,
    )


def starting_weights(outer_head, drift, *earlier):
    rows, entries = outer_head.shape

    def kernel(outer_ref, drift_ref, *refs):
        inner_ref, weights_ref = refs[-2:]
        inner = outer_ref[...] + drift_ref[0].astype(f32)
        inner_ref[...] = inner
        weights_ref[...] = inner.astype(bf16)

    return call(
        kernel,
        (outer_head, drift) + earlier,
        [VMEM, VMEM] + [ANY] * len(earlier),
        (like((rows, entries), f32), like((rows, entries), bf16)),
        (VMEM, VMEM),
        10,
    )


def pack_logits(out_ref, logits):
    half = logits.shape[1] // 2
    pack(out_ref, logits[:, :half], logits[:, half:])


def put_together(out_ref, refs, sizes):
    start = 0
    for ref, size in zip(refs, sizes):
        out_ref[start : start + size, :] = ref[0:size, :]
        start += size


def partner_logits(pieces, sizes, weights):
    tokens, cols = sum(sizes), pieces[0].shape[1]
    entries = weights.shape[1]

    def kernel(weights_ref, *refs):
        features_ref, out_ref = refs[-2:]
        put_together(features_ref, refs[:-2], sizes)
        pack_logits(out_ref, dot(features_ref[...], weights_ref[...]))

    return call(
        kernel,
        (weights,) + tuple(pieces),
        [VMEM] * (1 + len(pieces)),
        (like((tokens, cols), bf16), like((packed_rows(tokens), entries // 2), jnp.int32)),
        (VMEM, VMEM),
        10,
    )


def own_logits(normed, weights, *earlier):
    tokens = normed.shape[0]
    rows, entries = weights.shape

    def kernel(normed_ref, weights_ref, *refs):
        at = pl.ds(pl.multiple_of(lax.axis_index("fsdp") * rows, rows), rows)
        refs[-1][...] = dot(normed_ref[:, at], weights_ref[...])

    return call(
        kernel,
        (normed, weights) + earlier,
        [VMEM, VMEM] + [ANY] * len(earlier),
        like((tokens, entries), f32),
        VMEM,
        8,
    )


def gradients(own, received, refer_log, targets, valid, step, *earlier):
    tokens, entries = own.shape

    def kernel(own_ref, received_ref, refer_ref, targets_ref, valid_ref, *refs):
        raw = own_ref[...] + jnp.concatenate(unpack(received_ref), axis=1)
        policy = capped(raw)
        policy_log = log_softmax(policy)
        policy_prob = jnp.exp(policy_log)
        diverge = policy_log - refer_ref[...]
        kl_value = jnp.sum(policy_prob * diverge, axis=-1, keepdims=True)
        here = lax.broadcasted_iota(jnp.int32, policy.shape, 1)
        onehot = jnp.where(column(targets_ref, step) == here, 1.0, 0.0)
        upstream = column(valid_ref, step).astype(f32) * (
            policy_prob - onehot + kl_weight * policy_prob * (diverge - kl_value)
        )
        ratio = policy / soft_cap
        refs[-1][...] = (upstream * (1.0 - ratio * ratio) * (4.0 / math.sqrt(D))).astype(bf16)

    return call(
        kernel,
        (own, received, refer_log, targets, valid) + earlier,
        [VMEM] * 5 + [ANY] * len(earlier),
        like((tokens, entries), bf16),
        VMEM,
        8,
    )


def own_update(inner, normed, grads, *earlier):
    rows, entries = inner.shape
    tile = rows // 4

    def kernel(inner_ref, normed_ref, grads_ref, *refs):
        for k in range(4):
            at = pl.ds(k * tile, tile)
            columns = pl.ds(pl.multiple_of(lax.axis_index("fsdp") * rows + k * tile, tile), tile)
            refs[-1][at, :] = inner_ref[at, :] - inner_rate * dot_rows(normed_ref[:, columns], grads_ref[...])

    return call(
        kernel,
        (inner, normed, grads) + earlier,
        [VMEM] * 3 + [ANY] * len(earlier),
        like((rows, entries), f32),
        VMEM,
        10,
    )


def update(inner, features, grads, outer_head, plan, step, replicas, following=(), earlier=()):
    rows, entries = inner.shape
    tokens = features.shape[0]
    part = entries // FRAGS
    half = rows // 2
    tile = rows // 4
    pieces = len(following)

    def kernel(plan_ref, inner_ref, features_ref, grads_ref, outer_ref, *refs):
        following_refs, refs = refs[:pieces], refs[pieces + len(earlier) :]
        new_ref, sent_ref, kept_ref = refs[:3]
        for k in range(4):
            at = pl.ds(k * tile, tile)
            new = inner_ref[at, :] - inner_rate * dot_rows(features_ref[:, at], grads_ref[...])
            new_ref[at, :] = new
            if pieces:
                refs[4][at, :] = new.astype(bf16)
        if pieces:
            next_ref, weights_ref, partial_ref = refs[3:]
            put_together(next_ref, following_refs, [f.shape[0] for f in following])
            pack_logits(partial_ref, dot(next_ref[...], weights_ref[...]))
        columns = pl.ds(pl.multiple_of(plan_ref[step] * part, part), part)
        core = positions()[2]
        for place_ref, which in ((sent_ref, 1 - core), (kept_ref, core)):
            at = pl.ds(pl.multiple_of(which * half, half), half)
            place_ref[...] = (outer_ref[at, columns] - new_ref[at, columns]) * (1.0 / replicas)

    operands = (plan, inner, features, grads, outer_head) + tuple(following)
    out_shape = [like((rows, entries), f32), like((half, part), f32), like((half, part), f32)]
    if pieces:
        out_shape += [
            like((tokens, rows), bf16),
            like((rows, entries), bf16),
            like((packed_rows(tokens), entries // 2), jnp.int32),
        ]
    return call(
        kernel,
        operands + tuple(earlier),
        [SMEM] + [VMEM] * (len(operands) - 1) + [ANY] * len(earlier),
        out_shape,
        [VMEM] * len(out_shape),
        16,
    )


def pack_quarter(out_ref, quarter):
    half = quarter.shape[0] // 2
    pack(out_ref, quarter[:half], quarter[half:])


def unpack_quarter(ref, start=0, rows=None):
    return jnp.concatenate(unpack(ref, start, rows), axis=0)


def quarters(kept, received):
    rows, cols = kept.shape
    quarter = rows // MAJOR

    def kernel(kept_ref, received_ref, own_ref, *refs):
        major = positions()[3]

        def piece(mask):
            at = pl.ds(pl.multiple_of(jnp.bitwise_xor(major, mask) * quarter, quarter), quarter)
            return kept_ref[at, :] + received_ref[at, :]

        for mask, out_ref in zip(MASKS, refs):
            pack_quarter(out_ref, piece(mask))
        own_ref[...] = piece(0)

    small = like((packed_rows(quarter // 2), cols), jnp.int32)
    return call(
        kernel,
        (kept, received),
        [VMEM] * 2,
        [like((quarter, cols), f32)] + [small] * len(MASKS),
        [VMEM] * (1 + len(MASKS)),
        6,
    )


def quarter_sum(own, pieces, *earlier):
    def kernel(own_ref, *refs):
        total = own_ref[...]
        for ref in refs[: len(pieces)]:
            total = total + unpack_quarter(ref)
        pack_quarter(refs[-1], total)

    return call(
        kernel,
        (own,) + tuple(pieces) + earlier,
        [VMEM] * (1 + len(pieces)) + [ANY] * len(earlier),
        like(pieces[0].shape, jnp.int32),
        VMEM,
        4,
    )


def pair_sum(one, other, *earlier):
    def kernel(one_ref, other_ref, *refs):
        pack_quarter(refs[-1], unpack_quarter(one_ref) + unpack_quarter(other_ref))

    return call(
        kernel,
        (one, other) + earlier,
        [VMEM] * 2 + [ANY] * len(earlier),
        like(one.shape, jnp.int32),
        VMEM,
        4,
    )


def settled(outer_head, inner, means, plan):
    rows, entries = inner.shape
    part = entries // FRAGS
    tile = rows // (CORES * MAJOR)
    steps = CORES * MAJOR
    small = packed_rows(tile // 2)

    def kernel(plan_ref, outer_ref, inner_ref, own0, other0, own1, other1, new_outer_ref, new_inner_ref, *scratch):
        mean_ref, outer_held, inner_held, sems = scratch
        _, _, core, major = positions()
        copies = []
        for i in range(steps):
            start = pl.multiple_of(jnp.bitwise_xor(i % MAJOR, major) * small, small)
            at = pl.ds(i * tile, tile)

            @pl.when(i // MAJOR == core)
            def _():
                mean_ref[0] = unpack_quarter(own0, start, tile // 2)
                mean_ref[1] = unpack_quarter(own1, start, tile // 2)

            @pl.when(i // MAJOR != core)
            def _():
                mean_ref[0] = unpack_quarter(other0, start, tile // 2)
                mean_ref[1] = unpack_quarter(other1, start, tile // 2)

            for f in range(FRAGS):
                columns = pl.ds(f * part, part)
                mean = mean_ref[jnp.where(plan_ref[0] == f, 0, 1)]
                fresh = outer_ref[at, columns] - outer_rate * mean
                outer_held[at, columns] = fresh
                inner_held[at, columns] = mix_weight * inner_ref[at, columns] + (1.0 - mix_weight) * fresh
            for k, (held, out) in enumerate(((outer_held, new_outer_ref), (inner_held, new_inner_ref))):
                copies.append(pltpu.make_async_copy(held.at[at], out.at[at], sems.at[2 * i + k]))
                copies[-1].start()
        for copy in copies:
            copy.wait()

    return call(
        kernel,
        (plan, outer_head, inner) + tuple(means[0]) + tuple(means[1]),
        [SMEM] + [VMEM] * 6,
        [like((rows, entries), f32)] * 2,
        [HBM, HBM],
        14,
        [
            pltpu.VMEM((2, tile, part), f32),
            pltpu.VMEM((rows, entries), f32),
            pltpu.VMEM((rows, entries), f32),
            pltpu.SemaphoreType.DMA((2 * steps,)),
        ],
    )


def along(stack, *masks):
    array, marks = stack
    return (
        stacked([array] + [swap(array, "replica", m) for m in masks]),
        [(mark ^ m, bit) for m in (0,) + masks for mark, bit in marks],
    )


def across(stack, mask):
    array, marks = stack
    return swap(array, "replica", mask), [(mark ^ mask, bit) for mark, bit in marks]


def gathered_stacks(ref_own, ref_partner):
    along_z = [m * 2 * CORES for m in (1, 2, 3)]
    stacks = []
    for piece in ((ref_own, [(0, 0)]), (ref_partner, [(0, 1)])):
        first = along(piece, *along_z)
        second = across(first, CORES)
        stacks += [first, second, across(first, 1), across(second, 1)]
    return stacks


def quarters_along(own, order):
    got = {m: swap(own, "replica", m * 2 * CORES) for m in order}
    return [own] + [got[m] for m in range(1, MAJOR)]


def gathered_quarters(pieces):
    stack = stacked(pieces)
    return stack, swap(stack, "replica", 1)


def chip_quarters(sent, kept):
    own, *pieces = quarters(kept, swap(sent, "replica", 1))
    return own, [swap(p, "replica", m * 2 * CORES) for p, m in zip(pieces, MASKS)]


def shards_pair(hidden, targets, valid, plan, outer_head, drift, ref_head):
    replicas = lax.axis_size("replica")

    tokens = hidden.shape[1]
    sizes0 = (4 * tokens // 16, tokens - 4 * tokens // 16)
    sizes1 = (9 * tokens // 16, tokens - 9 * tokens // 16)

    normed0, *sent0 = normalized(hidden[0], sizes0, (), (ref_head,))
    features0 = [swap(s, "fsdp", 1) for s in sent0]
    normed1, sent1a, sent1b, ref_own = normalized(hidden[1], sizes1, (ref_head,), (), tuple(sent0))
    features1a = swap(sent1a, "fsdp", 1)
    stacks = gathered_stacks(ref_own, unfolded(features0[0], sizes0[0], ref_head.shape))

    inner, weights = starting_weights(outer_head, drift, normed1)
    features0, partial = partner_logits(features0, sizes0, weights)
    received = swap(partial, "fsdp", 1)
    own = own_logits(normed0, weights, partial)
    features1b = swap(after(sent1b, partial), "fsdp", 1)
    refer_log, whole = reference_logs(normed0, stacks, features1a)
    grads = gradients(own, received, refer_log, targets, valid, 0, features1a)
    partner_grads = swap(grads, "fsdp", 1)
    halfway = own_update(inner, normed0, grads, features1b)
    refer_log = more_reference_logs(normed1, whole, halfway)
    inner, sent, kept, features1, weights, partial = update(
        halfway, features0, partner_grads, outer_head, plan, 0, replicas, (features1a, features1b), (refer_log,)
    )

    received = swap(partial, "fsdp", 1)
    own = own_logits(normed1, weights)
    quarter, pieces = chip_quarters(sent, kept)
    grads = gradients(own, received, refer_log, targets, valid, 1, pieces[0])
    partner_grads = swap(grads, "fsdp", 1)
    halfway = own_update(inner, normed1, grads)
    quarter = quarter_sum(quarter, pieces, halfway)
    first = pair_sum(quarter, swap(quarter, "replica", CORES))
    inner, sent, kept = update(
        halfway, features1, partner_grads, outer_head, plan, 1, replicas, (), (quarter,)
    )

    quarter, pieces = chip_quarters(sent, kept)
    quarter = quarter_sum(quarter, pieces)
    first = quarters_along(first, (3, 1, 2))
    second = pair_sum(quarter, swap(quarter, "replica", CORES), first[1], first[2])
    means = [gathered_quarters(m) for m in (first, quarters_along(second, (1, 2, 3)))]
    new_outer, new_inner = settled(outer_head, inner, means, plan)
    return (new_outer, new_inner[None])


def solution(mesh):
    in_specs = (
        P(None, ("replica", "fsdp"), None),
        P(None, ("replica", "fsdp")),
        P(None, ("replica", "fsdp")),
        P(),
        P("fsdp", None),
        P("replica", "fsdp", None),
        P(("replica", "fsdp"), None),
    )
    out_specs = (P("fsdp", None), P("replica", "fsdp", None))
    chips = mesh.shape["replica"] // CORES
    pairs = mesh.shape["fsdp"] == 2 and chips == 2 * MAJOR
    shards = shards_pair if pairs else shards_any
    return jax.shard_map(shards, mesh=mesh, in_specs=in_specs, out_specs=out_specs, check_vma=False)
```

```python
import math

import jax
import jax.numpy as jnp
from jax import lax
from jax.experimental import pallas as pl
from jax.experimental.pallas import tpu as pltpu
from jax.sharding import PartitionSpec as P

D = 2048
FRAGS = 2
STEPS = 2
CORES = 2
MAJOR = 4

soft_cap = 30.0
kl_weight = 0.5
inner_rate = 0.5
outer_rate = 0.7
mix_weight = 0.5
norm_eps = 1e-05

f32 = jnp.float32
bf16 = jnp.bfloat16
f16 = jnp.float16
logit_type = jnp.float32


def swap(value, axis, mask):
    size = lax.axis_size(axis)
    return lax.ppermute(value, axis, [(i, i ^ mask) for i in range(size)])


def rows_at(value, block, count):
    return lax.dynamic_slice_in_dim(value, block * count, count, 0)


def columns_at(value, block, count):
    return lax.dynamic_slice_in_dim(value, block * count, count, 1)


def place(pieces, spots):
    count = pieces[0].shape[0]
    whole = jnp.zeros((count * len(pieces),) + pieces[0].shape[1:], pieces[0].dtype)
    for piece, spot in zip(pieces, spots):
        whole = lax.dynamic_update_slice_in_dim(whole, piece, spot * count, 0)
    return whole


def in_pair(first, own, other):
    return jnp.where(
        first, jnp.concatenate([own, other], 0), jnp.concatenate([other, own], 0)
    )


def grid_of_replicas():
    chips = lax.axis_size("replica") // CORES
    minor = chips // MAJOR
    me = lax.axis_index("replica")
    return minor, me % CORES, me // (CORES * minor)


def gather_reference(rows):
    minor, core, major = grid_of_replicas()
    fsdp = lax.axis_size("fsdp")
    me = lax.axis_index("fsdp")
    masks = range(fsdp)
    block = place([rows] + [swap(rows, "fsdp", m) for m in masks[1:]], [me ^ m for m in masks])
    spots = lax.axis_index("replica")
    blocks = [(block, spots)]
    step = CORES * minor
    blocks = [(swap(b, "replica", m * step) if m else b, s ^ (m * step)) for b, s in blocks for m in range(MAJOR)]
    mask = CORES
    while mask < step:
        stacked = jnp.concatenate([b for b, _ in blocks], 0)
        other = swap(stacked, "replica", mask)
        blocks = blocks + [
            (p, s ^ mask) for p, (_, s) in zip(jnp.split(other, len(blocks), 0), blocks)
        ]
        mask *= 2
    stacked = jnp.concatenate([b for b, _ in blocks], 0)
    other = swap(stacked, "replica", 1)
    blocks = blocks + [(p, s ^ 1) for p, (_, s) in zip(jnp.split(other, len(blocks), 0), blocks)]
    return place([b for b, _ in blocks], [s for _, s in blocks])


def mean_over_replicas(delta):
    minor, core, major = grid_of_replicas()
    replicas = lax.axis_size("replica")
    delta = delta * (1.0 / replicas)
    half = delta.shape[0] // CORES
    part = rows_at(delta, core, half) + swap(rows_at(delta, 1 - core, half), "replica", 1)
    step = CORES * minor
    quarter = half // MAJOR
    sent = part.astype(f16)
    own = rows_at(part, major, quarter)
    for m in (2, 1, 3):
        own = own + swap(rows_at(sent, major ^ m, quarter), "replica", m * step).astype(f32)
    mask = CORES
    while mask < step:
        own = own + swap(own, "replica", mask)
        mask *= 2
    own = own.astype(f16)
    pieces = [own] + [swap(own, "replica", m * step) for m in (2, 1, 3)]
    gathered = place(pieces, [major ^ m for m in (0, 2, 1, 3)])
    return in_pair(core == 0, gathered, swap(gathered, "replica", 1)).astype(f32)


def normalize(hidden_rows):
    values = hidden_rows.astype(f32)
    factor = lax.rsqrt(jnp.mean(values * values, axis=-1, keepdims=True) + norm_eps)
    return (values * factor).astype(bf16)


def capped(raw):
    return soft_cap * jnp.tanh(raw * (4.0 / math.sqrt(D)) / soft_cap)


def log_softmax(logits):
    return logits - jnp.log(jnp.sum(jnp.exp(logits), axis=-1, keepdims=True))


def logit_grads(policy, refer_log, target_ids, valid_rows):
    policy_log = log_softmax(policy)
    policy_prob = jnp.exp(policy_log)
    diverge = policy_log - refer_log
    kl_value = jnp.sum(policy_prob * diverge, axis=-1, keepdims=True)
    entries = jnp.arange(policy.shape[-1], dtype=jnp.int32)
    onehot = (target_ids[:, None] == entries[None, :]).astype(f32)
    upstream = valid_rows[:, None].astype(f32) * (
        policy_prob - onehot + kl_weight * policy_prob * (diverge - kl_value)
    )
    ratio = policy / soft_cap
    return (upstream * (1.0 - ratio * ratio) * (4.0 / math.sqrt(D))).astype(bf16)


def dot(a, b):
    return jnp.dot(a, b, preferred_element_type=f32)


def dot_rows(a, b):
    return lax.dot_general(a, b, (((0,), (0,)), ((), ())), preferred_element_type=f32)


def shards_any(hidden, targets, valid, plan, outer_head, drift, ref_head):
    rows_local, width = outer_head.shape
    part = width // FRAGS
    fsdp = lax.axis_size("fsdp")
    me = lax.axis_index("fsdp")
    masks = range(fsdp)

    normed = [normalize(hidden[s]) for s in range(STEPS)]
    features = [
        [columns_at(n, me, rows_local)]
        + [swap(columns_at(n, me ^ m, rows_local), "fsdp", m) for m in masks[1:]]
        for n in normed
    ]
    reference = gather_reference(ref_head)
    refer_log = [log_softmax(capped(dot(n, reference))) for n in normed]

    inner = outer_head + drift[0].astype(f32)
    means = []
    for s in range(STEPS):
        weights = inner.astype(bf16)
        raw = dot(features[s][0], weights)
        for m in masks[1:]:
            raw = raw + swap(dot(features[s][m], weights).astype(logit_type), "fsdp", m).astype(f32)
        grads = logit_grads(capped(raw), refer_log[s], targets[s], valid[s])
        total = dot_rows(features[s][0], grads)
        for m in masks[1:]:
            total = total + dot_rows(features[s][m], swap(grads, "fsdp", m))
        inner = inner - inner_rate * total
        start = plan[s] * part
        delta = lax.dynamic_slice_in_dim(outer_head - inner, start, part, 1)
        means.append(mean_over_replicas(delta))
    first, second = means
    mean = jnp.where(
        plan[0] == 0,
        jnp.concatenate([first, second], 1),
        jnp.concatenate([second, first], 1),
    )
    new_outer = outer_head - outer_rate * mean
    new_inner = mix_weight * inner + (1.0 - mix_weight) * new_outer
    return (new_outer, new_inner[None])


MASKS = (3, 2, 1)
COST = {
    "after": 100000000,
    "stacked": 5000000000,
    "more_reference_logs": 100000000,
    "own_logits": 100000000,
    "own_update": 5000000000,
    "update": 1000000000,
}
VMEM = pl.BlockSpec(memory_space=pltpu.VMEM)
SMEM = pl.BlockSpec(memory_space=pltpu.SMEM)
ANY = pl.BlockSpec(memory_space=pl.ANY)
HBM = pl.BlockSpec(memory_space=pltpu.HBM)


def call(kernel, operands, in_specs, out_shape, out_specs, room, scratch=(), **more):
    return pl.pallas_call(
        kernel,
        out_shape=out_shape,
        in_specs=in_specs,
        out_specs=out_specs,
        scratch_shapes=scratch,
        compiler_params=pltpu.CompilerParams(vmem_limit_bytes=room * 1024 * 1024),
        cost_estimate=pl.CostEstimate(flops=COST.get(kernel.__qualname__.split(".")[0], 1000), bytes_accessed=1000, transcendentals=0),
        **more,
    )(*operands)


def like(shape, kind):
    return jax.ShapeDtypeStruct(shape, kind)


def after(value, *earlier):
    def kernel(*refs):
        pass

    return call(
        kernel,
        (value,) + earlier,
        [ANY] * (1 + len(earlier)),
        like(value.shape, value.dtype),
        ANY,
        2,
        input_output_aliases={0: 0},
    )


def stacked(pieces):
    rows, cols = pieces[0].shape
    count = len(pieces)

    def kernel(*refs):
        out_ref, sems = refs[count:]
        copies = [
            pltpu.make_async_copy(refs[k], out_ref.at[pl.ds(k * rows, rows)], sems.at[k])
            for k in range(count)
        ]
        for copy in copies:
            copy.start()
        for copy in copies:
            copy.wait()

    return call(
        kernel,
        pieces,
        [ANY] * count,
        like((count * rows, cols), pieces[0].dtype),
        ANY,
        2,
        [pltpu.SemaphoreType.DMA((count,))],
    )


def positions():
    replica = lax.axis_index("replica")
    return lax.axis_index("fsdp"), replica, lax.rem(replica, CORES), replica // (2 * CORES)


LEVEL = math.log(2.0) / 64.0


def scale_of(code):
    return jnp.exp(code.astype(f32) * LEVEL)


def packed_rows(rows):
    return rows + 8


def pack(out_ref, first, second):
    rows = first.shape[0]
    codes, values = [], []
    for x in (first, second):
        top = jnp.maximum(jnp.max(jnp.abs(x), axis=0, keepdims=True), 1e-30)
        code = jnp.ceil(jnp.log(top) * (1.0 / LEVEL)).astype(jnp.int32) + 1
        codes.append(code)
        values.append(jnp.round(x * (32767.0 / scale_of(code))).astype(jnp.int32))
    out_ref[0:rows, :] = (values[0] << 16) | (values[1] & 0xFFFF)
    row = lax.broadcasted_iota(jnp.int32, (8, first.shape[1]), 0)
    out_ref[rows : rows + 8, :] = jnp.where(row == 0, codes[0], codes[1])


def unpack(ref, start=0, rows=None):
    rows = ref.shape[0] - 8 if rows is None else rows
    both = ref[pl.ds(start, rows), :]
    codes = ref[pl.ds(start + rows, 8), :]
    unit = scale_of(codes) * (1.0 / 32767.0)
    return (both >> 16).astype(f32) * unit[0:1, :], ((both << 16) >> 16).astype(f32) * unit[1:2, :]


def column(ref, step):
    row = ref[step : step + 1, :]
    return jnp.broadcast_to(row, (128, row.shape[1])).T[:, 0:1]


def normalized(hidden, sizes, passed=(), folded=(), earlier=()):
    tokens, width = hidden.shape
    cols = width // 2
    tile = 16
    extra = [f.shape[0] * f.shape[1] // cols for f in folded]
    starts = [sum(sizes[:k]) for k in range(len(sizes))]
    lengths = [size + sum(extra) * (k == 0) for k, size in enumerate(sizes)]

    def kernel(hidden_ref, *refs):
        passed_refs, refs = refs[: len(passed)], refs[len(passed) :]
        folded_refs, refs = refs[: len(folded)], refs[len(folded) + len(earlier) :]
        normed_ref, sent_refs, copy_refs = refs[0], refs[1 : 1 + len(sizes)], refs[1 + len(sizes) :]
        other = pl.multiple_of((1 - lax.axis_index("fsdp")) * cols, cols)
        for source, target in zip(passed_refs, copy_refs):
            target[...] = source[...]
        for ref, rows in zip(folded_refs, extra):
            part = ref.shape[1]
            for k in range(cols // part):
                sent_refs[0][sizes[0] : sizes[0] + rows, k * part : (k + 1) * part] = ref[k * rows : (k + 1) * rows, :]
        for start, size, sent_ref in zip(starts, sizes, sent_refs):
            for k in range(0, size, tile):
                at = pl.ds(start + k, tile)
                normed_ref[at, :] = normalize(hidden_ref[at, :])
                sent_ref[k : k + tile, :] = normed_ref[at, pl.ds(other, cols)]

    return call(
        kernel,
        (hidden,) + passed + folded + earlier,
        [VMEM] * (1 + len(passed) + len(folded)) + [ANY] * len(earlier),
        [like((tokens, width), bf16)]
        + [like((length, cols), bf16) for length in lengths]
        + [like(p.shape, p.dtype) for p in passed],
        [VMEM] * (1 + len(sizes) + len(passed)),
        8,
    )


def unfolded(message, start, shape):
    def kernel(message_ref, out_ref):
        rows = message.shape[0] - start
        for k in range(shape[0] // rows):
            out_ref[k * rows : (k + 1) * rows, :] = message_ref[start:, k * shape[1] : (k + 1) * shape[1]]

    return call(kernel, (message,), [VMEM], like(shape, message.dtype), VMEM, 4)


def reference_logs(normed, stacks, *earlier):
    tokens, width = normed.shape
    entries = stacks[0][0].shape[1]
    marks = [m for _, m in stacks]
    stacks = tuple(a for a, _ in stacks)
    rows = stacks[0].shape[0] // len(marks[0])
    count = len(stacks)

    def kernel(normed_ref, *refs):
        out_ref, whole_ref = refs[count + len(earlier) :]
        fsdp, me, _, _ = positions()
        for number in range(count):
            for p, (mask, bit_fsdp) in enumerate(marks[number]):
                block = jnp.bitwise_xor(me, mask) * 2 + jnp.bitwise_xor(fsdp, bit_fsdp)
                to = pl.ds(pl.multiple_of(block * rows, rows), rows)
                whole_ref[to, :] = refs[number][p * rows : (p + 1) * rows, :]
        out_ref[...] = log_softmax(capped(dot(normed_ref[...], whole_ref[...])))

    return call(
        kernel,
        (normed,) + tuple(stacks) + earlier,
        [VMEM] * (1 + count) + [ANY] * len(earlier),
        (like((tokens, entries), f32), like((width, entries), bf16)),
        (VMEM, VMEM),
        10,
    )


def more_reference_logs(normed, whole, *earlier):
    def kernel(normed_ref, whole_ref, *refs):
        refs[-1][...] = log_softmax(capped(dot(normed_ref[...], whole_ref[...])))

    return call(
        kernel,
        (normed, whole) + earlier,
        [VMEM, VMEM] + [ANY] * len(earlier),
        like((normed.shape[0], whole.shape[1]), f32),
        VMEM,
        8,
    )


def starting_weights(outer_head, drift, *earlier):
    rows, entries = outer_head.shape

    def kernel(outer_ref, drift_ref, *refs):
        inner_ref, weights_ref = refs[-2:]
        inner = outer_ref[...] + drift_ref[0].astype(f32)
        inner_ref[...] = inner
        weights_ref[...] = inner.astype(bf16)

    return call(
        kernel,
        (outer_head, drift) + earlier,
        [VMEM, VMEM] + [ANY] * len(earlier),
        (like((rows, entries), f32), like((rows, entries), bf16)),
        (VMEM, VMEM),
        10,
    )


def pack_logits(out_ref, logits):
    half = logits.shape[1] // 2
    pack(out_ref, logits[:, :half], logits[:, half:])


def put_together(out_ref, refs, sizes):
    start = 0
    for ref, size in zip(refs, sizes):
        out_ref[start : start + size, :] = ref[0:size, :]
        start += size


def partner_logits(pieces, sizes, weights):
    tokens, cols = sum(sizes), pieces[0].shape[1]
    entries = weights.shape[1]

    def kernel(weights_ref, *refs):
        features_ref, out_ref = refs[-2:]
        put_together(features_ref, refs[:-2], sizes)
        pack_logits(out_ref, dot(features_ref[...], weights_ref[...]))

    return call(
        kernel,
        (weights,) + tuple(pieces),
        [VMEM] * (1 + len(pieces)),
        (like((tokens, cols), bf16), like((packed_rows(tokens), entries // 2), jnp.int32)),
        (VMEM, VMEM),
        10,
    )


def own_logits(normed, weights, *earlier):
    tokens = normed.shape[0]
    rows, entries = weights.shape

    def kernel(normed_ref, weights_ref, *refs):
        at = pl.ds(pl.multiple_of(lax.axis_index("fsdp") * rows, rows), rows)
        refs[-1][...] = dot(normed_ref[:, at], weights_ref[...])

    return call(
        kernel,
        (normed, weights) + earlier,
        [VMEM, VMEM] + [ANY] * len(earlier),
        like((tokens, entries), f32),
        VMEM,
        8,
    )


def gradients(own, received, refer_log, targets, valid, step, *earlier):
    tokens, entries = own.shape

    def kernel(own_ref, received_ref, refer_ref, targets_ref, valid_ref, *refs):
        raw = own_ref[...] + jnp.concatenate(unpack(received_ref), axis=1)
        policy = capped(raw)
        policy_log = log_softmax(policy)
        policy_prob = jnp.exp(policy_log)
        diverge = policy_log - refer_ref[...]
        kl_value = jnp.sum(policy_prob * diverge, axis=-1, keepdims=True)
        here = lax.broadcasted_iota(jnp.int32, policy.shape, 1)
        onehot = jnp.where(column(targets_ref, step) == here, 1.0, 0.0)
        upstream = column(valid_ref, step).astype(f32) * (
            policy_prob - onehot + kl_weight * policy_prob * (diverge - kl_value)
        )
        ratio = policy / soft_cap
        refs[-1][...] = (upstream * (1.0 - ratio * ratio) * (4.0 / math.sqrt(D))).astype(bf16)

    return call(
        kernel,
        (own, received, refer_log, targets, valid) + earlier,
        [VMEM] * 5 + [ANY] * len(earlier),
        like((tokens, entries), bf16),
        VMEM,
        8,
    )


def own_update(inner, normed, grads, *earlier):
    rows, entries = inner.shape
    tile = rows // 4

    def kernel(inner_ref, normed_ref, grads_ref, *refs):
        for k in range(4):
            at = pl.ds(k * tile, tile)
            columns = pl.ds(pl.multiple_of(lax.axis_index("fsdp") * rows + k * tile, tile), tile)
            refs[-1][at, :] = inner_ref[at, :] - inner_rate * dot_rows(normed_ref[:, columns], grads_ref[...])

    return call(
        kernel,
        (inner, normed, grads) + earlier,
        [VMEM] * 3 + [ANY] * len(earlier),
        like((rows, entries), f32),
        VMEM,
        10,
    )


def update(inner, features, grads, outer_head, plan, step, replicas, following=(), earlier=()):
    rows, entries = inner.shape
    tokens = features.shape[0]
    part = entries // FRAGS
    half = rows // 2
    tile = rows // 4
    pieces = len(following)

    def kernel(plan_ref, inner_ref, features_ref, grads_ref, outer_ref, *refs):
        following_refs, refs = refs[:pieces], refs[pieces + len(earlier) :]
        new_ref, sent_ref, kept_ref = refs[:3]
        for k in range(4):
            at = pl.ds(k * tile, tile)
            new = inner_ref[at, :] - inner_rate * dot_rows(features_ref[:, at], grads_ref[...])
            new_ref[at, :] = new
            if pieces:
                refs[4][at, :] = new.astype(bf16)
        if pieces:
            next_ref, weights_ref, partial_ref = refs[3:]
            put_together(next_ref, following_refs, [f.shape[0] for f in following])
            pack_logits(partial_ref, dot(next_ref[...], weights_ref[...]))
        columns = pl.ds(pl.multiple_of(plan_ref[step] * part, part), part)
        core = positions()[2]
        for place_ref, which in ((sent_ref, 1 - core), (kept_ref, core)):
            at = pl.ds(pl.multiple_of(which * half, half), half)
            place_ref[...] = (outer_ref[at, columns] - new_ref[at, columns]) * (1.0 / replicas)

    operands = (plan, inner, features, grads, outer_head) + tuple(following)
    out_shape = [like((rows, entries), f32), like((half, part), f32), like((half, part), f32)]
    if pieces:
        out_shape += [
            like((tokens, rows), bf16),
            like((rows, entries), bf16),
            like((packed_rows(tokens), entries // 2), jnp.int32),
        ]
    return call(
        kernel,
        operands + tuple(earlier),
        [SMEM] + [VMEM] * (len(operands) - 1) + [ANY] * len(earlier),
        out_shape,
        [VMEM] * len(out_shape),
        16,
    )


def pack_quarter(out_ref, quarter):
    half = quarter.shape[0] // 2
    pack(out_ref, quarter[:half], quarter[half:])


def unpack_quarter(ref, start=0, rows=None):
    return jnp.concatenate(unpack(ref, start, rows), axis=0)


def quarters(kept, received):
    rows, cols = kept.shape
    quarter = rows // MAJOR

    def kernel(kept_ref, received_ref, own_ref, *refs):
        major = positions()[3]

        def piece(mask):
            at = pl.ds(pl.multiple_of(jnp.bitwise_xor(major, mask) * quarter, quarter), quarter)
            return kept_ref[at, :] + received_ref[at, :]

        for mask, out_ref in zip(MASKS, refs):
            pack_quarter(out_ref, piece(mask))
        own_ref[...] = piece(0)

    small = like((packed_rows(quarter // 2), cols), jnp.int32)
    return call(
        kernel,
        (kept, received),
        [VMEM] * 2,
        [like((quarter, cols), f32)] + [small] * len(MASKS),
        [VMEM] * (1 + len(MASKS)),
        6,
    )


def quarter_sum(own, pieces, *earlier):
    def kernel(own_ref, *refs):
        total = own_ref[...]
        for ref in refs[: len(pieces)]:
            total = total + unpack_quarter(ref)
        pack_quarter(refs[-1], total)

    return call(
        kernel,
        (own,) + tuple(pieces) + earlier,
        [VMEM] * (1 + len(pieces)) + [ANY] * len(earlier),
        like(pieces[0].shape, jnp.int32),
        VMEM,
        4,
    )


def pair_sum(one, other, *earlier):
    def kernel(one_ref, other_ref, *refs):
        pack_quarter(refs[-1], unpack_quarter(one_ref) + unpack_quarter(other_ref))

    return call(
        kernel,
        (one, other) + earlier,
        [VMEM] * 2 + [ANY] * len(earlier),
        like(one.shape, jnp.int32),
        VMEM,
        4,
    )


def settled(outer_head, inner, means, plan):
    rows, entries = inner.shape
    part = entries // FRAGS
    tile = rows // (CORES * MAJOR)
    steps = CORES * MAJOR
    small = packed_rows(tile // 2)

    def kernel(plan_ref, outer_ref, inner_ref, own0, other0, own1, other1, new_outer_ref, new_inner_ref, *scratch):
        mean_ref, outer_held, inner_held, sems = scratch
        _, _, core, major = positions()
        copies = []
        for i in range(steps):
            start = pl.multiple_of(jnp.bitwise_xor(i % MAJOR, major) * small, small)
            at = pl.ds(i * tile, tile)

            @pl.when(i // MAJOR == core)
            def _():
                mean_ref[0] = unpack_quarter(own0, start, tile // 2)
                mean_ref[1] = unpack_quarter(own1, start, tile // 2)

            @pl.when(i // MAJOR != core)
            def _():
                mean_ref[0] = unpack_quarter(other0, start, tile // 2)
                mean_ref[1] = unpack_quarter(other1, start, tile // 2)

            for f in range(FRAGS):
                columns = pl.ds(f * part, part)
                mean = mean_ref[jnp.where(plan_ref[0] == f, 0, 1)]
                fresh = outer_ref[at, columns] - outer_rate * mean
                outer_held[at, columns] = fresh
                inner_held[at, columns] = mix_weight * inner_ref[at, columns] + (1.0 - mix_weight) * fresh
            for k, (held, out) in enumerate(((outer_held, new_outer_ref), (inner_held, new_inner_ref))):
                copies.append(pltpu.make_async_copy(held.at[at], out.at[at], sems.at[2 * i + k]))
                copies[-1].start()
        for copy in copies:
            copy.wait()

    return call(
        kernel,
        (plan, outer_head, inner) + tuple(means[0]) + tuple(means[1]),
        [SMEM] + [VMEM] * 6,
        [like((rows, entries), f32)] * 2,
        [HBM, HBM],
        14,
        [
            pltpu.VMEM((2, tile, part), f32),
            pltpu.VMEM((rows, entries), f32),
            pltpu.VMEM((rows, entries), f32),
            pltpu.SemaphoreType.DMA((2 * steps,)),
        ],
    )


def along(stack, *masks):
    array, marks = stack
    return (
        stacked([array] + [swap(array, "replica", m) for m in masks]),
        [(mark ^ m, bit) for m in (0,) + masks for mark, bit in marks],
    )


def across(stack, mask):
    array, marks = stack
    return swap(array, "replica", mask), [(mark ^ mask, bit) for mark, bit in marks]


def gathered_stacks(ref_own, ref_partner):
    along_z = [m * 2 * CORES for m in (1, 2, 3)]
    stacks = []
    for piece in ((ref_own, [(0, 0)]), (ref_partner, [(0, 1)])):
        first = along(piece, *along_z)
        second = across(first, CORES)
        stacks += [first, second, across(first, 1), across(second, 1)]
    return stacks


def quarters_along(own, order):
    got = {m: swap(own, "replica", m * 2 * CORES) for m in order}
    return [own] + [got[m] for m in range(1, MAJOR)]


def gathered_quarters(pieces):
    stack = stacked(pieces)
    return stack, swap(stack, "replica", 1)


def chip_quarters(sent, kept):
    own, *pieces = quarters(kept, swap(sent, "replica", 1))
    return own, [swap(p, "replica", m * 2 * CORES) for p, m in zip(pieces, MASKS)]


def shards_pair(hidden, targets, valid, plan, outer_head, drift, ref_head):
    replicas = lax.axis_size("replica")

    tokens = hidden.shape[1]
    sizes0 = (4 * tokens // 16, tokens - 4 * tokens // 16)
    sizes1 = (9 * tokens // 16, tokens - 9 * tokens // 16)

    normed0, *sent0 = normalized(hidden[0], sizes0, (), (ref_head,))
    features0 = [swap(s, "fsdp", 1) for s in sent0]
    normed1, sent1a, sent1b, ref_own = normalized(hidden[1], sizes1, (ref_head,), (), tuple(sent0))
    features1a = swap(sent1a, "fsdp", 1)
    stacks = gathered_stacks(ref_own, unfolded(features0[0], sizes0[0], ref_head.shape))

    inner, weights = starting_weights(outer_head, drift, normed1)
    features0, partial = partner_logits(features0, sizes0, weights)
    received = swap(partial, "fsdp", 1)
    own = own_logits(normed0, weights, partial)
    features1b = swap(after(sent1b, partial), "fsdp", 1)
    refer_log, whole = reference_logs(normed0, stacks, features1a)
    grads = gradients(own, received, refer_log, targets, valid, 0, features1a)
    partner_grads = swap(grads, "fsdp", 1)
    halfway = own_update(inner, normed0, grads, features1b)
    refer_log = more_reference_logs(normed1, whole, halfway)
    inner, sent, kept, features1, weights, partial = update(
        halfway, features0, partner_grads, outer_head, plan, 0, replicas, (features1a, features1b), ()
    )

    received = swap(partial, "fsdp", 1)
    own = own_logits(normed1, weights)
    quarter, pieces = chip_quarters(sent, kept)
    grads = gradients(own, received, refer_log, targets, valid, 1, pieces[0])
    partner_grads = swap(grads, "fsdp", 1)
    halfway = own_update(inner, normed1, grads)
    quarter = quarter_sum(quarter, pieces, halfway)
    first = pair_sum(quarter, swap(quarter, "replica", CORES))
    inner, sent, kept = update(
        halfway, features1, partner_grads, outer_head, plan, 1, replicas, (), (quarter,)
    )

    quarter, pieces = chip_quarters(sent, kept)
    quarter = quarter_sum(quarter, pieces)
    first = quarters_along(first, (3, 1, 2))
    second = pair_sum(quarter, swap(quarter, "replica", CORES), first[1], first[2])
    means = [gathered_quarters(m) for m in (first, quarters_along(second, (1, 2, 3)))]
    new_outer, new_inner = settled(outer_head, inner, means, plan)
    return (new_outer, new_inner[None])


def solution(mesh):
    in_specs = (
        P(None, ("replica", "fsdp"), None),
        P(None, ("replica", "fsdp")),
        P(None, ("replica", "fsdp")),
        P(),
        P("fsdp", None),
        P("replica", "fsdp", None),
        P(("replica", "fsdp"), None),
    )
    out_specs = (P("fsdp", None), P("replica", "fsdp", None))
    chips = mesh.shape["replica"] // CORES
    pairs = mesh.shape["fsdp"] == 2 and chips == 2 * MAJOR
    shards = shards_pair if pairs else shards_any
    return jax.shard_map(shards, mesh=mesh, in_specs=in_specs, out_specs=out_specs, check_vma=False)
```

```python
import math

import jax
import jax.numpy as jnp
from jax import lax
from jax.experimental import pallas as pl
from jax.experimental.pallas import tpu as pltpu
from jax.sharding import PartitionSpec as P

D = 2048
FRAGS = 2
STEPS = 2
CORES = 2
MAJOR = 4

soft_cap = 30.0
kl_weight = 0.5
inner_rate = 0.5
outer_rate = 0.7
mix_weight = 0.5
norm_eps = 1e-05

f32 = jnp.float32
bf16 = jnp.bfloat16
f16 = jnp.float16
logit_type = jnp.float32


def swap(value, axis, mask):
    size = lax.axis_size(axis)
    return lax.ppermute(value, axis, [(i, i ^ mask) for i in range(size)])


def rows_at(value, block, count):
    return lax.dynamic_slice_in_dim(value, block * count, count, 0)


def columns_at(value, block, count):
    return lax.dynamic_slice_in_dim(value, block * count, count, 1)


def place(pieces, spots):
    count = pieces[0].shape[0]
    whole = jnp.zeros((count * len(pieces),) + pieces[0].shape[1:], pieces[0].dtype)
    for piece, spot in zip(pieces, spots):
        whole = lax.dynamic_update_slice_in_dim(whole, piece, spot * count, 0)
    return whole


def in_pair(first, own, other):
    return jnp.where(
        first, jnp.concatenate([own, other], 0), jnp.concatenate([other, own], 0)
    )


def grid_of_replicas():
    chips = lax.axis_size("replica") // CORES
    minor = chips // MAJOR
    me = lax.axis_index("replica")
    return minor, me % CORES, me // (CORES * minor)


def gather_reference(rows):
    minor, core, major = grid_of_replicas()
    fsdp = lax.axis_size("fsdp")
    me = lax.axis_index("fsdp")
    masks = range(fsdp)
    block = place([rows] + [swap(rows, "fsdp", m) for m in masks[1:]], [me ^ m for m in masks])
    spots = lax.axis_index("replica")
    blocks = [(block, spots)]
    step = CORES * minor
    blocks = [(swap(b, "replica", m * step) if m else b, s ^ (m * step)) for b, s in blocks for m in range(MAJOR)]
    mask = CORES
    while mask < step:
        stacked = jnp.concatenate([b for b, _ in blocks], 0)
        other = swap(stacked, "replica", mask)
        blocks = blocks + [
            (p, s ^ mask) for p, (_, s) in zip(jnp.split(other, len(blocks), 0), blocks)
        ]
        mask *= 2
    stacked = jnp.concatenate([b for b, _ in blocks], 0)
    other = swap(stacked, "replica", 1)
    blocks = blocks + [(p, s ^ 1) for p, (_, s) in zip(jnp.split(other, len(blocks), 0), blocks)]
    return place([b for b, _ in blocks], [s for _, s in blocks])


def mean_over_replicas(delta):
    minor, core, major = grid_of_replicas()
    replicas = lax.axis_size("replica")
    delta = delta * (1.0 / replicas)
    half = delta.shape[0] // CORES
    part = rows_at(delta, core, half) + swap(rows_at(delta, 1 - core, half), "replica", 1)
    step = CORES * minor
    quarter = half // MAJOR
    sent = part.astype(f16)
    own = rows_at(part, major, quarter)
    for m in (2, 1, 3):
        own = own + swap(rows_at(sent, major ^ m, quarter), "replica", m * step).astype(f32)
    mask = CORES
    while mask < step:
        own = own + swap(own, "replica", mask)
        mask *= 2
    own = own.astype(f16)
    pieces = [own] + [swap(own, "replica", m * step) for m in (2, 1, 3)]
    gathered = place(pieces, [major ^ m for m in (0, 2, 1, 3)])
    return in_pair(core == 0, gathered, swap(gathered, "replica", 1)).astype(f32)


def normalize(hidden_rows):
    values = hidden_rows.astype(f32)
    factor = lax.rsqrt(jnp.mean(values * values, axis=-1, keepdims=True) + norm_eps)
    return (values * factor).astype(bf16)


def capped(raw):
    return soft_cap * jnp.tanh(raw * (4.0 / math.sqrt(D)) / soft_cap)


def log_softmax(logits):
    return logits - jnp.log(jnp.sum(jnp.exp(logits), axis=-1, keepdims=True))


def logit_grads(policy, refer_log, target_ids, valid_rows):
    policy_log = log_softmax(policy)
    policy_prob = jnp.exp(policy_log)
    diverge = policy_log - refer_log
    kl_value = jnp.sum(policy_prob * diverge, axis=-1, keepdims=True)
    entries = jnp.arange(policy.shape[-1], dtype=jnp.int32)
    onehot = (target_ids[:, None] == entries[None, :]).astype(f32)
    upstream = valid_rows[:, None].astype(f32) * (
        policy_prob - onehot + kl_weight * policy_prob * (diverge - kl_value)
    )
    ratio = policy / soft_cap
    return (upstream * (1.0 - ratio * ratio) * (4.0 / math.sqrt(D))).astype(bf16)


def dot(a, b):
    return jnp.dot(a, b, preferred_element_type=f32)


def dot_rows(a, b):
    return lax.dot_general(a, b, (((0,), (0,)), ((), ())), preferred_element_type=f32)


def shards_any(hidden, targets, valid, plan, outer_head, drift, ref_head):
    rows_local, width = outer_head.shape
    part = width // FRAGS
    fsdp = lax.axis_size("fsdp")
    me = lax.axis_index("fsdp")
    masks = range(fsdp)

    normed = [normalize(hidden[s]) for s in range(STEPS)]
    features = [
        [columns_at(n, me, rows_local)]
        + [swap(columns_at(n, me ^ m, rows_local), "fsdp", m) for m in masks[1:]]
        for n in normed
    ]
    reference = gather_reference(ref_head)
    refer_log = [log_softmax(capped(dot(n, reference))) for n in normed]

    inner = outer_head + drift[0].astype(f32)
    means = []
    for s in range(STEPS):
        weights = inner.astype(bf16)
        raw = dot(features[s][0], weights)
        for m in masks[1:]:
            raw = raw + swap(dot(features[s][m], weights).astype(logit_type), "fsdp", m).astype(f32)
        grads = logit_grads(capped(raw), refer_log[s], targets[s], valid[s])
        total = dot_rows(features[s][0], grads)
        for m in masks[1:]:
            total = total + dot_rows(features[s][m], swap(grads, "fsdp", m))
        inner = inner - inner_rate * total
        start = plan[s] * part
        delta = lax.dynamic_slice_in_dim(outer_head - inner, start, part, 1)
        means.append(mean_over_replicas(delta))
    first, second = means
    mean = jnp.where(
        plan[0] == 0,
        jnp.concatenate([first, second], 1),
        jnp.concatenate([second, first], 1),
    )
    new_outer = outer_head - outer_rate * mean
    new_inner = mix_weight * inner + (1.0 - mix_weight) * new_outer
    return (new_outer, new_inner[None])


MASKS = (3, 2, 1)
COST = {
    "after": 100000000,
    "stacked": 5000000000,
    "more_reference_logs": 100000000,
    "own_logits": 100000000,
    "own_update": 5000000000,
    "update": 1000000000,
}
VMEM = pl.BlockSpec(memory_space=pltpu.VMEM)
SMEM = pl.BlockSpec(memory_space=pltpu.SMEM)
ANY = pl.BlockSpec(memory_space=pl.ANY)
HBM = pl.BlockSpec(memory_space=pltpu.HBM)


def call(kernel, operands, in_specs, out_shape, out_specs, room, scratch=(), **more):
    return pl.pallas_call(
        kernel,
        out_shape=out_shape,
        in_specs=in_specs,
        out_specs=out_specs,
        scratch_shapes=scratch,
        compiler_params=pltpu.CompilerParams(vmem_limit_bytes=room * 1024 * 1024),
        cost_estimate=pl.CostEstimate(flops=COST.get(kernel.__qualname__.split(".")[0], 1000), bytes_accessed=1000, transcendentals=0),
        **more,
    )(*operands)


def like(shape, kind):
    return jax.ShapeDtypeStruct(shape, kind)


def after(value, *earlier):
    def kernel(*refs):
        pass

    return call(
        kernel,
        (value,) + earlier,
        [ANY] * (1 + len(earlier)),
        like(value.shape, value.dtype),
        ANY,
        2,
        input_output_aliases={0: 0},
    )


def stacked(pieces):
    rows, cols = pieces[0].shape
    count = len(pieces)

    def kernel(*refs):
        out_ref, sems = refs[count:]
        copies = [
            pltpu.make_async_copy(refs[k], out_ref.at[pl.ds(k * rows, rows)], sems.at[k])
            for k in range(count)
        ]
        for copy in copies:
            copy.start()
        for copy in copies:
            copy.wait()

    return call(
        kernel,
        pieces,
        [ANY] * count,
        like((count * rows, cols), pieces[0].dtype),
        ANY,
        2,
        [pltpu.SemaphoreType.DMA((count,))],
    )


def positions():
    replica = lax.axis_index("replica")
    return lax.axis_index("fsdp"), replica, lax.rem(replica, CORES), replica // (2 * CORES)


LEVEL = math.log(2.0) / 64.0


def scale_of(code):
    return jnp.exp(code.astype(f32) * LEVEL)


def packed_rows(rows):
    return rows + 8


def pack(out_ref, first, second):
    rows = first.shape[0]
    codes, values = [], []
    for x in (first, second):
        top = jnp.maximum(jnp.max(jnp.abs(x), axis=0, keepdims=True), 1e-30)
        code = jnp.ceil(jnp.log(top) * (1.0 / LEVEL)).astype(jnp.int32) + 1
        codes.append(code)
        values.append(jnp.round(x * (32767.0 / scale_of(code))).astype(jnp.int32))
    out_ref[0:rows, :] = (values[0] << 16) | (values[1] & 0xFFFF)
    row = lax.broadcasted_iota(jnp.int32, (8, first.shape[1]), 0)
    out_ref[rows : rows + 8, :] = jnp.where(row == 0, codes[0], codes[1])


def unpack(ref, start=0, rows=None):
    rows = ref.shape[0] - 8 if rows is None else rows
    both = ref[pl.ds(start, rows), :]
    codes = ref[pl.ds(start + rows, 8), :]
    unit = scale_of(codes) * (1.0 / 32767.0)
    return (both >> 16).astype(f32) * unit[0:1, :], ((both << 16) >> 16).astype(f32) * unit[1:2, :]


def column(ref, step):
    row = ref[step : step + 1, :]
    return jnp.broadcast_to(row, (128, row.shape[1])).T[:, 0:1]


def normalized(hidden, sizes, passed=(), folded=(), earlier=()):
    tokens, width = hidden.shape
    cols = width // 2
    tile = 16
    extra = [f.shape[0] * f.shape[1] // cols for f in folded]
    starts = [sum(sizes[:k]) for k in range(len(sizes))]
    lengths = [size + sum(extra) * (k == 0) for k, size in enumerate(sizes)]

    def kernel(hidden_ref, *refs):
        passed_refs, refs = refs[: len(passed)], refs[len(passed) :]
        folded_refs, refs = refs[: len(folded)], refs[len(folded) + len(earlier) :]
        normed_ref, sent_refs, copy_refs = refs[0], refs[1 : 1 + len(sizes)], refs[1 + len(sizes) :]
        other = pl.multiple_of((1 - lax.axis_index("fsdp")) * cols, cols)
        for source, target in zip(passed_refs, copy_refs):
            target[...] = source[...]
        for ref, rows in zip(folded_refs, extra):
            part = ref.shape[1]
            for k in range(cols // part):
                sent_refs[0][sizes[0] : sizes[0] + rows, k * part : (k + 1) * part] = ref[k * rows : (k + 1) * rows, :]
        for start, size, sent_ref in zip(starts, sizes, sent_refs):
            for k in range(0, size, tile):
                at = pl.ds(start + k, tile)
                normed_ref[at, :] = normalize(hidden_ref[at, :])
                sent_ref[k : k + tile, :] = normed_ref[at, pl.ds(other, cols)]

    return call(
        kernel,
        (hidden,) + passed + folded + earlier,
        [VMEM] * (1 + len(passed) + len(folded)) + [ANY] * len(earlier),
        [like((tokens, width), bf16)]
        + [like((length, cols), bf16) for length in lengths]
        + [like(p.shape, p.dtype) for p in passed],
        [VMEM] * (1 + len(sizes) + len(passed)),
        8,
    )


def unfolded(message, start, shape):
    def kernel(message_ref, out_ref):
        rows = message.shape[0] - start
        for k in range(shape[0] // rows):
            out_ref[k * rows : (k + 1) * rows, :] = message_ref[start:, k * shape[1] : (k + 1) * shape[1]]

    return call(kernel, (message,), [VMEM], like(shape, message.dtype), VMEM, 4)


def reference_logs(normed, stacks, *earlier):
    tokens, width = normed.shape
    entries = stacks[0][0].shape[1]
    marks = [m for _, m in stacks]
    stacks = tuple(a for a, _ in stacks)
    rows = stacks[0].shape[0] // len(marks[0])
    count = len(stacks)

    def kernel(normed_ref, *refs):
        out_ref, whole_ref = refs[count + len(earlier) :]
        fsdp, me, _, _ = positions()
        for number in range(count):
            for p, (mask, bit_fsdp) in enumerate(marks[number]):
                block = jnp.bitwise_xor(me, mask) * 2 + jnp.bitwise_xor(fsdp, bit_fsdp)
                to = pl.ds(pl.multiple_of(block * rows, rows), rows)
                whole_ref[to, :] = refs[number][p * rows : (p + 1) * rows, :]
        out_ref[...] = log_softmax(capped(dot(normed_ref[...], whole_ref[...])))

    return call(
        kernel,
        (normed,) + tuple(stacks) + earlier,
        [VMEM] * (1 + count) + [ANY] * len(earlier),
        (like((tokens, entries), f32), like((width, entries), bf16)),
        (VMEM, VMEM),
        10,
    )


def more_reference_logs(normed, whole, *earlier):
    def kernel(normed_ref, whole_ref, *refs):
        refs[-1][...] = log_softmax(capped(dot(normed_ref[...], whole_ref[...])))

    return call(
        kernel,
        (normed, whole) + earlier,
        [VMEM, VMEM] + [ANY] * len(earlier),
        like((normed.shape[0], whole.shape[1]), f32),
        VMEM,
        8,
    )


def starting_weights(outer_head, drift, *earlier):
    rows, entries = outer_head.shape

    def kernel(outer_ref, drift_ref, *refs):
        inner_ref, weights_ref = refs[-2:]
        inner = outer_ref[...] + drift_ref[0].astype(f32)
        inner_ref[...] = inner
        weights_ref[...] = inner.astype(bf16)

    return call(
        kernel,
        (outer_head, drift) + earlier,
        [VMEM, VMEM] + [ANY] * len(earlier),
        (like((rows, entries), f32), like((rows, entries), bf16)),
        (VMEM, VMEM),
        10,
    )


def pack_logits(out_ref, logits):
    half = logits.shape[1] // 2
    pack(out_ref, logits[:, :half], logits[:, half:])


def put_together(out_ref, refs, sizes):
    start = 0
    for ref, size in zip(refs, sizes):
        out_ref[start : start + size, :] = ref[0:size, :]
        start += size


def partner_logits(pieces, sizes, weights):
    tokens, cols = sum(sizes), pieces[0].shape[1]
    entries = weights.shape[1]

    def kernel(weights_ref, *refs):
        features_ref, out_ref = refs[-2:]
        put_together(features_ref, refs[:-2], sizes)
        pack_logits(out_ref, dot(features_ref[...], weights_ref[...]))

    return call(
        kernel,
        (weights,) + tuple(pieces),
        [VMEM] * (1 + len(pieces)),
        (like((tokens, cols), bf16), like((packed_rows(tokens), entries // 2), jnp.int32)),
        (VMEM, VMEM),
        10,
    )


def own_logits(normed, weights, *earlier):
    tokens = normed.shape[0]
    rows, entries = weights.shape

    def kernel(normed_ref, weights_ref, *refs):
        at = pl.ds(pl.multiple_of(lax.axis_index("fsdp") * rows, rows), rows)
        refs[-1][...] = dot(normed_ref[:, at], weights_ref[...])

    return call(
        kernel,
        (normed, weights) + earlier,
        [VMEM, VMEM] + [ANY] * len(earlier),
        like((tokens, entries), f32),
        VMEM,
        8,
    )


def gradients(own, received, refer_log, targets, valid, step, *earlier):
    tokens, entries = own.shape

    def kernel(own_ref, received_ref, refer_ref, targets_ref, valid_ref, *refs):
        raw = own_ref[...] + jnp.concatenate(unpack(received_ref), axis=1)
        policy = capped(raw)
        policy_log = log_softmax(policy)
        policy_prob = jnp.exp(policy_log)
        diverge = policy_log - refer_ref[...]
        kl_value = jnp.sum(policy_prob * diverge, axis=-1, keepdims=True)
        here = lax.broadcasted_iota(jnp.int32, policy.shape, 1)
        onehot = jnp.where(column(targets_ref, step) == here, 1.0, 0.0)
        upstream = column(valid_ref, step).astype(f32) * (
            policy_prob - onehot + kl_weight * policy_prob * (diverge - kl_value)
        )
        ratio = policy / soft_cap
        refs[-1][...] = (upstream * (1.0 - ratio * ratio) * (4.0 / math.sqrt(D))).astype(bf16)

    return call(
        kernel,
        (own, received, refer_log, targets, valid) + earlier,
        [VMEM] * 5 + [ANY] * len(earlier),
        like((tokens, entries), bf16),
        VMEM,
        8,
    )


def own_update(inner, normed, grads, *earlier):
    rows, entries = inner.shape
    tile = rows // 4

    def kernel(inner_ref, normed_ref, grads_ref, *refs):
        for k in range(4):
            at = pl.ds(k * tile, tile)
            columns = pl.ds(pl.multiple_of(lax.axis_index("fsdp") * rows + k * tile, tile), tile)
            refs[-1][at, :] = inner_ref[at, :] - inner_rate * dot_rows(normed_ref[:, columns], grads_ref[...])

    return call(
        kernel,
        (inner, normed, grads) + earlier,
        [VMEM] * 3 + [ANY] * len(earlier),
        like((rows, entries), f32),
        VMEM,
        10,
    )


def update(inner, features, grads, outer_head, plan, step, replicas, following=(), earlier=()):
    rows, entries = inner.shape
    tokens = features.shape[0]
    part = entries // FRAGS
    half = rows // 2
    tile = rows // 4
    pieces = len(following)

    def kernel(plan_ref, inner_ref, features_ref, grads_ref, outer_ref, *refs):
        following_refs, refs = refs[:pieces], refs[pieces + len(earlier) :]
        new_ref, sent_ref, kept_ref = refs[:3]
        for k in range(4):
            at = pl.ds(k * tile, tile)
            new = inner_ref[at, :] - inner_rate * dot_rows(features_ref[:, at], grads_ref[...])
            new_ref[at, :] = new
            if pieces:
                refs[4][at, :] = new.astype(bf16)
        if pieces:
            next_ref, weights_ref, partial_ref = refs[3:]
            put_together(next_ref, following_refs, [f.shape[0] for f in following])
            pack_logits(partial_ref, dot(next_ref[...], weights_ref[...]))
        columns = pl.ds(pl.multiple_of(plan_ref[step] * part, part), part)
        core = positions()[2]
        for place_ref, which in ((sent_ref, 1 - core), (kept_ref, core)):
            at = pl.ds(pl.multiple_of(which * half, half), half)
            place_ref[...] = (outer_ref[at, columns] - new_ref[at, columns]) * (1.0 / replicas)

    operands = (plan, inner, features, grads, outer_head) + tuple(following)
    out_shape = [like((rows, entries), f32), like((half, part), f32), like((half, part), f32)]
    if pieces:
        out_shape += [
            like((tokens, rows), bf16),
            like((rows, entries), bf16),
            like((packed_rows(tokens), entries // 2), jnp.int32),
        ]
    return call(
        kernel,
        operands + tuple(earlier),
        [SMEM] + [VMEM] * (len(operands) - 1) + [ANY] * len(earlier),
        out_shape,
        [VMEM] * len(out_shape),
        16,
    )


def pack_quarter(out_ref, quarter):
    half = quarter.shape[0] // 2
    pack(out_ref, quarter[:half], quarter[half:])


def unpack_quarter(ref, start=0, rows=None):
    return jnp.concatenate(unpack(ref, start, rows), axis=0)


def quarters(kept, received):
    rows, cols = kept.shape
    quarter = rows // MAJOR

    def kernel(kept_ref, received_ref, own_ref, *refs):
        major = positions()[3]

        def piece(mask):
            at = pl.ds(pl.multiple_of(jnp.bitwise_xor(major, mask) * quarter, quarter), quarter)
            return kept_ref[at, :] + received_ref[at, :]

        for mask, out_ref in zip(MASKS, refs):
            pack_quarter(out_ref, piece(mask))
        own_ref[...] = piece(0)

    small = like((packed_rows(quarter // 2), cols), jnp.int32)
    return call(
        kernel,
        (kept, received),
        [VMEM] * 2,
        [like((quarter, cols), f32)] + [small] * len(MASKS),
        [VMEM] * (1 + len(MASKS)),
        6,
    )


def quarter_sum(own, pieces, *earlier):
    def kernel(own_ref, *refs):
        total = own_ref[...]
        for ref in refs[: len(pieces)]:
            total = total + unpack_quarter(ref)
        pack_quarter(refs[-1], total)

    return call(
        kernel,
        (own,) + tuple(pieces) + earlier,
        [VMEM] * (1 + len(pieces)) + [ANY] * len(earlier),
        like(pieces[0].shape, jnp.int32),
        VMEM,
        4,
    )


def pair_sum(one, other, *earlier):
    def kernel(one_ref, other_ref, *refs):
        pack_quarter(refs[-1], unpack_quarter(one_ref) + unpack_quarter(other_ref))

    return call(
        kernel,
        (one, other) + earlier,
        [VMEM] * 2 + [ANY] * len(earlier),
        like(one.shape, jnp.int32),
        VMEM,
        4,
    )


def settled(outer_head, inner, means, plan):
    rows, entries = inner.shape
    part = entries // FRAGS
    tile = rows // (CORES * MAJOR)
    steps = CORES * MAJOR
    small = packed_rows(tile // 2)

    def kernel(plan_ref, outer_ref, inner_ref, own0, other0, own1, other1, new_outer_ref, new_inner_ref, *scratch):
        mean_ref, outer_held, inner_held, sems = scratch
        _, _, core, major = positions()
        copies = []
        for i in range(steps):
            start = pl.multiple_of(jnp.bitwise_xor(i % MAJOR, major) * small, small)
            at = pl.ds(i * tile, tile)

            @pl.when(i // MAJOR == core)
            def _():
                mean_ref[0] = unpack_quarter(own0, start, tile // 2)
                mean_ref[1] = unpack_quarter(own1, start, tile // 2)

            @pl.when(i // MAJOR != core)
            def _():
                mean_ref[0] = unpack_quarter(other0, start, tile // 2)
                mean_ref[1] = unpack_quarter(other1, start, tile // 2)

            for f in range(FRAGS):
                columns = pl.ds(f * part, part)
                mean = mean_ref[jnp.where(plan_ref[0] == f, 0, 1)]
                fresh = outer_ref[at, columns] - outer_rate * mean
                outer_held[at, columns] = fresh
                inner_held[at, columns] = mix_weight * inner_ref[at, columns] + (1.0 - mix_weight) * fresh
            if i % 2 == 1:
                at = pl.ds((i - 1) * tile, 2 * tile)
                for k, (held, out) in enumerate(((outer_held, new_outer_ref), (inner_held, new_inner_ref))):
                    copies.append(pltpu.make_async_copy(held.at[at], out.at[at], sems.at[2 * i + k]))
                    copies[-1].start()
        for copy in copies:
            copy.wait()

    return call(
        kernel,
        (plan, outer_head, inner) + tuple(means[0]) + tuple(means[1]),
        [SMEM] + [VMEM] * 6,
        [like((rows, entries), f32)] * 2,
        [HBM, HBM],
        14,
        [
            pltpu.VMEM((2, tile, part), f32),
            pltpu.VMEM((rows, entries), f32),
            pltpu.VMEM((rows, entries), f32),
            pltpu.SemaphoreType.DMA((2 * steps,)),
        ],
    )


def along(stack, *masks):
    array, marks = stack
    return (
        stacked([array] + [swap(array, "replica", m) for m in masks]),
        [(mark ^ m, bit) for m in (0,) + masks for mark, bit in marks],
    )


def across(stack, mask):
    array, marks = stack
    return swap(array, "replica", mask), [(mark ^ mask, bit) for mark, bit in marks]


def gathered_stacks(ref_own, ref_partner):
    along_z = [m * 2 * CORES for m in (1, 2, 3)]
    stacks = []
    for piece in ((ref_own, [(0, 0)]), (ref_partner, [(0, 1)])):
        first = along(piece, *along_z)
        second = across(first, CORES)
        stacks += [first, second, across(first, 1), across(second, 1)]
    return stacks


def quarters_along(own, order):
    got = {m: swap(own, "replica", m * 2 * CORES) for m in order}
    return [own] + [got[m] for m in range(1, MAJOR)]


def gathered_quarters(pieces):
    stack = stacked(pieces)
    return stack, swap(stack, "replica", 1)


def chip_quarters(sent, kept):
    own, *pieces = quarters(kept, swap(sent, "replica", 1))
    return own, [swap(p, "replica", m * 2 * CORES) for p, m in zip(pieces, MASKS)]


def shards_pair(hidden, targets, valid, plan, outer_head, drift, ref_head):
    replicas = lax.axis_size("replica")

    tokens = hidden.shape[1]
    sizes0 = (4 * tokens // 16, tokens - 4 * tokens // 16)
    sizes1 = (9 * tokens // 16, tokens - 9 * tokens // 16)

    normed0, *sent0 = normalized(hidden[0], sizes0, (), (ref_head,))
    features0 = [swap(s, "fsdp", 1) for s in sent0]
    normed1, sent1a, sent1b, ref_own = normalized(hidden[1], sizes1, (ref_head,), (), tuple(sent0))
    features1a = swap(sent1a, "fsdp", 1)
    stacks = gathered_stacks(ref_own, unfolded(features0[0], sizes0[0], ref_head.shape))

    inner, weights = starting_weights(outer_head, drift, normed1)
    features0, partial = partner_logits(features0, sizes0, weights)
    received = swap(partial, "fsdp", 1)
    own = own_logits(normed0, weights, partial)
    features1b = swap(after(sent1b, partial), "fsdp", 1)
    refer_log, whole = reference_logs(normed0, stacks, features1a)
    grads = gradients(own, received, refer_log, targets, valid, 0, features1a)
    partner_grads = swap(grads, "fsdp", 1)
    halfway = own_update(inner, normed0, grads, features1b)
    refer_log = more_reference_logs(normed1, whole, halfway)
    inner, sent, kept, features1, weights, partial = update(
        halfway, features0, partner_grads, outer_head, plan, 0, replicas, (features1a, features1b), ()
    )

    received = swap(partial, "fsdp", 1)
    own = own_logits(normed1, weights)
    quarter, pieces = chip_quarters(sent, kept)
    grads = gradients(own, received, refer_log, targets, valid, 1, pieces[0])
    partner_grads = swap(grads, "fsdp", 1)
    halfway = own_update(inner, normed1, grads)
    quarter = quarter_sum(quarter, pieces, halfway)
    first = pair_sum(quarter, swap(quarter, "replica", CORES))
    inner, sent, kept = update(
        halfway, features1, partner_grads, outer_head, plan, 1, replicas, (), (quarter,)
    )

    quarter, pieces = chip_quarters(sent, kept)
    quarter = quarter_sum(quarter, pieces)
    first = quarters_along(first, (3, 1, 2))
    second = pair_sum(quarter, swap(quarter, "replica", CORES), first[1], first[2])
    means = [gathered_quarters(m) for m in (first, quarters_along(second, (1, 2, 3)))]
    new_outer, new_inner = settled(outer_head, inner, means, plan)
    return (new_outer, new_inner[None])


def solution(mesh):
    in_specs = (
        P(None, ("replica", "fsdp"), None),
        P(None, ("replica", "fsdp")),
        P(None, ("replica", "fsdp")),
        P(),
        P("fsdp", None),
        P("replica", "fsdp", None),
        P(("replica", "fsdp"), None),
    )
    out_specs = (P("fsdp", None), P("replica", "fsdp", None))
    chips = mesh.shape["replica"] // CORES
    pairs = mesh.shape["fsdp"] == 2 and chips == 2 * MAJOR
    shards = shards_pair if pairs else shards_any
    return jax.shard_map(shards, mesh=mesh, in_specs=in_specs, out_specs=out_specs, check_vma=False)
```
